32 devices in a mesh: mem: 16 (over z, y, x), lat: 2 (over core).
Axes of the slice: x: 2, y: 2, z: 4, core: 2. Of those that a mesh axis runs over, the one named last changes fastest.
Arguments:
- ensemble: bfloat16 [16, 4, 64, 8, 512], P('mem', None, 'lat')
- weights: float32 [16, 64, 8, 512], P('mem', 'lat')
- obs_cell: int32 [4, 16384], P(None, 'lat'), may hold values from 0 to 262143, as said below
- innovation: float32 [4, 16384], P(None, 'lat'), may hold values from -6 to 6
- obs_weight: float32 [4, 16384], P(None, 'lat'), may hold values from 1 to 10
- quality: int32 [4, 16384], P(None, 'lat'), may hold values 0 or 1
Outputs:
- new_weights: float32 [16, 64, 8, 512], P('mem', 'lat')
- cost: float32 [], replicated
The draws below stay inside these ranges and needn't reach their ends.
Inputs may be any that keep to these rules, and one draw needn't show every extreme that they name: `obs_cell`: columns b * 8192 to (b + 1) * 8192 - 1 name cells in latitude rows b * 32 to (b + 1) * 32 - 1; cells may repeat.
All inputs are finite; a program needn't handle non-finite values. No bound on the sum of `quality` on one device may be relied on, other than what follows from the above.
Results may differ from the reference program's by a relative error of at most 0.0003.
Values sent between devices are 32-bit elements; how exact they have to be, the bound alone decides.
No kernel may reach another device: no remote copies, remote signals or barrier semaphores. Data moves between devices by JAX's collectives and lax.ppermute only.
A program may use at most 64 MiB of HBM per device.

```python
import math
import jax
import jax.numpy as jnp
from jax import lax

MEMBERS = 16
SLOTS = 4
ROWS_DEV = 32
NLAT = 64
LEV = 8
NLON = 512
HALF = 8
OBS_DEV = 8192
OBS = 16384


def draw_ensemble(key, part):
    shape = (MEMBERS, SLOTS, NLAT, LEV, NLON)
    noise = jax.random.normal(key, shape, jnp.float32)
    ranked = jnp.arange(MEMBERS).astype(jnp.float32) / (MEMBERS - 1)
    factor = 0.6 * 3.0 ** ranked
    return (noise * factor[:, None, None, None, None]).astype(jnp.bfloat16)


def draw_weights(key, part):
    shape = (MEMBERS, NLAT, LEV, NLON)
    noise = jax.random.normal(key, shape, jnp.float32)
    ranked = jnp.arange(MEMBERS).astype(jnp.float32) / (MEMBERS - 1)
    rowed = jnp.arange(NLAT).astype(jnp.float32) / (NLAT - 1)
    factor = 0.35 * (3.0 ** ranked)[:, None] * (3.0 ** rowed)[None, :]
    return noise * factor[:, :, None, None]


def draw_obs_cell(key, part):
    first, second, third = jax.random.split(jax.random.fold_in(key, 3), 3)
    block = (jnp.arange(OBS, dtype=jnp.int32) // OBS_DEV)[None, :]
    row_pick = block * ROWS_DEV + jax.random.randint(first, (SLOTS, OBS), 0, ROWS_DEV, jnp.int32)
    level_pick = jax.random.randint(second, (SLOTS, OBS), 0, LEV, jnp.int32)
    lon_pick = jax.random.randint(third, (SLOTS, OBS), 0, NLON, jnp.int32)
    cells = (row_pick * LEV + level_pick) * NLON + lon_pick
    cells = cells.at[0, 0].set(0)
    cells = cells.at[SLOTS - 1, OBS - 1].set(NLAT * LEV * NLON - 1)
    return cells


def plant(drawn, stream_key, smallest, largest):
    shape = drawn.shape
    place = [jax.random.randint(jax.random.fold_in(stream_key, axis), (), 0, shape[axis]) for axis in range(len(shape))]
    drawn = drawn.at[tuple(place)].set(smallest)
    longest = shape.index(max(shape))
    place[longest] = (place[longest] + 1) % shape[longest]
    return drawn.at[tuple(place)].set(largest)


def shard_levels(rng, extent, cuts, smallest, largest):
    gain, own = 1.0, jax.random.fold_in(rng, 6)
    for axis_at, parts in cuts:
        steps = jnp.exp(jax.random.uniform(jax.random.fold_in(own, axis_at), (parts,), jnp.float32, smallest / len(cuts), largest / len(cuts)))
        gain = gain * jnp.repeat(steps, extent[axis_at] // parts).reshape([-1 if axis == axis_at else 1 for axis in range(len(extent))])
    return gain


def scatter_about(key, shape, spread, bound, shards=(), kind=jnp.bfloat16):
    values = spread * jax.random.normal(key, shape, jnp.float32)
    if shards:
        values = values * shard_levels(key, shape, shards, -0.22, 0.18)
    return jnp.clip(values, -bound, bound).astype(kind)


def setup_inputs(seed: int = 0) -> dict:
    key_of = jax.random.split(jax.random.key(seed), 7)
    return {
        "ensemble": draw_ensemble(jax.random.fold_in(key_of[6], 71), 0),
        "weights": draw_weights(jax.random.fold_in(key_of[6], 71), 0),
        "obs_cell": draw_obs_cell(jax.random.fold_in(key_of[6], 71), 0),
        "innovation": scatter_about(key_of[3], (SLOTS, OBS), 1.0, 6.0, ((1, 2),), jnp.float32),
        "obs_weight": jnp.clip(jnp.exp(math.log(10.0) - 2.3025851 * jax.random.uniform(key_of[4], (SLOTS, OBS), jnp.float32) ** shard_levels(key_of[4], (SLOTS, OBS), ((1, 2),), -0.2, 0.2)), 1.0, 10.0),
        "quality": plant((jax.random.randint(key_of[5], (SLOTS, OBS), 0, 5) < 4).astype(jnp.int32), jax.random.fold_in(key_of[5], 1), 0, 1),
    }


def tap_values(offset):
    sigma = HALF / 2.0
    every = jnp.arange(-HALF, HALF + 1).astype(jnp.float32)
    normal = jnp.sqrt(jnp.sum(jnp.exp(-(every / sigma) ** 2)))
    return jnp.exp(-0.5 * (offset / sigma) ** 2) / normal

def localize(field):
    padded = jnp.pad(field, ((HALF, HALF), (0, 0), (0, 0)))
    by_rows = jnp.zeros(field.shape, jnp.float32)
    for shift_by in range(-HALF, HALF + 1):
        by_rows = by_rows + tap_values(jnp.float32(shift_by)) * padded[HALF + shift_by:HALF + shift_by + field.shape[0]]
    result = jnp.zeros(field.shape, jnp.float32)
    for shift_by in range(-HALF, HALF + 1):
        result = result + tap_values(jnp.float32(shift_by)) * jnp.roll(by_rows, shift_by, axis=2)
    return result

def reference(ensemble, weights, obs_cell, innovation, obs_weight, quality):
    norm_scale = 1.0 / jnp.sqrt(jnp.float32(MEMBERS - 1))
    local_weights = lax.map(localize, weights)

    def accumulate(running, member_pair):
        member, loc_field = member_pair
        return (running + member.astype(jnp.float32) * loc_field[None], None)
    start_field = jnp.zeros((SLOTS, NLAT, LEV, NLON), jnp.float32)
    increment = lax.scan(accumulate, start_field, (ensemble, local_weights))[0] * norm_scale
    flat_incr = increment.reshape(SLOTS, NLAT * LEV * NLON)
    observed = jnp.take_along_axis(flat_incr, obs_cell, axis=1)
    resid = observed - innovation
    keep_weight = quality.astype(jnp.float32) * obs_weight
    weighted = keep_weight * resid
    slot_ids = jnp.broadcast_to(jnp.arange(SLOTS, dtype=jnp.int32)[:, None], obs_cell.shape)
    grad_increment = jnp.zeros_like(flat_incr).at[slot_ids, obs_cell].add(weighted).reshape(increment.shape)

    def backward(member_pair):
        member, alpha_field = member_pair
        summed = lax.optimization_barrier(jnp.sum(member.astype(jnp.float32) * grad_increment, axis=0)) * norm_scale
        return alpha_field + localize(summed)
    grad = lax.map(backward, (ensemble, weights))
    entries = jnp.float32(MEMBERS * NLAT * LEV * NLON)
    cost = (0.5 * jnp.sum(weights * weights) + 0.5 * jnp.sum(weighted * resid)) / entries
    length = jnp.sqrt(jnp.sum(grad * grad) / entries + 1e-06)
    new_weights = weights - 0.5 * grad / length
    return (new_weights, cost)
```

```python
import functools
import math

import jax
import jax.numpy as jnp
import numpy as np
from jax import lax
from jax.experimental import pallas as pl
from jax.experimental.pallas import tpu as pltpu
from jax.sharding import PartitionSpec as P

HALF = 8
STEP_LENGTH = 0.5
EPSILON = 1e-06
TILE = 512
MIB = 1024 * 1024


def taps():
    sigma = HALF / 2.0
    every = np.arange(-HALF, HALF + 1).astype(np.float64)
    normal = np.sqrt(np.sum(np.exp(-((every / sigma) ** 2))))
    return np.exp(-0.5 * (every / sigma) ** 2) / normal


def circulant_parts(lon_count):
    full = np.zeros((lon_count, lon_count), np.float32)
    at = np.arange(lon_count)
    for shift_by, tap in zip(range(-HALF, HALF + 1), taps()):
        full[at, (at + shift_by) % lon_count] += np.float32(tap)
    high = full.astype(jnp.bfloat16)
    low = (full - high.astype(np.float32)).astype(jnp.bfloat16)
    return high, low


def two_parts(value):
    high = value.astype(jnp.bfloat16)
    low = (value - high.astype(jnp.float32)).astype(jnp.bfloat16)
    return high, low


def smooth_rows(low, own, high):
    tap = [float(t) for t in taps()]
    padded = jnp.concatenate([low, own, high], axis=0)
    rows = own.shape[0]
    total = padded[HALF : HALF + rows] * tap[HALF]
    for away in range(1, HALF + 1):
        pair = padded[HALF - away : HALF - away + rows] + padded[HALF + away : HALF + away + rows]
        total = total + pair * tap[HALF + away]
    return total


def smooth_lons(field, circ_high, circ_low):
    first, second = two_parts(field)
    dot = functools.partial(jnp.dot, preferred_element_type=jnp.float32)
    return dot(first, circ_high) + (dot(second, circ_high) + dot(first, circ_low))


def split_cell(cell, lon_count, lane_count):
    lon = lax.rem(cell, lon_count)
    return lax.div(cell, lon_count), lax.div(lon, lane_count), lax.rem(lon, lane_count)


def pick_kernel(low_ref, own_ref, high_ref, circ_high_ref, circ_low_ref, ens_ref, cell_ref, out_ref, local_ref, lhs_ref):
    rows, levels, lons = own_ref.shape
    slots = ens_ref.shape[0]
    keys = rows * levels
    lanes = 256
    halves = lons // lanes
    mixed = smooth_rows(low_ref[...], own_ref[...], high_ref[...]).reshape(keys, lons)
    local_ref[...] = smooth_lons(mixed, circ_high_ref[...], circ_low_ref[...])
    count = cell_ref.shape[1]
    key_ids = lax.broadcasted_iota(jnp.int32, (keys, TILE), 0)
    lane_ids = lax.broadcasted_iota(jnp.int32, (lanes, TILE), 0)
    for slot in range(slots):
        field = ens_ref[slot].reshape(keys, lons).astype(jnp.float32) * local_ref[...]
        first, second = two_parts(field.T)
        for half in range(halves):
            lhs_ref[:, pl.ds(half * keys, keys)] = first[half * lanes : (half + 1) * lanes]
            lhs_ref[:, pl.ds((halves + half) * keys, keys)] = second[half * lanes : (half + 1) * lanes]

        @pl.loop(0, count // TILE)
        def _(step):
            here = pl.ds(pl.multiple_of(step * TILE, TILE), TILE)
            key, half_of, lane = split_cell(cell_ref[pl.ds(slot, 1), here], lons, lanes)
            hots = []
            for half in range(halves):
                wanted = jnp.where(half_of == half, key, -1)
                hots.append((key_ids == wanted).astype(jnp.bfloat16))
            hot = jnp.concatenate(hots + hots, axis=0)
            found = jnp.dot(lhs_ref[...], hot, preferred_element_type=jnp.float32)
            out_ref[pl.ds(slot, 1), here] = jnp.sum(jnp.where(lane_ids == lane, found, 0.0), axis=0, keepdims=True)


def scatter_kernel(norm_scale, seen_ref, innov_ref, weight_ref, quality_ref, cell_ref, ens_ref, back_ref, cost_ref, acc_ref):
    slots, rows, levels, lons = ens_ref.shape
    keys = rows * levels
    lanes = 256
    halves = lons // lanes
    count = cell_ref.shape[1]
    key_ids = lax.broadcasted_iota(jnp.int32, (keys, TILE), 0)
    lane_ids = lax.broadcasted_iota(jnp.int32, (lanes, TILE), 0)
    resid = seen_ref[...] * norm_scale - innov_ref[...]
    keep = quality_ref[...].astype(jnp.float32) * weight_ref[...]
    cost_ref[...] = jnp.sum(keep * resid * resid).reshape(1, 1)
    for slot in range(slots):
        acc_ref[...] = jnp.zeros_like(acc_ref)

        @pl.loop(0, count // TILE)
        def _(step):
            here = pl.ds(pl.multiple_of(step * TILE, TILE), TILE)
            at = (pl.ds(slot, 1), here)
            key, half_of, lane = split_cell(cell_ref[at], lons, lanes)
            resid = seen_ref[at] * norm_scale - innov_ref[at]
            wres = quality_ref[at].astype(jnp.float32) * weight_ref[at] * resid
            first, second = two_parts(wres)
            chosen = lane_ids == lane
            placed = jnp.concatenate(
                [
                    jnp.where(chosen, first.astype(jnp.float32), 0.0).astype(jnp.bfloat16),
                    jnp.where(chosen, second.astype(jnp.float32), 0.0).astype(jnp.bfloat16),
                ],
                axis=1,
            )
            hots = []
            for half in range(halves):
                wanted = jnp.where(half_of == half, key, -1)
                hots.append((key_ids == wanted).astype(jnp.bfloat16))
            hot = jnp.concatenate(hots, axis=0)
            hot = jnp.concatenate([hot, hot], axis=1)
            acc_ref[...] += lax.dot_general(
                hot, placed, (((1,), (1,)), ((), ())), preferred_element_type=jnp.float32
            )

        grad = jnp.concatenate([acc_ref[pl.ds(h * keys, keys), :] for h in range(halves)], axis=1)
        term = ens_ref[slot].reshape(keys, lons).astype(jnp.float32) * grad
        term = term.reshape(rows, levels, lons)
        back_ref[...] = term if slot == 0 else back_ref[...] + term
    back_ref[...] *= norm_scale


def grad_kernel(low_ref, own_ref, high_ref, circ_high_ref, circ_low_ref, weights_ref, obs_cost_ref, grad_ref, sums_ref):
    rows, levels, lons = own_ref.shape
    mixed = smooth_rows(low_ref[...], own_ref[...], high_ref[...]).reshape(rows * levels, lons)
    weights = weights_ref[...].reshape(rows * levels, lons)
    grad = weights + smooth_lons(mixed, circ_high_ref[...], circ_low_ref[...])
    grad_ref[...] = grad.reshape(grad_ref.shape)
    lane = lax.broadcasted_iota(jnp.int32, sums_ref.shape, 1)
    prior = jnp.sum(weights * weights)
    square = jnp.sum(grad * grad)
    sums_ref[...] = jnp.where(lane == 0, square, jnp.where(lane == 1, prior, jnp.where(lane == 2, obs_cost_ref[...], 0.0)))


def call(body, out_shape, scratch, flops, *operands):
    vmem = pl.BlockSpec(memory_space=pltpu.VMEM)
    return pl.pallas_call(
        body,
        out_shape=out_shape,
        in_specs=[vmem] * len(operands),
        out_specs=jax.tree.map(lambda _: vmem, out_shape),
        scratch_shapes=scratch,
        compiler_params=pltpu.CompilerParams(vmem_limit_bytes=48 * MIB),
        cost_estimate=pl.CostEstimate(flops=flops, bytes_accessed=2 * MIB, transcendentals=0),
    )(*operands)


def edges(field):
    count = lax.axis_size("lat")
    forward = [(i, i + 1) for i in range(count - 1)]
    backward = [(target, source) for source, target in forward]
    low = lax.ppermute(field[-HALF:], "lat", forward)
    high = lax.ppermute(field[:HALF], "lat", backward)
    return low, high


def summed(value, axis):
    count = lax.axis_size(axis)
    if count & (count - 1):
        return lax.psum(value, axis)
    away = 1
    while away < count:
        value = value + lax.ppermute(value, axis, [(i, i ^ away) for i in range(count)])
        away *= 2
    return value


def local(ensemble, weights, obs_cell, innovation, obs_weight, quality):
    _, rows, levels, lons = weights.shape
    slots, obs = obs_cell.shape
    members = lax.axis_size("mem")
    lat_count = lax.axis_size("lat")
    norm_scale = 1.0 / math.sqrt(members - 1)
    cells = rows * levels * lons
    ens, own = ensemble[0], weights[0]
    offset = lax.rem(obs_cell, cells)
    circ_high, circ_low = (jnp.asarray(part) for part in circulant_parts(lons))
    f32 = jnp.float32
    low, high = edges(own)
    picked = call(
        pick_kernel,
        jax.ShapeDtypeStruct((slots, obs), f32),
        [pltpu.VMEM((rows * levels, lons), f32), pltpu.VMEM((256, 2 * cells // 256), jnp.bfloat16)],
        4 * slots * obs * cells,
        low, own, high, circ_high, circ_low, ens, offset,
    )
    seen = summed(picked, "mem")
    back, obs_cost = call(
        functools.partial(scatter_kernel, norm_scale),
        (jax.ShapeDtypeStruct((rows, levels, lons), f32), jax.ShapeDtypeStruct((1, 1), f32)),
        [pltpu.VMEM((cells // 256, 256), f32)],
        4 * slots * obs * cells,
        seen, innovation, obs_weight, quality, offset, ens,
    )
    back_low, back_high = edges(back)
    grad, sums = call(
        grad_kernel,
        (jax.ShapeDtypeStruct((rows, levels, lons), f32), jax.ShapeDtypeStruct((1, 128), f32)),
        [],
        10**9,
        back_low, back, back_high, circ_high, circ_low, own, obs_cost,
    )
    totals = summed(summed(sums, "lat"), "mem")
    entries = f32(members * lat_count * cells)
    cost = (0.5 * totals[0, 1] + 0.5 * totals[0, 2] / members) / entries
    length = jnp.sqrt(totals[0, 0] / entries + EPSILON)
    new_weights = own - STEP_LENGTH * grad / length
    return new_weights[None], cost


def solution(mesh):
    placed = (
        P("mem", None, "lat", None, None),
        P("mem", "lat", None, None),
        P(None, "lat"),
        P(None, "lat"),
        P(None, "lat"),
        P(None, "lat"),
    )
    return jax.shard_map(
        local,
        mesh=mesh,
        in_specs=placed,
        out_specs=(P("mem", "lat", None, None), P()),
        check_vma=False,
    )
```

```python
import functools
import math

import jax
import jax.numpy as jnp
import numpy as np
from jax import lax
from jax.experimental import pallas as pl
from jax.experimental.pallas import tpu as pltpu
from jax.sharding import PartitionSpec as P

HALF = 8
STEP_LENGTH = 0.5
EPSILON = 1e-06
LANES = 256
WINDOW = 3
MIB = 1024 * 1024


def taps():
    sigma = HALF / 2.0
    every = np.arange(-HALF, HALF + 1).astype(np.float64)
    normal = np.sqrt(np.sum(np.exp(-((every / sigma) ** 2))))
    return np.exp(-0.5 * (every / sigma) ** 2) / normal


def circulant_parts(lon_count):
    full = np.zeros((lon_count, lon_count), np.float32)
    at = np.arange(lon_count)
    for shift_by, tap in zip(range(-HALF, HALF + 1), taps()):
        full[at, (at + shift_by) % lon_count] += np.float32(tap)
    high = full.astype(jnp.bfloat16)
    low = (full - high.astype(np.float32)).astype(jnp.bfloat16)
    return high, low


def two_parts(value):
    high = value.astype(jnp.bfloat16)
    low = (value - high.astype(jnp.float32)).astype(jnp.bfloat16)
    return high, low


def smooth_rows(low, own, high):
    tap = [float(t) for t in taps()]
    padded = jnp.concatenate([low, own, high], axis=0)
    rows = own.shape[0]
    total = padded[HALF : HALF + rows] * tap[HALF]
    for away in range(1, HALF + 1):
        pair = padded[HALF - away : HALF - away + rows] + padded[HALF + away : HALF + away + rows]
        total = total + pair * tap[HALF + away]
    return total


def smooth_lons(field, circ_high, circ_low):
    first, second = two_parts(field)
    dot = functools.partial(jnp.dot, preferred_element_type=jnp.float32)
    return dot(first, circ_high) + (dot(second, circ_high) + dot(first, circ_low))


def one_hot(ids, at):
    return (ids == at).astype(jnp.bfloat16)


def ids_of(shape, dim):
    return lax.broadcasted_iota(jnp.int32, shape, dim)


def across(left, right):
    return lax.dot_general(left, right, (((1,), (1,)), ((), ())), preferred_element_type=jnp.float32)


def permute(pos, values, tiles):
    hi_ids = ids_of((tiles, LANES), 0)
    lo_ids = ids_of((LANES, LANES), 0)
    hi, lo = lax.div(pos, LANES), lax.rem(pos, LANES)
    total = jnp.zeros((len(values) * tiles, LANES), jnp.float32)
    for at in range(tiles):
        here = slice(at * LANES, (at + 1) * LANES)
        chosen = hi_ids == hi[:, here]
        left = jnp.concatenate([jnp.where(chosen, v[:, here], 0.0) for v in values], axis=0)
        total += across(left.astype(jnp.bfloat16), one_hot(lo_ids, lo[:, here]))
    return [total[k * tiles : (k + 1) * tiles] for k in range(len(values))]


def sort_kernel(shape, cell_ref, pos_ref, key_ref, lane_ref, first_ref, last_ref, far_ref, prefix_ref):
    rows, levels, lons = shape
    slots, obs = cell_ref.shape
    tiles = obs // LANES
    row_ids = ids_of((rows, LANES), 0)
    square = (LANES, LANES)
    upper = (ids_of(square, 0) <= ids_of(square, 1)).astype(jnp.bfloat16)
    counting = jnp.concatenate([upper, jnp.ones(square, jnp.bfloat16)], axis=1)
    before = (ids_of((rows, rows), 1) < ids_of((rows, rows), 0)).astype(jnp.float32)
    for slot in range(slots):
        cell = lax.rem(cell_ref[pl.ds(slot, 1), :], rows * levels * lons)
        key, lon = lax.div(cell, lons), lax.rem(cell, lons)
        row = lax.div(key, levels)
        parts = [row[:, at * LANES : (at + 1) * LANES] for at in range(tiles)]
        hot = jnp.concatenate([one_hot(row_ids, part) for part in parts], axis=0)
        prefix_ref[...] = jnp.dot(hot, counting, preferred_element_type=jnp.float32)
        total = jnp.zeros((rows, LANES), jnp.float32)
        for at in range(tiles):
            total += prefix_ref[pl.ds(at * rows, rows), pl.ds(LANES, LANES)]
        carry = jnp.dot(before, total, precision=lax.Precision.HIGHEST, preferred_element_type=jnp.float32) - 1.0
        places = []
        for at in range(tiles):
            here = pl.ds(at * rows, rows)
            place = jnp.where(row_ids == parts[at], prefix_ref[here, pl.ds(0, LANES)] + carry, 0.0)
            places.append(jnp.sum(place, axis=0, keepdims=True))
            carry += prefix_ref[here, pl.ds(LANES, LANES)]
        pos = jnp.concatenate(places, axis=1).astype(jnp.int32)
        pos_ref[pl.ds(slot, 1), :] = pos
        lane = jnp.where(lon < LANES, lon, LANES - 1 - lon)
        keys, lanes = permute(pos, [key.astype(jnp.float32), lane.astype(jnp.float32)], tiles)
        keys = keys.astype(jnp.int32)
        here = pl.ds(slot * tiles, tiles)
        key_ref[here, :] = keys
        lane_ref[here, :] = lanes.astype(jnp.int32)
        in_row = lax.div(keys, levels)
        first = jnp.minimum(in_row[:, :1], rows - WINDOW)
        last = in_row[:, LANES - 1 :]
        far = jnp.max(last - first, axis=0, keepdims=True)
        across_lanes = lambda v: jnp.broadcast_to(v.astype(jnp.float32), (tiles, 128)).T[:1].astype(jnp.int32)
        first_ref[pl.ds(slot, 1), :] = across_lanes(first)
        last_ref[pl.ds(slot, 1), :] = across_lanes(last)
        far_ref[pl.ds(slot, 1), :] = far


def arrange_kernel(pos_ref, innov_ref, weight_ref, quality_ref, keep_ref, want_ref):
    slots, obs = pos_ref.shape
    tiles = obs // LANES
    for slot in range(slots):
        at = pl.ds(slot, 1)
        keep = quality_ref[at, :].astype(jnp.float32) * weight_ref[at, :]
        values = []
        for value in (keep, innov_ref[at, :]):
            first = value.astype(jnp.bfloat16).astype(jnp.float32)
            values += [first, value - first]
        moved = permute(pos_ref[at, :], values, tiles)
        here = pl.ds(slot * tiles, tiles)
        keep_ref[here, :] = moved[0] + moved[1]
        want_ref[here, :] = moved[2] + moved[3]


def place_of(key, lane, start, levels):
    half = lane < 0
    return key - start * levels + jnp.where(half, WINDOW * levels, 0), jnp.where(half, -1 - lane, lane)


def pick_kernel(
    low_ref, own_ref, high_ref, circ_high_ref, circ_low_ref, ens_ref, key_ref, lane_ref, first_ref, last_ref, far_ref,
    out_ref, local_ref, *part_refs,
):
    rows, levels, lons = own_ref.shape
    slots = ens_ref.shape[0]
    tiles = first_ref.shape[1]
    mixed = smooth_rows(low_ref[...], own_ref[...], high_ref[...]).reshape(rows * levels, lons)
    local_ref[...] = smooth_lons(mixed, circ_high_ref[...], circ_low_ref[...]).reshape(local_ref.shape)
    for slot in range(slots):
        field = ens_ref[slot].astype(jnp.float32) * local_ref[...]
        first = field.astype(jnp.bfloat16).astype(jnp.float32)
        part_refs[slot][...] = jnp.concatenate([first, field - first], axis=1).astype(jnp.bfloat16)
    place_ids = ids_of((2 * WINDOW * levels, LANES), 0)
    lane_ids = ids_of((LANES, LANES), 0)

    def found(slot, at, start, low_row):
        key, lane = key_ref[pl.ds(at, 1), :], lane_ref[pl.ds(at, 1), :]
        place, lane = place_of(key, lane, start, levels)
        if low_row is not None:
            place = jnp.where(lax.div(key, levels) < low_row, -1, place)
            place = jnp.where(lax.div(key, levels) >= start + WINDOW, -1, place)
        else:
            place = jnp.where(lax.div(key, levels) >= start + WINDOW, -1, place)
        part = part_refs[slot][pl.ds(start, WINDOW)].reshape(WINDOW * 2 * levels, lons)
        left = jnp.concatenate([part[:, :LANES], part[:, LANES:]], axis=0)
        both = jnp.dot(left, one_hot(lane_ids, lane), preferred_element_type=jnp.float32)
        both = both.reshape(2 * WINDOW, 2, levels, LANES)
        value = (both[:, 0] + both[:, 1]).reshape(2 * WINDOW * levels, LANES)
        return jnp.sum(jnp.where(place_ids == place, value, 0.0), axis=0, keepdims=True)

    @pl.loop(0, tiles)
    def _(tile):
        for slot in range(slots):
            at = slot * tiles + tile
            out_ref[pl.ds(at, 1), :] = found(slot, at, first_ref[slot, tile], None)

    for slot in range(slots):

        @pl.when(far_ref[slot, 0] >= WINDOW)
        def _():
            @pl.loop(0, tiles)
            def _(tile):
                at = slot * tiles + tile
                begin = first_ref[slot, tile]

                @pl.loop(1, lax.div(last_ref[slot, tile] - begin, WINDOW) + 1)
                def _(turn):
                    low_row = begin + turn * WINDOW
                    start = jnp.minimum(low_row, rows - WINDOW)
                    out_ref[pl.ds(at, 1), :] += found(slot, at, start, low_row)


def scatter_kernel(
    norm_scale, seen_ref, want_ref, keep_ref, key_ref, lane_ref, ens_ref, first_ref, last_ref, far_ref,
    back_ref, cost_ref, wres_ref, *grad_refs,
):
    slots, rows, levels, lons = ens_ref.shape
    tiles = first_ref.shape[1]
    resid = seen_ref[...] * norm_scale - want_ref[...]
    wres_ref[...] = keep_ref[...] * resid
    cost_ref[...] = jnp.sum(wres_ref[...] * resid).reshape(1, 1)
    place_ids = ids_of((2 * WINDOW * levels, LANES), 0)
    lane_ids = ids_of((LANES, LANES), 0)
    for slot in range(slots):
        grad_refs[slot][...] = jnp.zeros(grad_refs[slot].shape, jnp.float32)

    def spread(slot, at, start, low_row):
        key, lane = key_ref[pl.ds(at, 1), :], lane_ref[pl.ds(at, 1), :]
        place, lane = place_of(key, lane, start, levels)
        if low_row is not None:
            place = jnp.where(lax.div(key, levels) < low_row, -1, place)
        place = jnp.where(lax.div(key, levels) >= start + WINDOW, -1, place)
        wres = wres_ref[pl.ds(at, 1), :]
        first = wres.astype(jnp.bfloat16).astype(jnp.float32)
        chosen = place_ids == place
        left = jnp.concatenate([jnp.where(chosen, first, 0.0), jnp.where(chosen, wres - first, 0.0)], axis=0)
        both = across(left.astype(jnp.bfloat16), one_hot(lane_ids, lane))
        size = 2 * WINDOW * levels
        value = (both[:size] + both[size:]).reshape(2, WINDOW, levels, LANES)
        for half in range(2):
            grad_refs[slot][half, pl.ds(start, WINDOW)] += value[half]

    @pl.loop(0, tiles)
    def _(tile):
        for slot in range(slots):
            spread(slot, slot * tiles + tile, first_ref[slot, tile], None)

    for slot in range(slots):

        @pl.when(far_ref[slot, 0] >= WINDOW)
        def _():
            @pl.loop(0, tiles)
            def _(tile):
                begin = first_ref[slot, tile]

                @pl.loop(1, lax.div(last_ref[slot, tile] - begin, WINDOW) + 1)
                def _(turn):
                    low_row = begin + turn * WINDOW
                    spread(slot, slot * tiles + tile, jnp.minimum(low_row, rows - WINDOW), low_row)

    total = jnp.zeros((rows, levels, lons), jnp.float32)
    for slot in range(slots):
        grad = jnp.concatenate([grad_refs[slot][0], grad_refs[slot][1]], axis=2)
        total += ens_ref[slot].astype(jnp.float32) * grad
    back_ref[...] = total * norm_scale


def grad_kernel(low_ref, own_ref, high_ref, circ_high_ref, circ_low_ref, weights_ref, obs_cost_ref, grad_ref, sums_ref):
    rows, levels, lons = own_ref.shape
    mixed = smooth_rows(low_ref[...], own_ref[...], high_ref[...]).reshape(rows * levels, lons)
    weights = weights_ref[...].reshape(rows * levels, lons)
    grad = weights + smooth_lons(mixed, circ_high_ref[...], circ_low_ref[...])
    grad_ref[...] = grad.reshape(grad_ref.shape)
    lane = lax.broadcasted_iota(jnp.int32, sums_ref.shape, 1)
    prior = jnp.sum(weights * weights)
    square = jnp.sum(grad * grad)
    sums_ref[...] = jnp.where(lane == 0, square, jnp.where(lane == 1, prior, jnp.where(lane == 2, obs_cost_ref[...], 0.0)))


def call(body, out_shape, scratch, flops, *operands, scalars=()):
    vmem, smem = pl.BlockSpec(memory_space=pltpu.VMEM), pl.BlockSpec(memory_space=pltpu.SMEM)
    return pl.pallas_call(
        body,
        out_shape=out_shape,
        in_specs=[vmem] * len(operands) + [smem] * len(scalars),
        out_specs=jax.tree.map(lambda _: vmem, out_shape),
        scratch_shapes=scratch,
        compiler_params=pltpu.CompilerParams(vmem_limit_bytes=48 * MIB),
        cost_estimate=pl.CostEstimate(flops=flops, bytes_accessed=2 * MIB, transcendentals=0),
    )(*operands, *scalars)


def edges(field):
    count = lax.axis_size("lat")
    forward = [(i, i + 1) for i in range(count - 1)]
    backward = [(target, source) for source, target in forward]
    low = lax.ppermute(field[-HALF:], "lat", forward)
    high = lax.ppermute(field[:HALF], "lat", backward)
    return low, high


def summed(value, axis):
    count = lax.axis_size(axis)
    if count & (count - 1):
        return lax.psum(value, axis)
    away = 1
    while away < count:
        value = value + lax.ppermute(value, axis, [(i, i ^ away) for i in range(count)])
        away *= 2
    return value


def local(ensemble, weights, obs_cell, innovation, obs_weight, quality):
    _, rows, levels, lons = weights.shape
    slots, obs = obs_cell.shape
    members = lax.axis_size("mem")
    lat_count = lax.axis_size("lat")
    norm_scale = 1.0 / math.sqrt(members - 1)
    cells = rows * levels * lons
    ens, own = ensemble[0], weights[0]
    circ_high, circ_low = (jnp.asarray(part) for part in circulant_parts(lons))
    f32, i32 = jnp.float32, jnp.int32
    tiles = obs // LANES
    ordered = (slots * tiles, LANES)
    shape = (rows, levels, lons)
    like = jax.ShapeDtypeStruct
    low, high = edges(own)
    pos, key, lane, *bounds = call(
        functools.partial(sort_kernel, shape),
        (like((slots, obs), i32), like(ordered, i32), like(ordered, i32), like((slots, tiles), i32), like((slots, tiles), i32), like((slots, 1), i32)),
        [pltpu.VMEM((tiles * rows, 2 * LANES), f32)],
        10**9,
        obs_cell,
    )
    keep, want = call(
        arrange_kernel, (like(ordered, f32), like(ordered, f32)), [], 10**9, pos, innovation, obs_weight, quality
    )
    picked = call(
        pick_kernel,
        like(ordered, f32),
        [pltpu.VMEM(shape, f32)] + [pltpu.VMEM((rows, 2 * levels, lons), jnp.bfloat16)] * slots,
        10**9,
        low, own, high, circ_high, circ_low, ens, key, lane,
        scalars=bounds,
    )
    seen = summed(picked, "mem")
    back, obs_cost = call(
        functools.partial(scatter_kernel, norm_scale),
        (like(shape, f32), like((1, 1), f32)),
        [pltpu.VMEM(ordered, f32)] + [pltpu.VMEM((2, rows, levels, LANES), f32)] * slots,
        10**9,
        seen, want, keep, key, lane, ens,
        scalars=bounds,
    )
    back_low, back_high = edges(back)
    grad, sums = call(
        grad_kernel,
        (jax.ShapeDtypeStruct((rows, levels, lons), f32), jax.ShapeDtypeStruct((1, 128), f32)),
        [],
        10**9,
        back_low, back, back_high, circ_high, circ_low, own, obs_cost,
    )
    totals = summed(summed(sums, "lat"), "mem")
    entries = f32(members * lat_count * cells)
    cost = (0.5 * totals[0, 1] + 0.5 * totals[0, 2] / members) / entries
    length = jnp.sqrt(totals[0, 0] / entries + EPSILON)
    new_weights = own - STEP_LENGTH * grad / length
    return new_weights[None], cost


def solution(mesh):
    placed = (
        P("mem", None, "lat", None, None),
        P("mem", "lat", None, None),
        P(None, "lat"),
        P(None, "lat"),
        P(None, "lat"),
        P(None, "lat"),
    )
    return jax.shard_map(
        local,
        mesh=mesh,
        in_specs=placed,
        out_specs=(P("mem", "lat", None, None), P()),
        check_vma=False,
    )
```

```python
import functools
import math

import jax
import jax.numpy as jnp
import numpy as np
from jax import lax
from jax.experimental import pallas as pl
from jax.experimental.pallas import tpu as pltpu
from jax.sharding import PartitionSpec as P

HALF = 8
STEP_LENGTH = 0.5
EPSILON = 1e-06
LANES = 256
GROUP = 1024
WINDOW = 3
UNROLL = 8
MIB = 1024 * 1024


def taps():
    sigma = HALF / 2.0
    every = np.arange(-HALF, HALF + 1).astype(np.float64)
    normal = np.sqrt(np.sum(np.exp(-((every / sigma) ** 2))))
    return np.exp(-0.5 * (every / sigma) ** 2) / normal


def circulant_parts(lon_count):
    full = np.zeros((lon_count, lon_count), np.float32)
    at = np.arange(lon_count)
    for shift_by, tap in zip(range(-HALF, HALF + 1), taps()):
        full[at, (at + shift_by) % lon_count] += np.float32(tap)
    high = full.astype(jnp.bfloat16)
    low = (full - high.astype(np.float32)).astype(jnp.bfloat16)
    return high, low


def two_parts(value):
    high = value.astype(jnp.bfloat16)
    low = (value - high.astype(jnp.float32)).astype(jnp.bfloat16)
    return high, low


def smooth_rows(low, own, high):
    tap = [float(t) for t in taps()]
    padded = jnp.concatenate([low, own, high], axis=0)
    rows = own.shape[0]
    total = padded[HALF : HALF + rows] * tap[HALF]
    for away in range(1, HALF + 1):
        pair = padded[HALF - away : HALF - away + rows] + padded[HALF + away : HALF + away + rows]
        total = total + pair * tap[HALF + away]
    return total


def smooth_lons(field, circ_high, circ_low):
    first, second = two_parts(field)
    dot = functools.partial(jnp.dot, preferred_element_type=jnp.float32)
    return dot(first, circ_high) + (dot(second, circ_high) + dot(first, circ_low))


def quotient(value, by):
    if by & (by - 1):
        return lax.div(value, by), lax.rem(value, by)
    return lax.shift_right_logical(value, by.bit_length() - 1), lax.bitwise_and(value, by - 1)


def small_ids(shape):
    return lax.broadcasted_iota(jnp.int32, shape, 0).astype(jnp.bfloat16)


def one_hot(ids, at):
    return jnp.where(ids == at, jnp.bfloat16(1), jnp.bfloat16(0))


def ids_of(shape, dim):
    return lax.broadcasted_iota(jnp.int32, shape, dim)


def across(left, right):
    return lax.dot_general(left, right, (((1,), (1,)), ((), ())), preferred_element_type=jnp.float32)


def permute(pos, values, tiles):
    hi_ids, lo_ids = small_ids((tiles, GROUP)), small_ids((LANES, GROUP))
    hi, lo = (part.astype(jnp.float32).astype(jnp.bfloat16) for part in quotient(pos, LANES))
    total = jnp.zeros((len(values) * tiles, LANES), jnp.float32)
    for at in range(0, pos.shape[1], GROUP):
        here = slice(at, at + GROUP)
        chosen = hi_ids == hi[:, here]
        left = jnp.concatenate([jnp.where(chosen, v[:, here], jnp.bfloat16(0)) for v in values], axis=0)
        total += across(left, one_hot(lo_ids, lo[:, here]))
    return [total[k * tiles : (k + 1) * tiles] for k in range(len(values))]


def sort_kernel(shape, cell_ref, pos_ref, place_ref, lane_ref, first_ref, last_ref, far_ref, prefix_ref):
    rows, levels, lons = shape
    slots, obs = cell_ref.shape
    tiles = obs // LANES
    row_ids = small_ids((rows, LANES))
    square = (LANES, LANES)
    upper = (ids_of(square, 0) <= ids_of(square, 1)).astype(jnp.bfloat16)
    counting = jnp.concatenate([upper, jnp.ones((LANES, 128), jnp.bfloat16)], axis=1)
    before = (ids_of((rows, rows), 1) < ids_of((rows, rows), 0)).astype(jnp.float32)
    wide = lambda v: jnp.concatenate([v] * (LANES // 128), axis=1)
    _, cells = quotient(cell_ref[...], rows * levels * lons)
    keys, lons_of = quotient(cells, lons)
    rows_of, _ = quotient(keys, levels)
    signed = jnp.where(lons_of < LANES, lons_of, LANES - 1 - lons_of)
    keys, rows_of, signed = (v.astype(jnp.float32).astype(jnp.bfloat16) for v in (keys, rows_of, signed))
    for slot in range(slots):
        row = rows_of[slot : slot + 1]
        hots = [one_hot(row_ids, row[:, at * LANES : (at + 1) * LANES]) for at in range(tiles)]
        prefix_ref[...] = jnp.dot(jnp.concatenate(hots, axis=0), counting, preferred_element_type=jnp.float32)
        total = jnp.zeros((rows, 128), jnp.float32)
        for at in range(tiles):
            total += prefix_ref[pl.ds(at * rows, rows), pl.ds(LANES, 128)]
        carry = jnp.dot(before, total, precision=lax.Precision.HIGHEST, preferred_element_type=jnp.float32) - 1.0
        places = []
        for at in range(tiles):
            here = pl.ds(at * rows, rows)
            place = (prefix_ref[here, pl.ds(0, LANES)] + wide(carry)) * hots[at].astype(jnp.float32)
            places.append(jnp.sum(place, axis=0, keepdims=True))
            carry += prefix_ref[here, pl.ds(LANES, 128)]
        pos = jnp.concatenate(places, axis=1).astype(jnp.int32)
        pos_ref[pl.ds(slot, 1), :] = pos
        key, lane = permute(pos, [keys[slot : slot + 1], signed[slot : slot + 1]], tiles)
        key, lane = key.astype(jnp.int32), lane.astype(jnp.int32)
        row, level = quotient(key, levels)
        second = lane < 0
        here = pl.ds(slot * tiles, tiles)
        place_ref[here, :] = (2 * row + jnp.where(second, 1, 0)) * levels + level
        lane_ref[here, :] = jnp.where(second, -1 - lane, lane).astype(jnp.float32)
        first = jnp.minimum(row[:, :1], rows - WINDOW)
        last = row[:, LANES - 1 :]
        far = jnp.max(last - first, axis=0, keepdims=True)
        as_row = lambda v: jnp.broadcast_to(v.astype(jnp.float32), (tiles, 128)).T[:1].astype(jnp.int32)
        first_ref[pl.ds(slot, 1), :] = as_row(first)
        last_ref[pl.ds(slot, 1), :] = as_row(last)
        far_ref[pl.ds(slot, 1), :] = far


def arrange_kernel(pos_ref, innov_ref, weight_ref, quality_ref, keep_ref, want_ref):
    slots, obs = pos_ref.shape
    tiles = obs // LANES
    keeps = two_parts(quality_ref[...].astype(jnp.float32) * weight_ref[...])
    wants = two_parts(innov_ref[...])
    for slot in range(slots):
        at = slice(slot, slot + 1)
        moved = permute(pos_ref[at, :], [part[at] for part in keeps + wants], tiles)
        here = pl.ds(slot * tiles, tiles)
        keep_ref[here, :] = moved[0] + moved[1]
        want_ref[here, :] = moved[2] + moved[3]


def window_places(place_ref, at, start, low_row, levels):
    place = place_ref[pl.ds(at, 1), :] - start * (2 * levels)
    if low_row is None:
        return place
    return jnp.where(place < (low_row - start) * (2 * levels), -1, place)


def over_windows(tiles, slots, rows, first_ref, last_ref, far_ref, unroll, step):
    @pl.loop(0, tiles, unroll=unroll)
    def _(tile):
        for slot in range(slots):
            step(slot, tile, first_ref[slot, tile], None)

    for slot in range(slots):

        @pl.when(far_ref[slot, 0] >= WINDOW)
        def _():
            @pl.loop(0, tiles)
            def _(tile):
                begin = first_ref[slot, tile]

                @pl.loop(1, lax.div(last_ref[slot, tile] - begin, WINDOW) + 1)
                def _(turn):
                    low_row = begin + turn * WINDOW
                    step(slot, tile, jnp.minimum(low_row, rows - WINDOW), low_row)


def pick_kernel(sides, *refs):
    low, high = halo(refs[:sides])
    own_ref, circ_high_ref, circ_low_ref, ens_ref, place_ref, lane_ref, *refs = refs[sides:]
    first_ref, last_ref, far_ref, out_ref, local_ref, *part_refs = refs
    rows, levels, lons = own_ref.shape
    slots = ens_ref.shape[0]
    tiles = first_ref.shape[1]
    mixed = smooth_rows(low, own_ref[...], high).reshape(rows * levels, lons)
    local_ref[...] = smooth_lons(mixed, circ_high_ref[...], circ_low_ref[...]).reshape(local_ref.shape)
    for slot in range(slots):
        field = ens_ref[slot].astype(jnp.float32) * local_ref[...]
        first = field.astype(jnp.bfloat16).astype(jnp.float32)
        part_refs[slot][...] = jnp.concatenate([first, field - first], axis=1).astype(jnp.bfloat16)
    size = 2 * WINDOW * levels
    place_ids = ids_of((size, LANES), 0)
    lane_ids = small_ids((LANES, LANES))

    def step(slot, tile, start, low_row):
        at = slot * tiles + tile
        place = window_places(place_ref, at, start, low_row, levels)
        part = part_refs[slot][pl.ds(start, WINDOW)]
        left = jnp.stack([part[:, :, :LANES], part[:, :, LANES:]], axis=1).reshape(2 * size, LANES)
        hot = one_hot(lane_ids, lane_ref[pl.ds(at, 1), :].astype(jnp.bfloat16))
        both = jnp.dot(left, hot, preferred_element_type=jnp.float32).reshape(2 * WINDOW, 2, levels, LANES)
        value = (both[:, 0] + both[:, 1]).reshape(size, LANES)
        value = jnp.sum(jnp.where(place_ids == place, value, 0.0), axis=0, keepdims=True)
        if low_row is None:
            out_ref[pl.ds(at, 1), :] = value
        else:
            out_ref[pl.ds(at, 1), :] += value

    over_windows(tiles, slots, rows, first_ref, last_ref, far_ref, UNROLL, step)


def scatter_kernel(
    norm_scale, seen_ref, want_ref, keep_ref, place_ref, lane_ref, ens_ref, first_ref, last_ref, far_ref,
    back_ref, cost_ref, wres_ref, *grad_refs,
):
    slots, rows, levels, lons = ens_ref.shape
    tiles = first_ref.shape[1]
    resid = seen_ref[...] * norm_scale - want_ref[...]
    wres_ref[...] = keep_ref[...] * resid
    cost_ref[...] = jnp.sum(wres_ref[...] * resid).reshape(1, 1)
    size = 2 * WINDOW * levels
    place_ids = ids_of((size, LANES), 0)
    lane_ids = small_ids((LANES, LANES))
    for slot in range(slots):
        grad_refs[slot][...] = jnp.zeros(grad_refs[slot].shape, jnp.float32)

    def step(slot, tile, start, low_row):
        at = slot * tiles + tile
        place = window_places(place_ref, at, start, low_row, levels)
        wres = wres_ref[pl.ds(at, 1), :]
        first = wres.astype(jnp.bfloat16).astype(jnp.float32)
        chosen = place_ids == place
        left = jnp.concatenate([jnp.where(chosen, first, 0.0), jnp.where(chosen, wres - first, 0.0)], axis=0)
        hot = one_hot(lane_ids, lane_ref[pl.ds(at, 1), :].astype(jnp.bfloat16))
        both = across(left.astype(jnp.bfloat16), hot)
        grad_refs[slot][pl.ds(start, WINDOW)] += (both[:size] + both[size:]).reshape(WINDOW, 2, levels, LANES)

    over_windows(tiles, slots, rows, first_ref, last_ref, far_ref, UNROLL, step)
    total = jnp.zeros((rows, levels, lons), jnp.float32)
    for slot in range(slots):
        grad = jnp.concatenate([grad_refs[slot][:, 0], grad_refs[slot][:, 1]], axis=2)
        total += ens_ref[slot].astype(jnp.float32) * grad
    back_ref[...] = total * norm_scale


def grad_kernel(sides, *refs):
    low, high = halo(refs[:sides])
    own_ref, circ_high_ref, circ_low_ref, weights_ref, obs_cost_ref, grad_ref, sums_ref = refs[sides:]
    rows, levels, lons = own_ref.shape
    mixed = smooth_rows(low, own_ref[...], high).reshape(rows * levels, lons)
    weights = weights_ref[...].reshape(rows * levels, lons)
    grad = weights + smooth_lons(mixed, circ_high_ref[...], circ_low_ref[...])
    grad_ref[...] = grad.reshape(grad_ref.shape)
    lane = lax.broadcasted_iota(jnp.int32, sums_ref.shape, 1)
    prior = jnp.sum(weights * weights)
    square = jnp.sum(grad * grad)
    sums_ref[...] = jnp.where(lane == 0, square, jnp.where(lane == 1, prior, jnp.where(lane == 2, obs_cost_ref[...], 0.0)))


def update_kernel(members, entries, sums_ref, own_ref, grad_ref, new_ref, cost_ref):
    totals = jnp.sum(sums_ref[...], axis=0, keepdims=True)
    length = jnp.sqrt(totals[:, :1] / entries + EPSILON)
    new_ref[...] = own_ref[...] - grad_ref[...] * (STEP_LENGTH / length)[None]
    cost_ref[...] = (0.5 * totals[:, 1:2] + 0.5 * totals[:, 2:3] / members) / entries


def call(body, out_shape, scratch, flops, *operands, scalars=()):
    vmem, smem = pl.BlockSpec(memory_space=pltpu.VMEM), pl.BlockSpec(memory_space=pltpu.SMEM)
    return pl.pallas_call(
        body,
        out_shape=out_shape,
        in_specs=[vmem] * len(operands) + [smem] * len(scalars),
        out_specs=jax.tree.map(lambda _: vmem, out_shape),
        scratch_shapes=scratch,
        compiler_params=pltpu.CompilerParams(vmem_limit_bytes=48 * MIB),
        cost_estimate=pl.CostEstimate(flops=flops, bytes_accessed=2 * MIB, transcendentals=0),
    )(*operands, *scalars)


def edges(field):
    count = lax.axis_size("lat")
    if count == 2:
        rows = field.shape[0]
        start = (rows - HALF) * (1 - lax.axis_index("lat"))
        return swapped(lax.dynamic_slice_in_dim(field, start, HALF, 0))
    forward = [(i, i + 1) for i in range(count - 1)]
    backward = [(target, source) for source, target in forward]
    low = lax.ppermute(field[-HALF:], "lat", forward)
    high = lax.ppermute(field[:HALF], "lat", backward)
    return [low, high]


def swapped(edge):
    return [lax.ppermute(edge, "lat", [(0, 1), (1, 0)])]


def halo(refs):
    if len(refs) == 2:
        return refs[0][...], refs[1][...]
    last = lax.axis_index("lat") == 1
    return jnp.where(last, refs[0][...], 0.0), jnp.where(last, 0.0, refs[0][...])


def summed(value, axis):
    count = lax.axis_size(axis)
    if count & (count - 1):
        return lax.psum(value, axis)
    away = 1
    while away < count:
        value = value + lax.ppermute(value, axis, [(i, i ^ away) for i in range(count)])
        away *= 2
    return value


def like(shape, kind=jnp.float32):
    return jax.ShapeDtypeStruct(shape, kind)


def sort_cells(obs_cell, shape):
    slots, obs = obs_cell.shape
    tiles = obs // LANES
    whole, ordered, bound = (slots, obs), (slots * tiles, LANES), (slots, tiles)
    kinds = [like(whole, jnp.int32), like(ordered, jnp.int32), like(ordered)]
    kinds += [like(bound, jnp.int32), like(bound, jnp.int32), like((slots, 1), jnp.int32)]
    scratch = [pltpu.VMEM((tiles * shape[0], LANES + 128), jnp.float32)]
    pos, place, lane, *bounds = call(functools.partial(sort_kernel, shape), kinds, scratch, 10**9, obs_cell)
    return pos, (place, lane), bounds


def arrange(pos, innovation, obs_weight, quality):
    ordered = like((pos.size // LANES, LANES))
    return call(arrange_kernel, [ordered, ordered], [], 10**9, pos, innovation, obs_weight, quality)


def pick(sides, own, circ, ens, at, bounds):
    rows, levels, lons = own.shape
    scratch = [pltpu.VMEM(own.shape, jnp.float32)]
    scratch += [pltpu.VMEM((rows, 2 * levels, lons), jnp.bfloat16)] * ens.shape[0]
    body = functools.partial(pick_kernel, len(sides))
    return call(body, like(at[0].shape), scratch, 10**9, *sides, own, *circ, ens, *at, scalars=bounds)


def scatter(seen, want, keep, ens, at, bounds, norm_scale):
    slots, rows, levels, lons = ens.shape
    scratch = [pltpu.VMEM(seen.shape, jnp.float32)]
    scratch += [pltpu.VMEM((rows, 2, levels, LANES), jnp.float32)] * slots
    kinds = [like((rows, levels, lons)), like((1, 1))]
    body = functools.partial(scatter_kernel, norm_scale)
    return call(body, kinds, scratch, 10**9, seen, want, keep, *at, ens, scalars=bounds)


def gradient(sides, own, circ, weights, obs_cost, devices):
    kinds = [like(own.shape), like((devices, 128))]
    body = functools.partial(grad_kernel, len(sides))
    return call(body, kinds, [], 10**9, *sides, own, *circ, weights, obs_cost)


def local(ensemble, weights, obs_cell, innovation, obs_weight, quality):
    _, rows, levels, lons = weights.shape
    members, bands = lax.axis_size("mem"), lax.axis_size("lat")
    norm_scale = 1.0 / math.sqrt(members - 1)
    ens, own = ensemble[0], weights[0]
    circ = [jnp.asarray(part) for part in circulant_parts(lons)]
    sides = edges(own)
    pos, at, bounds = sort_cells(obs_cell, own.shape)
    keep, want = arrange(pos, innovation, obs_weight, quality)
    picked = pick(sides, own, circ, ens, at, bounds)
    seen = summed(picked, "mem")
    back, obs_cost = scatter(seen, want, keep, ens, at, bounds, norm_scale)
    grad, sums = gradient(edges(back), back, circ, own, obs_cost, members * bands)
    sums = lax.all_to_all(sums, ("mem", "lat"), 0, 0, tiled=True)
    body = functools.partial(update_kernel, members, float(members * bands * rows * levels * lons))
    new_weights, cost = call(body, [like(own.shape), like((1, 1))], [], 10**8, sums, own, grad)
    return new_weights[None], cost[0, 0]


def solution(mesh):
    placed = (
        P("mem", None, "lat", None, None),
        P("mem", "lat", None, None),
        P(None, "lat"),
        P(None, "lat"),
        P(None, "lat"),
        P(None, "lat"),
    )
    return jax.shard_map(
        local,
        mesh=mesh,
        in_specs=placed,
        out_specs=(P("mem", "lat", None, None), P()),
        check_vma=False,
    )
```

```python
import functools
import math

import jax
import jax.numpy as jnp
import numpy as np
from jax import lax
from jax.experimental import pallas as pl
from jax.experimental.pallas import tpu as pltpu
from jax.sharding import PartitionSpec as P

HALF = 8
STEP_LENGTH = 0.5
EPSILON = 1e-06
LANES = 256
PIECE = 128
PICK_LONS = 256
SCATTER_LONS = 128
GROUP = 1024
BIN = 2
WINDOW = 2 * BIN
PICK_UNROLL = 16
SCATTER_UNROLL = 16
MIB = 1024 * 1024


def taps():
    sigma = HALF / 2.0
    every = np.arange(-HALF, HALF + 1).astype(np.float64)
    normal = np.sqrt(np.sum(np.exp(-((every / sigma) ** 2))))
    return np.exp(-0.5 * (every / sigma) ** 2) / normal


def circulant_parts(lon_count):
    full = np.zeros((lon_count, lon_count), np.float32)
    at = np.arange(lon_count)
    for shift_by, tap in zip(range(-HALF, HALF + 1), taps()):
        full[at, (at + shift_by) % lon_count] += np.float32(tap)
    high = full.astype(jnp.bfloat16)
    low = (full - high.astype(np.float32)).astype(jnp.bfloat16)
    return high, low


def two_parts(value):
    high = value.astype(jnp.bfloat16)
    low = (value - high.astype(jnp.float32)).astype(jnp.bfloat16)
    return high, low


def smooth_rows(low, own, high):
    tap = [float(t) for t in taps()]
    padded = jnp.concatenate([low, own, high], axis=0)
    rows = own.shape[0]
    total = padded[HALF : HALF + rows] * tap[HALF]
    for away in range(1, HALF + 1):
        pair = padded[HALF - away : HALF - away + rows] + padded[HALF + away : HALF + away + rows]
        total = total + pair * tap[HALF + away]
    return total


def smooth_lons(field, circ_high, circ_low):
    first, second = two_parts(field)
    dot = functools.partial(jnp.dot, preferred_element_type=jnp.float32)
    return dot(first, circ_high) + (dot(second, circ_high) + dot(first, circ_low))


def quotient(value, by):
    if by & (by - 1):
        return lax.div(value, by), lax.rem(value, by)
    return lax.shift_right_logical(value, by.bit_length() - 1), lax.bitwise_and(value, by - 1)


def small_ids(shape):
    return lax.broadcasted_iota(jnp.int32, shape, 0).astype(jnp.bfloat16)


def one_hot(ids, at):
    return jnp.where(ids == at, jnp.bfloat16(1), jnp.bfloat16(0))


def ids_of(shape, dim):
    return lax.broadcasted_iota(jnp.int32, shape, dim)


def across(left, right):
    return lax.dot_general(left, right, (((1,), (1,)), ((), ())), preferred_element_type=jnp.float32)


def permute(pos, values, pieces):
    hi_ids, lo_ids = small_ids((pieces, GROUP)), small_ids((PIECE, GROUP))
    hi, lo = (part.astype(jnp.float32).astype(jnp.bfloat16) for part in quotient(pos, PIECE))
    total = jnp.zeros((len(values) * pieces, PIECE), jnp.float32)
    for at in range(0, pos.shape[1], GROUP):
        here = slice(at, at + GROUP)
        chosen = hi_ids == hi[:, here]
        left = jnp.concatenate([jnp.where(chosen, v[:, here], jnp.bfloat16(0)) for v in values], axis=0)
        total += across(left, one_hot(lo_ids, lo[:, here]))
    return [total[k * pieces : (k + 1) * pieces] for k in range(len(values))]


def sort_kernel(shape, cell_ref, pos_ref, *refs):
    *place_refs, first_ref, last_ref, far_ref, prefix_ref = refs
    rows, levels, lons = shape
    slots, obs = cell_ref.shape
    tiles, pieces = obs // LANES, obs // PIECE
    bins = rows // BIN
    bin_ids = small_ids((bins, LANES))
    square = (LANES, LANES)
    upper = (ids_of(square, 0) <= ids_of(square, 1)).astype(jnp.bfloat16)
    counting = jnp.concatenate([upper, jnp.ones((LANES, 128), jnp.bfloat16)], axis=1)
    before = (ids_of((bins, bins), 1) < ids_of((bins, bins), 0)).astype(jnp.float32)
    wide = lambda v: jnp.concatenate([v] * (LANES // 128), axis=1)
    _, cells = quotient(cell_ref[...], rows * levels * lons)
    keys, lons_of = quotient(cells, lons)
    bins_of, _ = quotient(keys, levels * BIN)
    middle = lons // 2
    signed = jnp.where(lons_of < middle, lons_of, middle - 1 - lons_of)
    keys, bins_of, signed = (v.astype(jnp.float32).astype(jnp.bfloat16) for v in (keys, bins_of, signed))
    for slot in range(slots):
        group = bins_of[slot : slot + 1]
        hots = [one_hot(bin_ids, group[:, at * LANES : (at + 1) * LANES]) for at in range(tiles)]
        prefix_ref[...] = jnp.dot(jnp.concatenate(hots, axis=0), counting, preferred_element_type=jnp.float32)
        total = jnp.zeros((bins, 128), jnp.float32)
        for at in range(tiles):
            total += prefix_ref[pl.ds(at * bins, bins), pl.ds(LANES, 128)]
        carry = jnp.dot(before, total, precision=lax.Precision.HIGHEST, preferred_element_type=jnp.float32) - 1.0
        places = []
        for at in range(tiles):
            here = pl.ds(at * bins, bins)
            place = (prefix_ref[here, pl.ds(0, LANES)] + wide(carry)) * hots[at].astype(jnp.float32)
            places.append(jnp.sum(place, axis=0, keepdims=True))
            carry += prefix_ref[here, pl.ds(LANES, 128)]
        pos = jnp.concatenate(places, axis=1).astype(jnp.int32)
        pos_ref[pl.ds(slot, 1), :] = pos
        key, lane = permute(pos, [keys[slot : slot + 1], signed[slot : slot + 1]], pieces)
        key, lane = key.astype(jnp.int32), lane.astype(jnp.int32)
        row, level = quotient(key, levels)
        lon = jnp.where(lane < 0, middle - 1 - lane, lane)
        here = pl.ds(slot * pieces, pieces)
        for near, place_ref, lane_ref in zip((PICK_LONS, SCATTER_LONS), place_refs[::2], place_refs[1::2]):
            part, lane = quotient(lon, near)
            place_ref[here, :] = (row * (lons // near) + part) * levels + level
            lane_ref[here, :] = lane.astype(jnp.float32)
        group = quotient(row, BIN)[0] * BIN
        first = jnp.minimum(group[:, :1], rows - WINDOW)
        last = group[:, PIECE - 1 :] + BIN - 1
        begin = jnp.concatenate([first[:1], first[:-1]], axis=0)
        ends_tile = quotient(ids_of((pieces, 1), 0), LANES // PIECE)[1] == LANES // PIECE - 1
        far = jnp.max(jnp.where(ends_tile, last - begin, 0), axis=0, keepdims=True)
        as_row = lambda v: jnp.broadcast_to(v.astype(jnp.float32), (pieces, 128)).T[:1].astype(jnp.int32)
        first_ref[pl.ds(slot, 1), :] = as_row(first)
        last_ref[pl.ds(slot, 1), :] = as_row(last)
        far_ref[pl.ds(slot, 1), :] = far


def arrange_kernel(pos_ref, innov_ref, weight_ref, quality_ref, keep_ref, want_ref):
    slots, obs = pos_ref.shape
    pieces = obs // PIECE
    keeps = two_parts(quality_ref[...].astype(jnp.float32) * weight_ref[...])
    wants = two_parts(innov_ref[...])
    for slot in range(slots):
        at = slice(slot, slot + 1)
        moved = permute(pos_ref[at, :], [part[at] for part in keeps + wants], pieces)
        here = pl.ds(slot * pieces, pieces)
        keep_ref[here, :] = moved[0] + moved[1]
        want_ref[here, :] = moved[2] + moved[3]


def tile_row(ref, at):
    parts = LANES // PIECE
    return jnp.concatenate([ref[pl.ds(at * parts + k, 1), :] for k in range(parts)], axis=1)


def window_places(place_ref, at, start, low_row, per_row):
    place = tile_row(place_ref, at) - start * per_row
    if low_row is None:
        return place
    return jnp.where(place < (low_row - start) * per_row, -1, place)


def over_windows(tiles, slots, rows, first_ref, last_ref, far_ref, unroll, step):
    @pl.loop(0, tiles, unroll=unroll)
    def _(tile):
        for slot in range(slots):
            step(slot, tile, first_ref[slot, tile * (LANES // PIECE)], None)

    for slot in range(slots):

        @pl.when(far_ref[slot, 0] >= WINDOW)
        def _():
            @pl.loop(0, tiles)
            def _(tile):
                begin = first_ref[slot, tile * (LANES // PIECE)]

                @pl.loop(1, lax.div(last_ref[slot, (tile + 1) * (LANES // PIECE) - 1] - begin, WINDOW) + 1)
                def _(turn):
                    low_row = begin + turn * WINDOW
                    step(slot, tile, jnp.minimum(low_row, rows - WINDOW), low_row)


def pick_kernel(sides, *refs):
    low, high = halo(refs[:sides])
    own_ref, circ_high_ref, circ_low_ref, ens_ref, place_ref, lane_ref, *refs = refs[sides:]
    first_ref, last_ref, far_ref, out_ref, local_ref, *part_refs = refs
    rows, levels, lons = own_ref.shape
    slots = ens_ref.shape[0]
    tiles = first_ref.shape[1] // (LANES // PIECE)
    mixed = smooth_rows(low, own_ref[...], high).reshape(rows * levels, lons)
    local_ref[...] = smooth_lons(mixed, circ_high_ref[...], circ_low_ref[...]).reshape(local_ref.shape)
    for slot in range(slots):
        field = ens_ref[slot].astype(jnp.float32) * local_ref[...]
        first = field.astype(jnp.bfloat16).astype(jnp.float32)
        part_refs[slot][...] = jnp.concatenate([first, field - first], axis=1).astype(jnp.bfloat16)
    parts = lons // PICK_LONS
    size = WINDOW * parts * levels
    place_ids = ids_of((size, LANES), 0)
    lane_ids = small_ids((PICK_LONS, LANES))

    def step(slot, tile, start, low_row):
        at = slot * tiles + tile
        place = window_places(place_ref, at, start, low_row, parts * levels)
        part = part_refs[slot][pl.ds(start, WINDOW)]
        left = jnp.stack([part[:, :, k * PICK_LONS : (k + 1) * PICK_LONS] for k in range(parts)], axis=1).reshape(2 * size, PICK_LONS)
        hot = one_hot(lane_ids, tile_row(lane_ref, at).astype(jnp.bfloat16))
        both = jnp.dot(left, hot, preferred_element_type=jnp.float32).reshape(WINDOW * parts, 2, levels, LANES)
        value = (both[:, 0] + both[:, 1]).reshape(size, LANES)
        value = jnp.sum(jnp.where(place_ids == place, value, 0.0), axis=0, keepdims=True)
        for k in range(LANES // PIECE):
            here, part = pl.ds(at * (LANES // PIECE) + k, 1), value[:, k * PIECE : (k + 1) * PIECE]
            out_ref[here, :] = part if low_row is None else out_ref[here, :] + part

    over_windows(tiles, slots, rows, first_ref, last_ref, far_ref, PICK_UNROLL, step)


def scatter_kernel(
    norm_scale, seen_ref, want_ref, keep_ref, place_ref, lane_ref, ens_ref, first_ref, last_ref, far_ref,
    back_ref, cost_ref, wres_ref, *grad_refs,
):
    slots, rows, levels, lons = ens_ref.shape
    tiles = first_ref.shape[1] // (LANES // PIECE)
    resid = seen_ref[...] * norm_scale - want_ref[...]
    wres_ref[...] = keep_ref[...] * resid
    cost_ref[...] = jnp.sum(wres_ref[...] * resid).reshape(1, 1)
    parts = lons // SCATTER_LONS
    size = WINDOW * parts * levels
    place_ids = small_ids((size, LANES))
    lane_ids = small_ids((SCATTER_LONS, LANES))
    for slot in range(slots):
        grad_refs[slot][...] = jnp.zeros(grad_refs[slot].shape, jnp.float32)

    def step(slot, tile, start, low_row):
        at = slot * tiles + tile
        place = window_places(place_ref, at, start, low_row, parts * levels)
        chosen = place_ids == place.astype(jnp.float32).astype(jnp.bfloat16)
        left = [jnp.where(chosen, part, jnp.bfloat16(0)) for part in two_parts(tile_row(wres_ref, at))]
        left = jnp.concatenate(left, axis=0)
        hot = one_hot(lane_ids, tile_row(lane_ref, at).astype(jnp.bfloat16))
        both = across(left, hot)
        grad_refs[slot][pl.ds(start, WINDOW)] += (both[:size] + both[size:]).reshape(WINDOW, parts, levels, SCATTER_LONS)

    over_windows(tiles, slots, rows, first_ref, last_ref, far_ref, SCATTER_UNROLL, step)
    total = jnp.zeros((rows, levels, lons), jnp.float32)
    for slot in range(slots):
        grad = jnp.concatenate([grad_refs[slot][:, k] for k in range(parts)], axis=2)
        total += ens_ref[slot].astype(jnp.float32) * grad
    back_ref[...] = total * norm_scale


def grad_kernel(sides, *refs):
    low, high = halo(refs[:sides])
    own_ref, circ_high_ref, circ_low_ref, weights_ref, obs_cost_ref, grad_ref, sums_ref = refs[sides:]
    rows, levels, lons = own_ref.shape
    mixed = smooth_rows(low, own_ref[...], high).reshape(rows * levels, lons)
    weights = weights_ref[...].reshape(rows * levels, lons)
    grad = weights + smooth_lons(mixed, circ_high_ref[...], circ_low_ref[...])
    grad_ref[...] = grad.reshape(grad_ref.shape)
    lane = lax.broadcasted_iota(jnp.int32, sums_ref.shape, 1)
    prior = jnp.sum(weights * weights)
    square = jnp.sum(grad * grad)
    sums_ref[...] = jnp.where(lane == 0, square, jnp.where(lane == 1, prior, jnp.where(lane == 2, obs_cost_ref[...], 0.0)))


def update_kernel(members, entries, sums_ref, own_ref, grad_ref, new_ref, cost_ref):
    totals = jnp.sum(sums_ref[...], axis=0, keepdims=True)
    length = jnp.sqrt(totals[:, :1] / entries + EPSILON)
    new_ref[...] = own_ref[...] - grad_ref[...] * (STEP_LENGTH / length)[None]
    cost_ref[...] = (0.5 * totals[:, 1:2] + 0.5 * totals[:, 2:3] / members) / entries


def call(body, out_shape, scratch, flops, *operands, scalars=()):
    vmem, smem = pl.BlockSpec(memory_space=pltpu.VMEM), pl.BlockSpec(memory_space=pltpu.SMEM)
    return pl.pallas_call(
        body,
        out_shape=out_shape,
        in_specs=[vmem] * len(operands) + [smem] * len(scalars),
        out_specs=jax.tree.map(lambda _: vmem, out_shape),
        scratch_shapes=scratch,
        compiler_params=pltpu.CompilerParams(vmem_limit_bytes=48 * MIB),
        cost_estimate=pl.CostEstimate(flops=flops, bytes_accessed=2 * MIB, transcendentals=0),
    )(*operands, *scalars)


def edges(field):
    count = lax.axis_size("lat")
    if count == 2:
        rows = field.shape[0]
        start = (rows - HALF) * (1 - lax.axis_index("lat"))
        return swapped(lax.dynamic_slice_in_dim(field, start, HALF, 0))
    forward = [(i, i + 1) for i in range(count - 1)]
    backward = [(target, source) for source, target in forward]
    low = lax.ppermute(field[-HALF:], "lat", forward)
    high = lax.ppermute(field[:HALF], "lat", backward)
    return [low, high]


def swapped(edge):
    return [lax.ppermute(edge, "lat", [(0, 1), (1, 0)])]


def halo(refs):
    if len(refs) == 2:
        return refs[0][...], refs[1][...]
    last = lax.axis_index("lat") == 1
    return jnp.where(last, refs[0][...], 0.0), jnp.where(last, 0.0, refs[0][...])


def summed(value, axis):
    count = lax.axis_size(axis)
    if count & (count - 1):
        return lax.psum(value, axis)
    away = 1
    while away < count:
        value = value + lax.ppermute(value, axis, [(i, i ^ away) for i in range(count)])
        away *= 2
    return value


def like(shape, kind=jnp.float32):
    return jax.ShapeDtypeStruct(shape, kind)


def sort_cells(obs_cell, shape):
    slots, obs = obs_cell.shape
    tiles = obs // LANES
    whole, ordered, bound = (slots, obs), (slots * obs // PIECE, PIECE), (slots, obs // PIECE)
    kinds = [like(whole, jnp.int32)] + [like(ordered, jnp.int32), like(ordered)] * 2
    kinds += [like(bound, jnp.int32), like(bound, jnp.int32), like((slots, 1), jnp.int32)]
    scratch = [pltpu.VMEM((tiles * shape[0] // BIN, LANES + 128), jnp.float32)]
    pos, *ats, first, last, far = call(functools.partial(sort_kernel, shape), kinds, scratch, 10**9, obs_cell)
    return pos, ats[:2], ats[2:], (first, last, far)


def arrange(pos, innovation, obs_weight, quality):
    ordered = like((pos.size // PIECE, PIECE))
    return call(arrange_kernel, [ordered, ordered], [], 10**9, pos, innovation, obs_weight, quality)


def pick(sides, own, circ, ens, at, bounds):
    rows, levels, lons = own.shape
    scratch = [pltpu.VMEM(own.shape, jnp.float32)]
    scratch += [pltpu.VMEM((rows, 2 * levels, lons), jnp.bfloat16)] * ens.shape[0]
    body = functools.partial(pick_kernel, len(sides))
    return call(body, like(at[0].shape), scratch, 10**9, *sides, own, *circ, ens, *at, scalars=bounds)


def scatter(seen, want, keep, ens, at, bounds, norm_scale):
    slots, rows, levels, lons = ens.shape
    scratch = [pltpu.VMEM(seen.shape, jnp.float32)]
    scratch += [pltpu.VMEM((rows, lons // SCATTER_LONS, levels, SCATTER_LONS), jnp.float32)] * slots
    kinds = [like((rows, levels, lons)), like((1, 1))]
    body = functools.partial(scatter_kernel, norm_scale)
    return call(body, kinds, scratch, 10**9, seen, want, keep, *at, ens, scalars=bounds)


def gradient(sides, own, circ, weights, obs_cost, devices):
    kinds = [like(own.shape), like((devices, 128))]
    body = functools.partial(grad_kernel, len(sides))
    return call(body, kinds, [], 10**9, *sides, own, *circ, weights, obs_cost)


def local(ensemble, weights, obs_cell, innovation, obs_weight, quality):
    _, rows, levels, lons = weights.shape
    members, bands = lax.axis_size("mem"), lax.axis_size("lat")
    norm_scale = 1.0 / math.sqrt(members - 1)
    ens, own = ensemble[0], weights[0]
    circ = [jnp.asarray(part) for part in circulant_parts(lons)]
    sides = edges(own)
    pos, pick_at, scatter_at, bounds = sort_cells(obs_cell, own.shape)
    keep, want = arrange(pos, innovation, obs_weight, quality)
    picked = pick(sides, own, circ, ens, pick_at, bounds)
    seen = summed(picked, "mem")
    back, obs_cost = scatter(seen, want, keep, ens, scatter_at, bounds, norm_scale)
    grad, sums = gradient(edges(back), back, circ, own, obs_cost, members * bands)
    sums = lax.all_to_all(sums, ("mem", "lat"), 0, 0, tiled=True)
    body = functools.partial(update_kernel, members, float(members * bands * rows * levels * lons))
    new_weights, cost = call(body, [like(own.shape), like((1, 1))], [], 10**8, sums, own, grad)
    return new_weights[None], cost[0, 0]


def solution(mesh):
    placed = (
        P("mem", None, "lat", None, None),
        P("mem", "lat", None, None),
        P(None, "lat"),
        P(None, "lat"),
        P(None, "lat"),
        P(None, "lat"),
    )
    return jax.shard_map(
        local,
        mesh=mesh,
        in_specs=placed,
        out_specs=(P("mem", "lat", None, None), P()),
        check_vma=False,
    )
```

```python
import functools
import math

import jax
import jax.numpy as jnp
import numpy as np
from jax import lax
from jax.experimental import pallas as pl
from jax.experimental.pallas import tpu as pltpu
from jax.sharding import PartitionSpec as P

HALF = 8
STEP_LENGTH = 0.5
EPSILON = 1e-06
LANES = 256
PIECE = 128
PICK_LONS = 256
SCATTER_LONS = 128
GROUP = 1024
BIN = 2
WINDOW = 2 * BIN
PICK_UNROLL = 16
SCATTER_UNROLL = 16
GROUPS = 2
COST = 10**9
MIB = 1024 * 1024


def taps():
    sigma = HALF / 2.0
    every = np.arange(-HALF, HALF + 1).astype(np.float64)
    normal = np.sqrt(np.sum(np.exp(-((every / sigma) ** 2))))
    return np.exp(-0.5 * (every / sigma) ** 2) / normal


def circulant_parts(lon_count):
    full = np.zeros((lon_count, lon_count), np.float32)
    at = np.arange(lon_count)
    for shift_by, tap in zip(range(-HALF, HALF + 1), taps()):
        full[at, (at + shift_by) % lon_count] += np.float32(tap)
    high = full.astype(jnp.bfloat16)
    low = (full - high.astype(np.float32)).astype(jnp.bfloat16)
    return high, low


def two_parts(value):
    high = value.astype(jnp.bfloat16)
    low = (value - high.astype(jnp.float32)).astype(jnp.bfloat16)
    return high, low


def smooth_rows(low, own, high):
    tap = [float(t) for t in taps()]
    padded = jnp.concatenate([low, own, high], axis=0)
    rows = own.shape[0]
    total = padded[HALF : HALF + rows] * tap[HALF]
    for away in range(1, HALF + 1):
        pair = padded[HALF - away : HALF - away + rows] + padded[HALF + away : HALF + away + rows]
        total = total + pair * tap[HALF + away]
    return total


def smooth_lons(field, circ_high, circ_low):
    first, second = two_parts(field)
    dot = functools.partial(jnp.dot, preferred_element_type=jnp.float32)
    return dot(first, circ_high) + (dot(second, circ_high) + dot(first, circ_low))


def quotient(value, by):
    if by & (by - 1):
        return lax.div(value, by), lax.rem(value, by)
    return lax.shift_right_logical(value, by.bit_length() - 1), lax.bitwise_and(value, by - 1)


def small_ids(shape):
    return lax.broadcasted_iota(jnp.int32, shape, 0).astype(jnp.bfloat16)


def one_hot(ids, at):
    return jnp.where(ids == at, jnp.bfloat16(1), jnp.bfloat16(0))


def ids_of(shape, dim):
    return lax.broadcasted_iota(jnp.int32, shape, dim)


def across(left, right):
    return lax.dot_general(left, right, (((1,), (1,)), ((), ())), preferred_element_type=jnp.float32)


def permute(pos, values, pieces):
    hi_ids, lo_ids = small_ids((pieces, GROUP)), small_ids((PIECE, GROUP))
    hi, lo = (part.astype(jnp.float32).astype(jnp.bfloat16) for part in quotient(pos, PIECE))
    total = jnp.zeros((len(values) * pieces, PIECE), jnp.float32)
    for at in range(0, pos.shape[1], GROUP):
        here = slice(at, at + GROUP)
        chosen = hi_ids == hi[:, here]
        left = jnp.concatenate([jnp.where(chosen, v[:, here], jnp.bfloat16(0)) for v in values], axis=0)
        total += across(left, one_hot(lo_ids, lo[:, here]))
    return [total[k * pieces : (k + 1) * pieces] for k in range(len(values))]


def sort_kernel(shape, groups, cell_ref, pos_ref, *refs):
    *refs, prefix_ref = refs
    rows, levels, lons = shape
    _, obs = cell_ref.shape
    tiles, pieces = obs // LANES, obs // PIECE
    bins = rows // BIN
    bin_ids = small_ids((bins, LANES))
    square = (LANES, LANES)
    upper = (ids_of(square, 0) <= ids_of(square, 1)).astype(jnp.bfloat16)
    counting = jnp.concatenate([upper, jnp.ones((LANES, 128), jnp.bfloat16)], axis=1)
    before = (ids_of((bins, bins), 1) < ids_of((bins, bins), 0)).astype(jnp.float32)
    wide = lambda v: jnp.concatenate([v] * (LANES // 128), axis=1)
    _, cells = quotient(cell_ref[...], rows * levels * lons)
    keys, lons_of = quotient(cells, lons)
    bins_of, _ = quotient(keys, levels * BIN)
    middle = lons // 2
    signed = jnp.where(lons_of < middle, lons_of, middle - 1 - lons_of)
    keys, bins_of, signed = (v.astype(jnp.float32).astype(jnp.bfloat16) for v in (keys, bins_of, signed))
    outs = len(refs) // len(groups)
    for slot, (group, mine) in enumerate([(g, m) for m, g in enumerate(groups) for _ in g]):
        *place_refs, first_ref, last_ref, far_ref = refs[mine * outs : (mine + 1) * outs]
        turn = slot - group[0]
        in_bin = bins_of[slot : slot + 1]
        hots = [one_hot(bin_ids, in_bin[:, at * LANES : (at + 1) * LANES]) for at in range(tiles)]
        prefix_ref[...] = jnp.dot(jnp.concatenate(hots, axis=0), counting, preferred_element_type=jnp.float32)
        total = jnp.zeros((bins, 128), jnp.float32)
        for at in range(tiles):
            total += prefix_ref[pl.ds(at * bins, bins), pl.ds(LANES, 128)]
        carry = jnp.dot(before, total, precision=lax.Precision.HIGHEST, preferred_element_type=jnp.float32) - 1.0
        places = []
        for at in range(tiles):
            here = pl.ds(at * bins, bins)
            place = (prefix_ref[here, pl.ds(0, LANES)] + wide(carry)) * hots[at].astype(jnp.float32)
            places.append(jnp.sum(place, axis=0, keepdims=True))
            carry += prefix_ref[here, pl.ds(LANES, 128)]
        pos = jnp.concatenate(places, axis=1).astype(jnp.int32)
        pos_ref[pl.ds(slot, 1), :] = pos
        key, lane = permute(pos, [keys[slot : slot + 1], signed[slot : slot + 1]], pieces)
        key, lane = key.astype(jnp.int32), lane.astype(jnp.int32)
        row, level = quotient(key, levels)
        lon = jnp.where(lane < 0, middle - 1 - lane, lane)
        here = pl.ds(turn * pieces, pieces)
        for near, place_ref, lane_ref in zip((PICK_LONS, SCATTER_LONS), place_refs[::2], place_refs[1::2]):
            part, lane = quotient(lon, near)
            place_ref[here, :] = (row * (lons // near) + part) * levels + level
            lane_ref[here, :] = lane.astype(jnp.float32)
        begin_row = quotient(row, BIN)[0] * BIN
        first = jnp.minimum(begin_row[:, :1], rows - WINDOW)
        last = begin_row[:, PIECE - 1 :] + BIN - 1
        begin = jnp.concatenate([first[:1], first[:-1]], axis=0)
        ends_tile = quotient(ids_of((pieces, 1), 0), LANES // PIECE)[1] == LANES // PIECE - 1
        far = jnp.max(jnp.where(ends_tile, last - begin, 0), axis=0, keepdims=True)
        as_row = lambda v: jnp.broadcast_to(v.astype(jnp.float32), (pieces, 128)).T[:1].astype(jnp.int32)
        first_ref[pl.ds(turn, 1), :] = as_row(first)
        last_ref[pl.ds(turn, 1), :] = as_row(last)
        far_ref[pl.ds(turn, 1), :] = far


def arrange_kernel(group, pos_ref, innov_ref, weight_ref, quality_ref, keep_ref, want_ref):
    pieces = pos_ref.shape[1] // PIECE
    mine = slice(group[0], group[-1] + 1)
    keeps = two_parts(quality_ref[mine, :].astype(jnp.float32) * weight_ref[mine, :])
    wants = two_parts(innov_ref[mine, :])
    for turn, slot in enumerate(group):
        at = slice(turn, turn + 1)
        moved = permute(pos_ref[slot : slot + 1, :], [part[at] for part in keeps + wants], pieces)
        here = pl.ds(turn * pieces, pieces)
        keep_ref[here, :] = moved[0] + moved[1]
        want_ref[here, :] = moved[2] + moved[3]


def tile_row(ref, at):
    parts = LANES // PIECE
    return jnp.concatenate([ref[pl.ds(at * parts + k, 1), :] for k in range(parts)], axis=1)


def window_places(place_ref, at, start, low_row, per_row):
    place = tile_row(place_ref, at) - start * per_row
    if low_row is None:
        return place
    return jnp.where(place < (low_row - start) * per_row, -1, place)


def over_windows(tiles, slots, rows, first_ref, last_ref, far_ref, unroll, step):
    @pl.loop(0, tiles, unroll=unroll)
    def _(tile):
        for slot in range(slots):
            step(slot, tile, first_ref[slot, tile * (LANES // PIECE)], None)

    for slot in range(slots):

        @pl.when(far_ref[slot, 0] >= WINDOW)
        def _():
            @pl.loop(0, tiles)
            def _(tile):
                begin = first_ref[slot, tile * (LANES // PIECE)]

                @pl.loop(1, lax.div(last_ref[slot, (tile + 1) * (LANES // PIECE) - 1] - begin, WINDOW) + 1)
                def _(turn):
                    low_row = begin + turn * WINDOW
                    step(slot, tile, jnp.minimum(low_row, rows - WINDOW), low_row)


def pick_kernel(group, sides, own_ref, circ_high_ref, circ_low_ref, *refs):
    if sides:
        low, high = halo(refs[:sides])
        refs = refs[sides:]
    ens_ref, place_ref, lane_ref, first_ref, last_ref, far_ref, out_ref, *part_refs = refs
    rows, levels, lons = own_ref.shape
    slots = len(group)
    tiles = first_ref.shape[1] // (LANES // PIECE)
    local_ref = own_ref
    if sides:
        local_ref, *part_refs = part_refs
        mixed = smooth_rows(low, own_ref[...], high).reshape(rows * levels, lons)
        local_ref[...] = smooth_lons(mixed, circ_high_ref[...], circ_low_ref[...]).reshape(local_ref.shape)
    for slot in range(slots):
        field = ens_ref[group[slot]].astype(jnp.float32) * local_ref[...]
        first = field.astype(jnp.bfloat16).astype(jnp.float32)
        part_refs[slot][...] = jnp.concatenate([first, field - first], axis=1).astype(jnp.bfloat16)
    parts = lons // PICK_LONS
    size = WINDOW * parts * levels
    place_ids = ids_of((size, LANES), 0)
    lane_ids = small_ids((PICK_LONS, LANES))

    def step(slot, tile, start, low_row):
        at = slot * tiles + tile
        place = window_places(place_ref, at, start, low_row, parts * levels)
        part = part_refs[slot][pl.ds(start, WINDOW)]
        left = jnp.stack([part[:, :, k * PICK_LONS : (k + 1) * PICK_LONS] for k in range(parts)], axis=1).reshape(2 * size, PICK_LONS)
        hot = one_hot(lane_ids, tile_row(lane_ref, at).astype(jnp.bfloat16))
        both = jnp.dot(left, hot, preferred_element_type=jnp.float32).reshape(WINDOW * parts, 2, levels, LANES)
        value = (both[:, 0] + both[:, 1]).reshape(size, LANES)
        value = jnp.sum(jnp.where(place_ids == place, value, 0.0), axis=0, keepdims=True)
        for k in range(LANES // PIECE):
            here, part = pl.ds(at * (LANES // PIECE) + k, 1), value[:, k * PIECE : (k + 1) * PIECE]
            out_ref[here, :] = part if low_row is None else out_ref[here, :] + part

    over_windows(tiles, slots, rows, first_ref, last_ref, far_ref, PICK_UNROLL, step)


def scatter_kernel(group, norm_scale, earlier, seen_ref, want_ref, keep_ref, place_ref, lane_ref, ens_ref, *refs):
    before_refs, refs = refs[:earlier], refs[earlier:]
    first_ref, last_ref, far_ref, back_ref, cost_ref, wres_ref, *grad_refs = refs
    slots = len(group)
    _, rows, levels, lons = ens_ref.shape
    tiles = first_ref.shape[1] // (LANES // PIECE)
    resid = seen_ref[...] * norm_scale - want_ref[...]
    wres_ref[...] = keep_ref[...] * resid
    cost = jnp.sum(wres_ref[...] * resid).reshape(1, 1)
    cost_ref[...] = cost + before_refs[1][...] if earlier else cost
    parts = lons // SCATTER_LONS
    size = WINDOW * parts * levels
    place_ids = small_ids((size, LANES))
    lane_ids = small_ids((SCATTER_LONS, LANES))
    for slot in range(slots):
        grad_refs[slot][...] = jnp.zeros(grad_refs[slot].shape, jnp.float32)

    def step(slot, tile, start, low_row):
        at = slot * tiles + tile
        place = window_places(place_ref, at, start, low_row, parts * levels)
        chosen = place_ids == place.astype(jnp.float32).astype(jnp.bfloat16)
        left = [jnp.where(chosen, part, jnp.bfloat16(0)) for part in two_parts(tile_row(wres_ref, at))]
        left = jnp.concatenate(left, axis=0)
        hot = one_hot(lane_ids, tile_row(lane_ref, at).astype(jnp.bfloat16))
        both = across(left, hot)
        grad_refs[slot][pl.ds(start, WINDOW)] += (both[:size] + both[size:]).reshape(WINDOW, parts, levels, SCATTER_LONS)

    over_windows(tiles, slots, rows, first_ref, last_ref, far_ref, SCATTER_UNROLL, step)
    total = jnp.zeros((rows, levels, lons), jnp.float32)
    for slot in range(slots):
        grad = jnp.concatenate([grad_refs[slot][:, k] for k in range(parts)], axis=2)
        total += ens_ref[group[slot]].astype(jnp.float32) * grad
    total = total * norm_scale
    back_ref[...] = total + before_refs[0][...] if earlier else total


def grad_kernel(sides, *refs):
    low, high = halo(refs[:sides])
    own_ref, circ_high_ref, circ_low_ref, weights_ref, obs_cost_ref, grad_ref, sums_ref = refs[sides:]
    rows, levels, lons = own_ref.shape
    mixed = smooth_rows(low, own_ref[...], high).reshape(rows * levels, lons)
    weights = weights_ref[...].reshape(rows * levels, lons)
    grad = weights + smooth_lons(mixed, circ_high_ref[...], circ_low_ref[...])
    grad_ref[...] = grad.reshape(grad_ref.shape)
    lane = lax.broadcasted_iota(jnp.int32, sums_ref.shape, 1)
    prior = jnp.sum(weights * weights)
    square = jnp.sum(grad * grad)
    sums_ref[...] = jnp.where(lane == 0, square, jnp.where(lane == 1, prior, jnp.where(lane == 2, obs_cost_ref[...], 0.0)))


def update_kernel(members, entries, sums_ref, own_ref, grad_ref, new_ref, cost_ref):
    totals = jnp.sum(sums_ref[...], axis=0, keepdims=True)
    length = jnp.sqrt(totals[:, :1] / entries + EPSILON)
    new_ref[...] = own_ref[...] - grad_ref[...] * (STEP_LENGTH / length)[None]
    cost_ref[...] = (0.5 * totals[:, 1:2] + 0.5 * totals[:, 2:3] / members) / entries


def call(body, out_shape, scratch, flops, *operands, scalars=()):
    vmem, smem = pl.BlockSpec(memory_space=pltpu.VMEM), pl.BlockSpec(memory_space=pltpu.SMEM)
    return pl.pallas_call(
        body,
        out_shape=out_shape,
        in_specs=[vmem] * len(operands) + [smem] * len(scalars),
        out_specs=jax.tree.map(lambda _: vmem, out_shape),
        scratch_shapes=scratch,
        compiler_params=pltpu.CompilerParams(vmem_limit_bytes=48 * MIB),
        cost_estimate=pl.CostEstimate(flops=flops, bytes_accessed=2 * MIB, transcendentals=0),
    )(*operands, *scalars)


def edges(field):
    count = lax.axis_size("lat")
    if count == 2:
        rows = field.shape[0]
        start = (rows - HALF) * (1 - lax.axis_index("lat"))
        edge = lax.dynamic_slice_in_dim(field, start, HALF, 0)
        return [lax.ppermute(edge, "lat", [(0, 1), (1, 0)])]
    forward = [(i, i + 1) for i in range(count - 1)]
    backward = [(target, source) for source, target in forward]
    low = lax.ppermute(field[-HALF:], "lat", forward)
    high = lax.ppermute(field[:HALF], "lat", backward)
    return [low, high]


def halo(refs):
    if len(refs) == 2:
        return refs[0][...], refs[1][...]
    last = lax.axis_index("lat") == 1
    return jnp.where(last, refs[0][...], 0.0), jnp.where(last, 0.0, refs[0][...])


def summed(value, axis, turn=0):
    count = lax.axis_size(axis)
    if count & (count - 1):
        return lax.psum(value, axis)
    aways = [1 << k for k in range(count.bit_length() - 1)]
    for away in aways[turn:] + aways[:turn]:
        value = value + lax.ppermute(value, axis, [(i, i ^ away) for i in range(count)])
    return value


def like(shape, kind=jnp.float32):
    return jax.ShapeDtypeStruct(shape, kind)


def sort_cells(obs_cell, shape, groups):
    slots, obs = obs_cell.shape
    kinds = [like((slots, obs), jnp.int32)]
    for group in groups:
        ordered, bound = (len(group) * obs // PIECE, PIECE), (len(group), obs // PIECE)
        kinds += [like(ordered, jnp.int32), like(ordered)] * 2
        kinds += [like(bound, jnp.int32), like(bound, jnp.int32), like((len(group), 1), jnp.int32)]
    scratch = [pltpu.VMEM((obs // LANES * shape[0] // BIN, LANES + 128), jnp.float32)]
    pos, *outs = call(functools.partial(sort_kernel, shape, groups), kinds, scratch, COST, obs_cell)
    outs = [outs[k : k + 7] for k in range(0, len(outs), 7)]
    return pos, [(out[:2], out[2:4], out[4:]) for out in outs]


def arrange(pos, innovation, obs_weight, quality, group):
    ordered = like((len(group) * pos.shape[1] // PIECE, PIECE))
    body = functools.partial(arrange_kernel, group)
    return call(body, [ordered, ordered], [], COST, pos, innovation, obs_weight, quality)


def pick(sides, own, circ, ens, at, bounds, group):
    rows, levels, lons = own.shape
    kinds = [like(at[0].shape)] + [like(own.shape)] * (len(sides) > 0)
    scratch = [pltpu.VMEM((rows, 2 * levels, lons), jnp.bfloat16)] * len(group)
    body = functools.partial(pick_kernel, group, len(sides))
    return call(body, kinds, scratch, COST, own, *circ, *sides, ens, *at, scalars=bounds)


def scatter(seen, want, keep, ens, at, bounds, norm_scale, group, earlier):
    _, rows, levels, lons = ens.shape
    scratch = [pltpu.VMEM(seen.shape, jnp.float32)]
    scratch += [pltpu.VMEM((rows, lons // SCATTER_LONS, levels, SCATTER_LONS), jnp.float32)] * len(group)
    kinds = [like((rows, levels, lons)), like((1, 1))]
    body = functools.partial(scatter_kernel, group, norm_scale, len(earlier))
    return call(body, kinds, scratch, COST, seen, want, keep, *at, ens, *earlier, scalars=bounds)


def gradient(sides, own, circ, weights, obs_cost, devices):
    kinds = [like(own.shape), like((devices, 128))]
    body = functools.partial(grad_kernel, len(sides))
    return call(body, kinds, [], COST, *sides, own, *circ, weights, obs_cost)


def local(ensemble, weights, obs_cell, innovation, obs_weight, quality):
    _, rows, levels, lons = weights.shape
    members, bands = lax.axis_size("mem"), lax.axis_size("lat")
    norm_scale = 1.0 / math.sqrt(members - 1)
    ens, own = ensemble[0], weights[0]
    circ = [jnp.asarray(part) for part in circulant_parts(lons)]
    slots = obs_cell.shape[0]
    size = slots // GROUPS
    groups = [range(k, k + size) for k in range(0, slots, size)]
    sides = edges(own)
    pos, ordered = sort_cells(obs_cell, own.shape, groups)
    arranged = [arrange(pos, innovation, obs_weight, quality, group) for group in groups]
    local_weights, seen = None, []
    for turn, (group, (pick_at, _, bounds)) in enumerate(zip(groups, ordered)):
        if turn == 0:
            picked, local_weights = pick(sides, own, circ, ens, pick_at, bounds, group)
        else:
            (picked,) = pick([], local_weights, circ, ens, pick_at, bounds, group)
        seen.append(summed(picked, "mem", 2 * turn))
    sofar = []
    for group, total, (keep, want), (_, scatter_at, bounds) in zip(groups, seen, arranged, ordered):
        sofar = scatter(total, want, keep, ens, scatter_at, bounds, norm_scale, group, sofar)
    back, obs_cost = sofar
    grad, sums = gradient(edges(back), back, circ, own, obs_cost, members * bands)
    sums = lax.all_to_all(sums, ("mem", "lat"), 0, 0, tiled=True)
    body = functools.partial(update_kernel, members, float(members * bands * rows * levels * lons))
    new_weights, cost = call(body, [like(own.shape), like((1, 1))], [], 10**8, sums, own, grad)
    return new_weights[None], cost[0, 0]


def solution(mesh):
    placed = (
        P("mem", None, "lat", None, None),
        P("mem", "lat", None, None),
        P(None, "lat"),
        P(None, "lat"),
        P(None, "lat"),
        P(None, "lat"),
    )
    return jax.shard_map(
        local,
        mesh=mesh,
        in_specs=placed,
        out_specs=(P("mem", "lat", None, None), P()),
        check_vma=False,
    )
```

```python
import functools
import math

import jax
import jax.numpy as jnp
import numpy as np
from jax import lax
from jax.experimental import pallas as pl
from jax.experimental.pallas import tpu as pltpu
from jax.sharding import PartitionSpec as P

HALF = 8
STEP_LENGTH = 0.5
EPSILON = 1e-06
LANES = 256
PIECE = 128
PICK_LONS = 256
SCATTER_LONS = 128
GROUP = 1024
BIN = 2
WINDOW = 2 * BIN
PICK_UNROLL = 16
SCATTER_UNROLL = 16
GROUPS = 2
COST = 10**9
MIB = 1024 * 1024


def taps():
    sigma = HALF / 2.0
    every = np.arange(-HALF, HALF + 1).astype(np.float64)
    normal = np.sqrt(np.sum(np.exp(-((every / sigma) ** 2))))
    return np.exp(-0.5 * (every / sigma) ** 2) / normal


def circulant_parts(lon_count):
    full = np.zeros((lon_count, lon_count), np.float32)
    at = np.arange(lon_count)
    for shift_by, tap in zip(range(-HALF, HALF + 1), taps()):
        full[at, (at + shift_by) % lon_count] += np.float32(tap)
    high = full.astype(jnp.bfloat16)
    low = (full - high.astype(np.float32)).astype(jnp.bfloat16)
    return high, low


def two_parts(value):
    high = value.astype(jnp.bfloat16)
    low = (value - high.astype(jnp.float32)).astype(jnp.bfloat16)
    return high, low


def smooth_rows(low, own, high):
    tap = [float(t) for t in taps()]
    padded = jnp.concatenate([low, own, high], axis=0)
    rows = own.shape[0]
    total = padded[HALF : HALF + rows] * tap[HALF]
    for away in range(1, HALF + 1):
        pair = padded[HALF - away : HALF - away + rows] + padded[HALF + away : HALF + away + rows]
        total = total + pair * tap[HALF + away]
    return total


def smooth_lons(field, circ_high, circ_low):
    first, second = two_parts(field)
    dot = functools.partial(jnp.dot, preferred_element_type=jnp.float32)
    return dot(first, circ_high) + (dot(second, circ_high) + dot(first, circ_low))


def quotient(value, by):
    if by & (by - 1):
        return lax.div(value, by), lax.rem(value, by)
    return lax.shift_right_logical(value, by.bit_length() - 1), lax.bitwise_and(value, by - 1)


def small_ids(shape):
    return lax.broadcasted_iota(jnp.int32, shape, 0).astype(jnp.bfloat16)


def one_hot(ids, at):
    return jnp.where(ids == at, jnp.bfloat16(1), jnp.bfloat16(0))


def ids_of(shape, dim):
    return lax.broadcasted_iota(jnp.int32, shape, dim)


def across(left, right):
    return lax.dot_general(left, right, (((1,), (1,)), ((), ())), preferred_element_type=jnp.float32)


def permute(pos, values, pieces):
    hi_ids, lo_ids = small_ids((pieces, GROUP)), small_ids((PIECE, GROUP))
    hi, lo = (part.astype(jnp.float32).astype(jnp.bfloat16) for part in quotient(pos, PIECE))
    total = jnp.zeros((len(values) * pieces, PIECE), jnp.float32)
    for at in range(0, pos.shape[1], GROUP):
        here = slice(at, at + GROUP)
        chosen = hi_ids == hi[:, here]
        left = jnp.concatenate([jnp.where(chosen, v[:, here], jnp.bfloat16(0)) for v in values], axis=0)
        total += across(left, one_hot(lo_ids, lo[:, here]))
    return [total[k * pieces : (k + 1) * pieces] for k in range(len(values))]


def sort_kernel(shape, groups, cell_ref, pos_ref, *refs):
    *refs, prefix_ref = refs
    rows, levels, lons = shape
    _, obs = cell_ref.shape
    tiles, pieces = obs // LANES, obs // PIECE
    bins = rows // BIN
    bin_ids = small_ids((bins, LANES))
    square = (LANES, LANES)
    upper = (ids_of(square, 0) <= ids_of(square, 1)).astype(jnp.bfloat16)
    counting = jnp.concatenate([upper, jnp.ones((LANES, 128), jnp.bfloat16)], axis=1)
    before = (ids_of((bins, bins), 1) < ids_of((bins, bins), 0)).astype(jnp.float32)
    wide = lambda v: jnp.concatenate([v] * (LANES // 128), axis=1)
    _, cells = quotient(cell_ref[...], rows * levels * lons)
    keys, lons_of = quotient(cells, lons)
    bins_of, _ = quotient(keys, levels * BIN)
    middle = lons // 2
    signed = jnp.where(lons_of < middle, lons_of, middle - 1 - lons_of)
    keys, bins_of, signed = (v.astype(jnp.float32).astype(jnp.bfloat16) for v in (keys, bins_of, signed))
    outs = len(refs) // len(groups)
    for slot, (group, mine) in enumerate([(g, m) for m, g in enumerate(groups) for _ in g]):
        *place_refs, bounds_ref = refs[mine * outs : (mine + 1) * outs]
        turn = slot - group[0]
        in_bin = bins_of[slot : slot + 1]
        hots = [one_hot(bin_ids, in_bin[:, at * LANES : (at + 1) * LANES]) for at in range(tiles)]
        prefix_ref[...] = jnp.dot(jnp.concatenate(hots, axis=0), counting, preferred_element_type=jnp.float32)
        total = jnp.zeros((bins, 128), jnp.float32)
        for at in range(tiles):
            total += prefix_ref[pl.ds(at * bins, bins), pl.ds(LANES, 128)]
        carry = jnp.dot(before, total, precision=lax.Precision.HIGHEST, preferred_element_type=jnp.float32) - 1.0
        places = []
        for at in range(tiles):
            here = pl.ds(at * bins, bins)
            place = (prefix_ref[here, pl.ds(0, LANES)] + wide(carry)) * hots[at].astype(jnp.float32)
            places.append(jnp.sum(place, axis=0, keepdims=True))
            carry += prefix_ref[here, pl.ds(LANES, 128)]
        pos = jnp.concatenate(places, axis=1).astype(jnp.int32)
        pos_ref[pl.ds(slot, 1), :] = pos
        key, lane = permute(pos, [keys[slot : slot + 1], signed[slot : slot + 1]], pieces)
        key, lane = key.astype(jnp.int32), lane.astype(jnp.int32)
        row, level = quotient(key, levels)
        lon = jnp.where(lane < 0, middle - 1 - lane, lane)
        here = pl.ds(turn * pieces, pieces)
        for near, place_ref, lane_ref in zip((PICK_LONS, SCATTER_LONS), place_refs[::2], place_refs[1::2]):
            part, lane = quotient(lon, near)
            place_ref[here, :] = (row * (lons // near) + part) * levels + level
            lane_ref[here, :] = lane.astype(jnp.float32)
        begin_row = quotient(row, BIN)[0] * BIN
        first = jnp.minimum(begin_row[:, :1], rows - WINDOW)
        last = begin_row[:, PIECE - 1 :] + BIN - 1
        begin = jnp.concatenate([first[:1], first[:-1]], axis=0)
        ends_tile = quotient(ids_of((pieces, 1), 0), LANES // PIECE)[1] == LANES // PIECE - 1
        far = jnp.max(jnp.where(ends_tile, last - begin, 0), axis=0, keepdims=True)
        spread = [jnp.broadcast_to(v.astype(jnp.float32), (pieces, 128)).T[:1].astype(jnp.int32) for v in (first, last)]
        spread.append(jnp.broadcast_to(far, (1, pieces)))
        for kind, v in enumerate(spread):
            bounds_ref[pl.ds(kind * len(group) + turn, 1), pl.ds(0, pieces)] = v


def arrange_kernel(group, pos_ref, innov_ref, weight_ref, quality_ref, keep_ref, want_ref):
    pieces = pos_ref.shape[1] // PIECE
    mine = slice(group[0], group[-1] + 1)
    keeps = two_parts(quality_ref[mine, :].astype(jnp.float32) * weight_ref[mine, :])
    wants = two_parts(innov_ref[mine, :])
    for turn, slot in enumerate(group):
        at = slice(turn, turn + 1)
        moved = permute(pos_ref[slot : slot + 1, :], [part[at] for part in keeps + wants], pieces)
        here = pl.ds(turn * pieces, pieces)
        keep_ref[here, :] = moved[0] + moved[1]
        want_ref[here, :] = moved[2] + moved[3]


def tile_row(ref, at):
    parts = LANES // PIECE
    return jnp.concatenate([ref[pl.ds(at * parts + k, 1), :] for k in range(parts)], axis=1)


def window_places(place_ref, at, start, low_row, per_row):
    place = tile_row(place_ref, at) - start * per_row
    if low_row is None:
        return place
    return jnp.where(place < (low_row - start) * per_row, -1, place)


def over_windows(tiles, slots, rows, bounds_ref, unroll, step):
    parts = LANES // PIECE

    @pl.loop(0, tiles, unroll=unroll)
    def _(tile):
        for slot in range(slots):
            step(slot, tile, bounds_ref[slot, tile * parts], None)

    for slot in range(slots):

        @pl.when(bounds_ref[2 * slots + slot, 0] >= WINDOW)
        def _():
            @pl.loop(0, tiles)
            def _(tile):
                begin = bounds_ref[slot, tile * parts]
                end = bounds_ref[slots + slot, (tile + 1) * parts - 1]

                @pl.loop(1, lax.div(end - begin, WINDOW) + 1)
                def _(turn):
                    low_row = begin + turn * WINDOW
                    step(slot, tile, jnp.minimum(low_row, rows - WINDOW), low_row)


def pick_kernel(group, sides, own_ref, circ_high_ref, circ_low_ref, *refs):
    if sides:
        low, high = halo(refs[:sides])
        refs = refs[sides:]
    ens_ref, place_ref, lane_ref, bounds_in_ref, out_ref, *part_refs, bounds_ref, sem = refs
    bounds_copy = pltpu.make_async_copy(bounds_in_ref, bounds_ref, sem)
    bounds_copy.start()
    rows, levels, lons = own_ref.shape
    slots = len(group)
    tiles = place_ref.shape[0] * PIECE // (slots * LANES)
    local_ref = own_ref
    if sides:
        local_ref, *part_refs = part_refs
        mixed = smooth_rows(low, own_ref[...], high).reshape(rows * levels, lons)
        local_ref[...] = smooth_lons(mixed, circ_high_ref[...], circ_low_ref[...]).reshape(local_ref.shape)
    for slot in range(slots):
        field = ens_ref[group[slot]].astype(jnp.float32) * local_ref[...]
        first = field.astype(jnp.bfloat16).astype(jnp.float32)
        part_refs[slot][...] = jnp.concatenate([first, field - first], axis=1).astype(jnp.bfloat16)
    parts = lons // PICK_LONS
    size = WINDOW * parts * levels
    place_ids = ids_of((size, LANES), 0)
    lane_ids = small_ids((PICK_LONS, LANES))

    def step(slot, tile, start, low_row):
        at = slot * tiles + tile
        place = window_places(place_ref, at, start, low_row, parts * levels)
        part = part_refs[slot][pl.ds(start, WINDOW)]
        left = jnp.stack([part[:, :, k * PICK_LONS : (k + 1) * PICK_LONS] for k in range(parts)], axis=1).reshape(2 * size, PICK_LONS)
        hot = one_hot(lane_ids, tile_row(lane_ref, at).astype(jnp.bfloat16))
        both = jnp.dot(left, hot, preferred_element_type=jnp.float32).reshape(WINDOW * parts, 2, levels, LANES)
        value = (both[:, 0] + both[:, 1]).reshape(size, LANES)
        value = jnp.sum(jnp.where(place_ids == place, value, 0.0), axis=0, keepdims=True)
        for k in range(LANES // PIECE):
            here, part = pl.ds(at * (LANES // PIECE) + k, 1), value[:, k * PIECE : (k + 1) * PIECE]
            out_ref[here, :] = part if low_row is None else out_ref[here, :] + part

    bounds_copy.wait()
    over_windows(tiles, slots, rows, bounds_ref, PICK_UNROLL, step)


def scatter_kernel(group, norm_scale, earlier, seen_ref, want_ref, keep_ref, place_ref, lane_ref, ens_ref, *refs):
    before_refs, refs = refs[:earlier], refs[earlier:]
    bounds_in_ref, back_ref, cost_ref, wres_ref, *grad_refs, bounds_ref, sem = refs
    bounds_copy = pltpu.make_async_copy(bounds_in_ref, bounds_ref, sem)
    bounds_copy.start()
    slots = len(group)
    _, rows, levels, lons = ens_ref.shape
    tiles = place_ref.shape[0] * PIECE // (slots * LANES)
    resid = seen_ref[...] * norm_scale - want_ref[...]
    wres_ref[...] = keep_ref[...] * resid
    cost = jnp.sum((wres_ref[...] * resid).reshape(-1, *cost_ref.shape), axis=0)
    cost_ref[...] = cost + before_refs[1][...] if earlier else cost
    parts = lons // SCATTER_LONS
    size = WINDOW * parts * levels
    place_ids = small_ids((size, LANES))
    lane_ids = small_ids((SCATTER_LONS, LANES))
    for slot in range(slots):
        grad_refs[slot][...] = jnp.zeros(grad_refs[slot].shape, jnp.float32)

    def step(slot, tile, start, low_row):
        at = slot * tiles + tile
        place = window_places(place_ref, at, start, low_row, parts * levels)
        chosen = place_ids == place.astype(jnp.float32).astype(jnp.bfloat16)
        left = [jnp.where(chosen, part, jnp.bfloat16(0)) for part in two_parts(tile_row(wres_ref, at))]
        left = jnp.concatenate(left, axis=0)
        hot = one_hot(lane_ids, tile_row(lane_ref, at).astype(jnp.bfloat16))
        both = across(left, hot)
        grad_refs[slot][pl.ds(start, WINDOW)] += (both[:size] + both[size:]).reshape(WINDOW, parts, levels, SCATTER_LONS)

    bounds_copy.wait()
    over_windows(tiles, slots, rows, bounds_ref, SCATTER_UNROLL, step)
    total = jnp.zeros((rows, levels, lons), jnp.float32)
    for slot in range(slots):
        grad = jnp.concatenate([grad_refs[slot][:, k] for k in range(parts)], axis=2)
        total += ens_ref[group[slot]].astype(jnp.float32) * grad
    total = total * norm_scale
    back_ref[...] = total + before_refs[0][...] if earlier else total


def grad_kernel(sides, *refs):
    low, high = halo(refs[:sides])
    own_ref, circ_high_ref, circ_low_ref, weights_ref, obs_cost_ref, grad_ref, sums_ref = refs[sides:]
    rows, levels, lons = own_ref.shape
    mixed = smooth_rows(low, own_ref[...], high).reshape(rows * levels, lons)
    weights = weights_ref[...].reshape(rows * levels, lons)
    grad = weights + smooth_lons(mixed, circ_high_ref[...], circ_low_ref[...])
    grad_ref[...] = grad.reshape(grad_ref.shape)
    lane = lax.broadcasted_iota(jnp.int32, sums_ref.shape, 1)
    prior = jnp.sum(weights * weights)
    square = jnp.sum(grad * grad)
    obs_cost = jnp.sum(obs_cost_ref[...])
    sums_ref[...] = jnp.where(lane == 0, square, jnp.where(lane == 1, prior, jnp.where(lane == 2, obs_cost, 0.0)))


def update_kernel(members, entries, sums_ref, own_ref, grad_ref, new_ref, cost_ref):
    totals = jnp.sum(sums_ref[...], axis=0, keepdims=True)
    length = jnp.sqrt(totals[:, :1] / entries + EPSILON)
    new_ref[...] = own_ref[...] - grad_ref[...] * (STEP_LENGTH / length)[None]
    cost_ref[...] = (0.5 * totals[:, 1:2] + 0.5 * totals[:, 2:3] / members) / entries


def call(body, out_shape, scratch, flops, *operands):
    vmem = pl.BlockSpec(memory_space=pltpu.VMEM)
    return pl.pallas_call(
        body,
        out_shape=out_shape,
        in_specs=[vmem] * len(operands),
        out_specs=jax.tree.map(lambda _: vmem, out_shape),
        scratch_shapes=scratch,
        compiler_params=pltpu.CompilerParams(vmem_limit_bytes=48 * MIB),
        cost_estimate=pl.CostEstimate(flops=flops, bytes_accessed=2 * MIB, transcendentals=0),
    )(*operands)


def edges(field):
    count = lax.axis_size("lat")
    if count == 2:
        rows = field.shape[0]
        start = (rows - HALF) * (1 - lax.axis_index("lat"))
        edge = lax.dynamic_slice_in_dim(field, start, HALF, 0)
        return [lax.ppermute(edge, "lat", [(0, 1), (1, 0)])]
    forward = [(i, i + 1) for i in range(count - 1)]
    backward = [(target, source) for source, target in forward]
    low = lax.ppermute(field[-HALF:], "lat", forward)
    high = lax.ppermute(field[:HALF], "lat", backward)
    return [low, high]


def halo(refs):
    if len(refs) == 2:
        return refs[0][...], refs[1][...]
    last = lax.axis_index("lat") == 1
    return jnp.where(last, refs[0][...], 0.0), jnp.where(last, 0.0, refs[0][...])


def summed(value, axis, turn=0):
    count = lax.axis_size(axis)
    if count & (count - 1):
        return lax.psum(value, axis)
    aways = [1 << k for k in range(count.bit_length() - 1)]
    for away in aways[turn:] + aways[:turn]:
        value = value + lax.ppermute(value, axis, [(i, i ^ away) for i in range(count)])
    return value


def like(shape, kind=jnp.float32):
    return jax.ShapeDtypeStruct(shape, kind)


def sort_cells(obs_cell, shape, groups):
    slots, obs = obs_cell.shape
    kinds = [like((slots, obs), jnp.int32)]
    for group in groups:
        ordered = (len(group) * obs // PIECE, PIECE)
        kinds += [like(ordered, jnp.int32), like(ordered)] * 2
        kinds += [like((-(-3 * len(group) // 8) * 8, -(-(obs // PIECE) // 128) * 128), jnp.int32)]
    scratch = [pltpu.VMEM((obs // LANES * shape[0] // BIN, LANES + 128), jnp.float32)]
    pos, *outs = call(functools.partial(sort_kernel, shape, groups), kinds, scratch, COST, obs_cell)
    outs = [outs[k : k + 5] for k in range(0, len(outs), 5)]
    return pos, [(out[:2], out[2:4], out[4]) for out in outs]


def arrange(pos, innovation, obs_weight, quality, group):
    ordered = like((len(group) * pos.shape[1] // PIECE, PIECE))
    body = functools.partial(arrange_kernel, group)
    return call(body, [ordered, ordered], [], COST, pos, innovation, obs_weight, quality)


def pick(sides, own, circ, ens, at, bounds, group):
    rows, levels, lons = own.shape
    kinds = [like(at[0].shape)] + [like(own.shape)] * (len(sides) > 0)
    scratch = [pltpu.VMEM((rows, 2 * levels, lons), jnp.bfloat16)] * len(group)
    scratch += [pltpu.SMEM(bounds.shape, jnp.int32), pltpu.SemaphoreType.DMA]
    body = functools.partial(pick_kernel, group, len(sides))
    return call(body, kinds, scratch, COST, own, *circ, *sides, ens, *at, bounds)


def scatter(seen, want, keep, ens, at, bounds, norm_scale, group, earlier):
    _, rows, levels, lons = ens.shape
    scratch = [pltpu.VMEM(seen.shape, jnp.float32)]
    scratch += [pltpu.VMEM((rows, lons // SCATTER_LONS, levels, SCATTER_LONS), jnp.float32)] * len(group)
    kinds = [like((rows, levels, lons)), like((8, 128))]
    scratch += [pltpu.SMEM(bounds.shape, jnp.int32), pltpu.SemaphoreType.DMA]
    body = functools.partial(scatter_kernel, group, norm_scale, len(earlier))
    return call(body, kinds, scratch, COST, seen, want, keep, *at, ens, *earlier, bounds)


def gradient(sides, own, circ, weights, obs_cost, devices):
    kinds = [like(own.shape), like((devices, 128))]
    body = functools.partial(grad_kernel, len(sides))
    return call(body, kinds, [], COST, *sides, own, *circ, weights, obs_cost)


def local(ensemble, weights, obs_cell, innovation, obs_weight, quality):
    _, rows, levels, lons = weights.shape
    members, bands = lax.axis_size("mem"), lax.axis_size("lat")
    norm_scale = 1.0 / math.sqrt(members - 1)
    ens, own = ensemble[0], weights[0]
    circ = [jnp.asarray(part) for part in circulant_parts(lons)]
    slots = obs_cell.shape[0]
    size = slots // GROUPS
    groups = [range(k, k + size) for k in range(0, slots, size)]
    sides = edges(own)
    pos, ordered = sort_cells(obs_cell, own.shape, groups)
    arranged = [arrange(pos, innovation, obs_weight, quality, group) for group in groups]
    local_weights, seen = None, []
    for turn, (group, (pick_at, _, bounds)) in enumerate(zip(groups, ordered)):
        if turn == 0:
            picked, local_weights = pick(sides, own, circ, ens, pick_at, bounds, group)
        else:
            (picked,) = pick([], local_weights, circ, ens, pick_at, bounds, group)
        seen.append(summed(picked, "mem", 2 * turn))
    sofar = []
    for group, total, (keep, want), (_, scatter_at, bounds) in zip(groups, seen, arranged, ordered):
        sofar = scatter(total, want, keep, ens, scatter_at, bounds, norm_scale, group, sofar)
    back, obs_cost = sofar
    grad, sums = gradient(edges(back), back, circ, own, obs_cost, members * bands)
    sums = lax.all_to_all(sums, ("mem", "lat"), 0, 0, tiled=True)
    body = functools.partial(update_kernel, members, float(members * bands * rows * levels * lons))
    new_weights, cost = call(body, [like(own.shape), like((1, 1))], [], 10**8, sums, own, grad)
    return new_weights[None], cost[0, 0]


def solution(mesh):
    placed = (
        P("mem", None, "lat", None, None),
        P("mem", "lat", None, None),
        P(None, "lat"),
        P(None, "lat"),
        P(None, "lat"),
        P(None, "lat"),
    )
    return jax.shard_map(
        local,
        mesh=mesh,
        in_specs=placed,
        out_specs=(P("mem", "lat", None, None), P()),
        check_vma=False,
    )
```

```python
import functools
import math

import jax
import jax.numpy as jnp
import numpy as np
from jax import lax
from jax.experimental import pallas as pl
from jax.experimental.pallas import tpu as pltpu
from jax.sharding import PartitionSpec as P

HALF = 8
STEP_LENGTH = 0.5
EPSILON = 1e-06
LANES = 256
PIECE = 128
PICK_LONS = 256
SCATTER_LONS = 128
GROUP = 1024
BIN = 2
WINDOW = 2 * BIN
GROUPS = 2
COST = 10**9
MIB = 1024 * 1024


def taps():
    sigma = HALF / 2.0
    every = np.arange(-HALF, HALF + 1).astype(np.float64)
    normal = np.sqrt(np.sum(np.exp(-((every / sigma) ** 2))))
    return np.exp(-0.5 * (every / sigma) ** 2) / normal


def circulant_parts(lon_count):
    full = np.zeros((lon_count, lon_count), np.float32)
    at = np.arange(lon_count)
    for shift_by, tap in zip(range(-HALF, HALF + 1), taps()):
        full[at, (at + shift_by) % lon_count] += np.float32(tap)
    high = full.astype(jnp.bfloat16)
    low = (full - high.astype(np.float32)).astype(jnp.bfloat16)
    return high, low


def two_parts(value):
    high = value.astype(jnp.bfloat16)
    low = (value - high.astype(jnp.float32)).astype(jnp.bfloat16)
    return high, low


def smooth_rows(low, own, high):
    tap = [float(t) for t in taps()]
    padded = jnp.concatenate([low, own, high], axis=0)
    rows = own.shape[0]
    total = padded[HALF : HALF + rows] * tap[HALF]
    for away in range(1, HALF + 1):
        pair = padded[HALF - away : HALF - away + rows] + padded[HALF + away : HALF + away + rows]
        total = total + pair * tap[HALF + away]
    return total


def smooth_lons(field, circ_high, circ_low):
    first, second = two_parts(field)
    dot = functools.partial(jnp.dot, preferred_element_type=jnp.float32)
    return dot(first, circ_high) + (dot(second, circ_high) + dot(first, circ_low))


def quotient(value, by):
    if by & (by - 1):
        return lax.div(value, by), lax.rem(value, by)
    return lax.shift_right_logical(value, by.bit_length() - 1), lax.bitwise_and(value, by - 1)


def small_ids(shape):
    return lax.broadcasted_iota(jnp.int32, shape, 0).astype(jnp.bfloat16)


def one_hot(ids, at):
    return jnp.where(ids == at, jnp.bfloat16(1), jnp.bfloat16(0))


def ids_of(shape, dim):
    return lax.broadcasted_iota(jnp.int32, shape, dim)


def across(left, right):
    return lax.dot_general(left, right, (((1,), (1,)), ((), ())), preferred_element_type=jnp.float32)


def permute(pos, values, pieces):
    hi_ids, lo_ids = small_ids((pieces, GROUP)), small_ids((PIECE, GROUP))
    hi, lo = (part.astype(jnp.float32).astype(jnp.bfloat16) for part in quotient(pos, PIECE))
    total = jnp.zeros((len(values) * pieces, PIECE), jnp.float32)
    for at in range(0, pos.shape[1], GROUP):
        here = slice(at, at + GROUP)
        chosen = hi_ids == hi[:, here]
        left = jnp.concatenate([jnp.where(chosen, v[:, here], jnp.bfloat16(0)) for v in values], axis=0)
        total += across(left, one_hot(lo_ids, lo[:, here]))
    return [total[k * pieces : (k + 1) * pieces] for k in range(len(values))]


def sort_kernel(shape, groups, cell_ref, pos_ref, *refs):
    *refs, prefix_ref = refs
    rows, levels, lons = shape
    _, obs = cell_ref.shape
    tiles, pieces = obs // LANES, obs // PIECE
    bins = rows // BIN
    bin_ids = small_ids((bins, LANES))
    square = (LANES, LANES)
    upper = (ids_of(square, 0) <= ids_of(square, 1)).astype(jnp.bfloat16)
    counting = jnp.concatenate([upper, jnp.ones((LANES, 128), jnp.bfloat16)], axis=1)
    before = (ids_of((bins, bins), 1) < ids_of((bins, bins), 0)).astype(jnp.float32)
    wide = lambda v: jnp.concatenate([v] * (LANES // 128), axis=1)
    _, cells = quotient(cell_ref[...], rows * levels * lons)
    keys, lons_of = quotient(cells, lons)
    bins_of, _ = quotient(keys, levels * BIN)
    middle = lons // 2
    signed = jnp.where(lons_of < middle, lons_of, middle - 1 - lons_of)
    keys, bins_of, signed = (v.astype(jnp.float32).astype(jnp.bfloat16) for v in (keys, bins_of, signed))
    outs = len(refs) // len(groups)
    for slot, (group, mine) in enumerate([(g, m) for m, g in enumerate(groups) for _ in g]):
        *place_refs, bounds_ref = refs[mine * outs : (mine + 1) * outs]
        turn = slot - group[0]
        in_bin = bins_of[slot : slot + 1]
        hots = [one_hot(bin_ids, in_bin[:, at * LANES : (at + 1) * LANES]) for at in range(tiles)]
        prefix_ref[...] = jnp.dot(jnp.concatenate(hots, axis=0), counting, preferred_element_type=jnp.float32)
        total = jnp.zeros((bins, 128), jnp.float32)
        for at in range(tiles):
            total += prefix_ref[pl.ds(at * bins, bins), pl.ds(LANES, 128)]
        carry = jnp.dot(before, total, precision=lax.Precision.HIGHEST, preferred_element_type=jnp.float32) - 1.0
        places = []
        for at in range(tiles):
            here = pl.ds(at * bins, bins)
            place = (prefix_ref[here, pl.ds(0, LANES)] + wide(carry)) * hots[at].astype(jnp.float32)
            places.append(jnp.sum(place, axis=0, keepdims=True))
            carry += prefix_ref[here, pl.ds(LANES, 128)]
        pos = jnp.concatenate(places, axis=1).astype(jnp.int32)
        pos_ref[pl.ds(slot, 1), :] = pos
        key, lane = permute(pos, [keys[slot : slot + 1], signed[slot : slot + 1]], pieces)
        key, lane = key.astype(jnp.int32), lane.astype(jnp.int32)
        row, level = quotient(key, levels)
        lon = jnp.where(lane < 0, middle - 1 - lane, lane)
        here = pl.ds(turn * pieces, pieces)
        for near, place_ref, lane_ref in zip((PICK_LONS, SCATTER_LONS), place_refs[::2], place_refs[1::2]):
            part, lane = quotient(lon, near)
            place_ref[here, :] = (row * (lons // near) + part) * levels + level
            lane_ref[here, :] = lane.astype(jnp.float32)
        begin_row = quotient(row, BIN)[0] * BIN
        first = jnp.minimum(begin_row[:, :1], rows - WINDOW)
        last = begin_row[:, PIECE - 1 :] + BIN - 1
        begin = jnp.concatenate([first[:1], first[:-1]], axis=0)
        ends_tile = quotient(ids_of((pieces, 1), 0), LANES // PIECE)[1] == LANES // PIECE - 1
        far = jnp.max(jnp.where(ends_tile, last - begin, 0), axis=0, keepdims=True)
        spread = [jnp.broadcast_to(v.astype(jnp.float32), (pieces, 128)).T[:1].astype(jnp.int32) for v in (first, last)]
        spread.append(jnp.broadcast_to(far, (1, pieces)))
        for kind, v in enumerate(spread):
            bounds_ref[pl.ds(kind * len(group) + turn, 1), pl.ds(0, pieces)] = v


def arrange_kernel(group, pos_ref, innov_ref, weight_ref, quality_ref, keep_ref, want_ref):
    pieces = pos_ref.shape[1] // PIECE
    mine = slice(group[0], group[-1] + 1)
    keeps = two_parts(quality_ref[mine, :].astype(jnp.float32) * weight_ref[mine, :])
    wants = two_parts(innov_ref[mine, :])
    for turn, slot in enumerate(group):
        at = slice(turn, turn + 1)
        moved = permute(pos_ref[slot : slot + 1, :], [part[at] for part in keeps + wants], pieces)
        here = pl.ds(turn * pieces, pieces)
        keep_ref[here, :] = moved[0] + moved[1]
        want_ref[here, :] = moved[2] + moved[3]


def tile_row(ref, at):
    parts = LANES // PIECE
    return jnp.concatenate([ref[pl.ds(at * parts + k, 1), :] for k in range(parts)], axis=1)


def window_places(place_ref, at, start, low_row, per_row):
    place = tile_row(place_ref, at) - start * per_row
    if low_row is None:
        return place
    return jnp.where(place < (low_row - start) * per_row, -1, place)


def over_windows(tiles, slots, rows, bounds_ref, scalar_ref, sem, step):
    parts = LANES // PIECE
    bounds = bounds_ref[...]
    for tile in range(tiles):
        for slot in range(slots):
            step(slot, tile, bounds[slot, tile * parts], None)

    for slot in range(slots):

        @pl.when(bounds[2 * slots + slot, 0] >= WINDOW)
        def _():
            pltpu.async_copy(bounds_ref, scalar_ref, sem).wait()

            @pl.loop(0, tiles)
            def _(tile):
                begin = scalar_ref[slot, tile * parts]
                end = scalar_ref[slots + slot, (tile + 1) * parts - 1]

                @pl.loop(1, lax.div(end - begin, WINDOW) + 1)
                def _(turn):
                    low_row = begin + turn * WINDOW
                    step(slot, tile, jnp.minimum(low_row, rows - WINDOW), low_row)


def pick_kernel(group, sides, own_ref, circ_high_ref, circ_low_ref, *refs):
    if sides:
        low, high = halo(refs[:sides])
        refs = refs[sides:]
    ens_ref, place_ref, lane_ref, bounds_ref, out_ref, *part_refs, scalar_ref, sem = refs
    rows, levels, lons = own_ref.shape
    slots = len(group)
    tiles = place_ref.shape[0] * PIECE // (slots * LANES)
    local_ref = own_ref
    if sides:
        local_ref, *part_refs = part_refs
        mixed = smooth_rows(low, own_ref[...], high).reshape(rows * levels, lons)
        local_ref[...] = smooth_lons(mixed, circ_high_ref[...], circ_low_ref[...]).reshape(local_ref.shape)
    for slot in range(slots):
        field = ens_ref[group[slot]].astype(jnp.float32) * local_ref[...]
        first = field.astype(jnp.bfloat16).astype(jnp.float32)
        part_refs[slot][...] = jnp.concatenate([first, field - first], axis=1).astype(jnp.bfloat16)
    parts = lons // PICK_LONS
    size = WINDOW * parts * levels
    place_ids = ids_of((size, LANES), 0)
    lane_ids = small_ids((PICK_LONS, LANES))

    def step(slot, tile, start, low_row):
        at = slot * tiles + tile
        place = window_places(place_ref, at, start, low_row, parts * levels)
        part = part_refs[slot][pl.ds(start, WINDOW)]
        left = jnp.stack([part[:, :, k * PICK_LONS : (k + 1) * PICK_LONS] for k in range(parts)], axis=1).reshape(2 * size, PICK_LONS)
        hot = one_hot(lane_ids, tile_row(lane_ref, at).astype(jnp.bfloat16))
        both = jnp.dot(left, hot, preferred_element_type=jnp.float32).reshape(WINDOW * parts, 2, levels, LANES)
        value = (both[:, 0] + both[:, 1]).reshape(size, LANES)
        value = jnp.sum(jnp.where(place_ids == place, value, 0.0), axis=0, keepdims=True)
        for k in range(LANES // PIECE):
            here, part = pl.ds(at * (LANES // PIECE) + k, 1), value[:, k * PIECE : (k + 1) * PIECE]
            out_ref[here, :] = part if low_row is None else out_ref[here, :] + part

    over_windows(tiles, slots, rows, bounds_ref, scalar_ref, sem, step)


def scatter_kernel(group, norm_scale, earlier, seen_ref, want_ref, keep_ref, place_ref, lane_ref, ens_ref, *refs):
    before_refs, refs = refs[:earlier], refs[earlier:]
    bounds_ref, back_ref, cost_ref, wres_ref, *grad_refs, scalar_ref, sem = refs
    slots = len(group)
    _, rows, levels, lons = ens_ref.shape
    tiles = place_ref.shape[0] * PIECE // (slots * LANES)
    resid = seen_ref[...] * norm_scale - want_ref[...]
    wres_ref[...] = keep_ref[...] * resid
    cost = jnp.sum((wres_ref[...] * resid).reshape(-1, *cost_ref.shape), axis=0)
    cost_ref[...] = cost + before_refs[1][...] if earlier else cost
    parts = lons // SCATTER_LONS
    size = WINDOW * parts * levels
    place_ids = small_ids((size, LANES))
    lane_ids = small_ids((SCATTER_LONS, LANES))
    for slot in range(slots):
        grad_refs[slot][...] = jnp.zeros(grad_refs[slot].shape, jnp.float32)

    def step(slot, tile, start, low_row):
        at = slot * tiles + tile
        place = window_places(place_ref, at, start, low_row, parts * levels)
        chosen = place_ids == place.astype(jnp.float32).astype(jnp.bfloat16)
        left = [jnp.where(chosen, part, jnp.bfloat16(0)) for part in two_parts(tile_row(wres_ref, at))]
        left = jnp.concatenate(left, axis=0)
        hot = one_hot(lane_ids, tile_row(lane_ref, at).astype(jnp.bfloat16))
        both = across(left, hot)
        grad_refs[slot][pl.ds(start, WINDOW)] += (both[:size] + both[size:]).reshape(WINDOW, parts, levels, SCATTER_LONS)

    over_windows(tiles, slots, rows, bounds_ref, scalar_ref, sem, step)
    total = jnp.zeros((rows, levels, lons), jnp.float32)
    for slot in range(slots):
        grad = jnp.concatenate([grad_refs[slot][:, k] for k in range(parts)], axis=2)
        total += ens_ref[group[slot]].astype(jnp.float32) * grad
    total = total * norm_scale
    back_ref[...] = total + before_refs[0][...] if earlier else total


def grad_kernel(sides, *refs):
    low, high = halo(refs[:sides])
    own_ref, circ_high_ref, circ_low_ref, weights_ref, obs_cost_ref, grad_ref, sums_ref = refs[sides:]
    rows, levels, lons = own_ref.shape
    mixed = smooth_rows(low, own_ref[...], high).reshape(rows * levels, lons)
    weights = weights_ref[...].reshape(rows * levels, lons)
    grad = weights + smooth_lons(mixed, circ_high_ref[...], circ_low_ref[...])
    grad_ref[...] = grad.reshape(grad_ref.shape)
    lane = lax.broadcasted_iota(jnp.int32, sums_ref.shape, 1)
    prior = jnp.sum(weights * weights)
    square = jnp.sum(grad * grad)
    obs_cost = jnp.sum(obs_cost_ref[...])
    sums_ref[...] = jnp.where(lane == 0, square, jnp.where(lane == 1, prior, jnp.where(lane == 2, obs_cost, 0.0)))


def update_kernel(members, entries, sums_ref, own_ref, grad_ref, new_ref, cost_ref):
    totals = jnp.sum(sums_ref[...], axis=0, keepdims=True)
    length = jnp.sqrt(totals[:, :1] / entries + EPSILON)
    new_ref[...] = own_ref[...] - grad_ref[...] * (STEP_LENGTH / length)[None]
    cost_ref[...] = (0.5 * totals[:, 1:2] + 0.5 * totals[:, 2:3] / members) / entries


def call(body, out_shape, scratch, flops, *operands):
    vmem = pl.BlockSpec(memory_space=pltpu.VMEM)
    return pl.pallas_call(
        body,
        out_shape=out_shape,
        in_specs=[vmem] * len(operands),
        out_specs=jax.tree.map(lambda _: vmem, out_shape),
        scratch_shapes=scratch,
        compiler_params=pltpu.CompilerParams(vmem_limit_bytes=48 * MIB),
        cost_estimate=pl.CostEstimate(flops=flops, bytes_accessed=2 * MIB, transcendentals=0),
    )(*operands)


def edges(field):
    count = lax.axis_size("lat")
    if count == 2:
        rows = field.shape[0]
        start = (rows - HALF) * (1 - lax.axis_index("lat"))
        edge = lax.dynamic_slice_in_dim(field, start, HALF, 0)
        return [lax.ppermute(edge, "lat", [(0, 1), (1, 0)])]
    forward = [(i, i + 1) for i in range(count - 1)]
    backward = [(target, source) for source, target in forward]
    low = lax.ppermute(field[-HALF:], "lat", forward)
    high = lax.ppermute(field[:HALF], "lat", backward)
    return [low, high]


def halo(refs):
    if len(refs) == 2:
        return refs[0][...], refs[1][...]
    last = lax.axis_index("lat") == 1
    return jnp.where(last, refs[0][...], 0.0), jnp.where(last, 0.0, refs[0][...])


def summed(value, axis, turn=0):
    count = lax.axis_size(axis)
    if count & (count - 1):
        return lax.psum(value, axis)
    aways = [1 << k for k in range(count.bit_length() - 1)]
    for away in aways[turn:] + aways[:turn]:
        value = value + lax.ppermute(value, axis, [(i, i ^ away) for i in range(count)])
    return value


def like(shape, kind=jnp.float32):
    return jax.ShapeDtypeStruct(shape, kind)


def sort_cells(obs_cell, shape, groups):
    slots, obs = obs_cell.shape
    kinds = [like((slots, obs), jnp.int32)]
    for group in groups:
        ordered = (len(group) * obs // PIECE, PIECE)
        kinds += [like(ordered, jnp.int32), like(ordered)] * 2
        kinds += [like((-(-3 * len(group) // 8) * 8, -(-(obs // PIECE) // 128) * 128), jnp.int32)]
    scratch = [pltpu.VMEM((obs // LANES * shape[0] // BIN, LANES + 128), jnp.float32)]
    pos, *outs = call(functools.partial(sort_kernel, shape, groups), kinds, scratch, COST, obs_cell)
    outs = [outs[k : k + 5] for k in range(0, len(outs), 5)]
    return pos, [(out[:2], out[2:4], out[4]) for out in outs]


def arrange(pos, innovation, obs_weight, quality, group):
    ordered = like((len(group) * pos.shape[1] // PIECE, PIECE))
    body = functools.partial(arrange_kernel, group)
    return call(body, [ordered, ordered], [], COST, pos, innovation, obs_weight, quality)


def pick(sides, own, circ, ens, at, bounds, group):
    rows, levels, lons = own.shape
    kinds = [like(at[0].shape)] + [like(own.shape)] * (len(sides) > 0)
    scratch = [pltpu.VMEM((rows, 2 * levels, lons), jnp.bfloat16)] * len(group)
    scratch += [pltpu.SMEM(bounds.shape, jnp.int32), pltpu.SemaphoreType.DMA]
    body = functools.partial(pick_kernel, group, len(sides))
    return call(body, kinds, scratch, COST, own, *circ, *sides, ens, *at, bounds)


def scatter(seen, want, keep, ens, at, bounds, norm_scale, group, earlier):
    _, rows, levels, lons = ens.shape
    scratch = [pltpu.VMEM(seen.shape, jnp.float32)]
    scratch += [pltpu.VMEM((rows, lons // SCATTER_LONS, levels, SCATTER_LONS), jnp.float32)] * len(group)
    kinds = [like((rows, levels, lons)), like((8, 128))]
    scratch += [pltpu.SMEM(bounds.shape, jnp.int32), pltpu.SemaphoreType.DMA]
    body = functools.partial(scatter_kernel, group, norm_scale, len(earlier))
    return call(body, kinds, scratch, COST, seen, want, keep, *at, ens, *earlier, bounds)


def gradient(sides, own, circ, weights, obs_cost, devices):
    kinds = [like(own.shape), like((devices, 128))]
    body = functools.partial(grad_kernel, len(sides))
    return call(body, kinds, [], COST, *sides, own, *circ, weights, obs_cost)


def local(ensemble, weights, obs_cell, innovation, obs_weight, quality):
    _, rows, levels, lons = weights.shape
    members, bands = lax.axis_size("mem"), lax.axis_size("lat")
    norm_scale = 1.0 / math.sqrt(members - 1)
    ens, own = ensemble[0], weights[0]
    circ = [jnp.asarray(part) for part in circulant_parts(lons)]
    slots = obs_cell.shape[0]
    size = slots // GROUPS
    groups = [range(k, k + size) for k in range(0, slots, size)]
    sides = edges(own)
    pos, ordered = sort_cells(obs_cell, own.shape, groups)
    arranged = [arrange(pos, innovation, obs_weight, quality, group) for group in groups]
    local_weights, seen = None, []
    for turn, (group, (pick_at, _, bounds)) in enumerate(zip(groups, ordered)):
        if turn == 0:
            picked, local_weights = pick(sides, own, circ, ens, pick_at, bounds, group)
        else:
            (picked,) = pick([], local_weights, circ, ens, pick_at, bounds, group)
        seen.append(summed(picked, "mem", 2 * turn))
    sofar = []
    for group, total, (keep, want), (_, scatter_at, bounds) in zip(groups, seen, arranged, ordered):
        sofar = scatter(total, want, keep, ens, scatter_at, bounds, norm_scale, group, sofar)
    back, obs_cost = sofar
    grad, sums = gradient(edges(back), back, circ, own, obs_cost, members * bands)
    sums = lax.all_to_all(sums, ("mem", "lat"), 0, 0, tiled=True)
    body = functools.partial(update_kernel, members, float(members * bands * rows * levels * lons))
    new_weights, cost = call(body, [like(own.shape), like((1, 1))], [], 10**8, sums, own, grad)
    return new_weights[None], cost[0, 0]


def solution(mesh):
    placed = (
        P("mem", None, "lat", None, None),
        P("mem", "lat", None, None),
        P(None, "lat"),
        P(None, "lat"),
        P(None, "lat"),
        P(None, "lat"),
    )
    return jax.shard_map(
        local,
        mesh=mesh,
        in_specs=placed,
        out_specs=(P("mem", "lat", None, None), P()),
        check_vma=False,
    )
```

```python
import functools
import math

import jax
import jax.numpy as jnp
import numpy as np
from jax import lax
from jax.experimental import pallas as pl
from jax.experimental.pallas import tpu as pltpu
from jax.sharding import PartitionSpec as P

HALF = 8
STEP_LENGTH = 0.5
EPSILON = 1e-06
LANES = 256
PIECE = 128
PICK_LONS = 256
SCATTER_LONS = 128
GROUP = 1024
BIN = 1
WINDOW = 3
GROUPS = 2
COST = 10**9
MIB = 1024 * 1024


def taps():
    sigma = HALF / 2.0
    every = np.arange(-HALF, HALF + 1).astype(np.float64)
    normal = np.sqrt(np.sum(np.exp(-((every / sigma) ** 2))))
    return np.exp(-0.5 * (every / sigma) ** 2) / normal


def circulant_parts(lon_count):
    full = np.zeros((lon_count, lon_count), np.float32)
    at = np.arange(lon_count)
    for shift_by, tap in zip(range(-HALF, HALF + 1), taps()):
        full[at, (at + shift_by) % lon_count] += np.float32(tap)
    high = full.astype(jnp.bfloat16)
    low = (full - high.astype(np.float32)).astype(jnp.bfloat16)
    return high, low


def two_parts(value):
    high = value.astype(jnp.bfloat16)
    low = (value - high.astype(jnp.float32)).astype(jnp.bfloat16)
    return high, low


def smooth_rows(low, own, high):
    tap = [float(t) for t in taps()]
    padded = jnp.concatenate([low, own, high], axis=0)
    rows = own.shape[0]
    total = padded[HALF : HALF + rows] * tap[HALF]
    for away in range(1, HALF + 1):
        pair = padded[HALF - away : HALF - away + rows] + padded[HALF + away : HALF + away + rows]
        total = total + pair * tap[HALF + away]
    return total


def smooth_lons(field, circ_high, circ_low):
    first, second = two_parts(field)
    dot = functools.partial(jnp.dot, preferred_element_type=jnp.float32)
    return dot(first, circ_high) + (dot(second, circ_high) + dot(first, circ_low))


def quotient(value, by):
    if by & (by - 1):
        return lax.div(value, by), lax.rem(value, by)
    return lax.shift_right_logical(value, by.bit_length() - 1), lax.bitwise_and(value, by - 1)


def small_ids(shape):
    return lax.broadcasted_iota(jnp.int32, shape, 0).astype(jnp.bfloat16)


def one_hot(ids, at):
    return jnp.where(ids == at, jnp.bfloat16(1), jnp.bfloat16(0))


def ids_of(shape, dim):
    return lax.broadcasted_iota(jnp.int32, shape, dim)


def across(left, right):
    return lax.dot_general(left, right, (((1,), (1,)), ((), ())), preferred_element_type=jnp.float32)


def permute(pos, values, pieces):
    hi_ids, lo_ids = small_ids((pieces, GROUP)), small_ids((PIECE, GROUP))
    hi, lo = (part.astype(jnp.float32).astype(jnp.bfloat16) for part in quotient(pos, PIECE))
    total = jnp.zeros((len(values) * pieces, PIECE), jnp.float32)
    for at in range(0, pos.shape[1], GROUP):
        here = slice(at, at + GROUP)
        chosen = hi_ids == hi[:, here]
        left = jnp.concatenate([jnp.where(chosen, v[:, here], jnp.bfloat16(0)) for v in values], axis=0)
        total += across(left, one_hot(lo_ids, lo[:, here]))
    return [total[k * pieces : (k + 1) * pieces] for k in range(len(values))]


def sort_kernel(shape, groups, cell_ref, pos_ref, *refs):
    slots, obs = cell_ref.shape
    refs, prefix_refs = refs[:-slots], refs[-slots:]
    rows, levels, lons = shape
    tiles, pieces = obs // LANES, obs // PIECE
    bins = rows // BIN
    bin_ids = small_ids((bins, LANES))
    square = (LANES, LANES)
    upper = (ids_of(square, 0) <= ids_of(square, 1)).astype(jnp.bfloat16)
    counting = jnp.concatenate([upper, jnp.ones((LANES, 128), jnp.bfloat16)], axis=1)
    before = (ids_of((bins, bins), 1) < ids_of((bins, bins), 0)).astype(jnp.bfloat16)
    count = functools.partial(jnp.dot, before, preferred_element_type=jnp.float32)
    wide = lambda v: jnp.concatenate([v] * (LANES // 128), axis=1)
    _, cells = quotient(cell_ref[...], rows * levels * lons)
    keys, lons_of = quotient(cells, lons)
    bins_of, _ = quotient(keys, levels * BIN)
    middle = lons // 2
    signed = jnp.where(lons_of < middle, lons_of, middle - 1 - lons_of)
    keys, bins_of, signed = (v.astype(jnp.float32).astype(jnp.bfloat16) for v in (keys, bins_of, signed))
    outs = len(refs) // len(groups)
    for slot, (group, mine) in enumerate([(g, m) for m, g in enumerate(groups) for _ in g]):
        *place_refs, bounds_ref = refs[mine * outs : (mine + 1) * outs]
        turn = slot - group[0]
        prefix_ref = prefix_refs[slot]
        in_bin = bins_of[slot : slot + 1]
        hots = [one_hot(bin_ids, in_bin[:, at * LANES : (at + 1) * LANES]) for at in range(tiles)]
        prefix_ref[...] = jnp.dot(jnp.concatenate(hots, axis=0), counting, preferred_element_type=jnp.float32)
        total = jnp.zeros((bins, 128), jnp.float32)
        for at in range(tiles):
            total += prefix_ref[pl.ds(at * bins, bins), pl.ds(LANES, 128)]
        many = jnp.floor(total * (1.0 / LANES))
        few = total - many * LANES
        carry = count(many.astype(jnp.bfloat16)) * LANES + count(few.astype(jnp.bfloat16)) - 1.0
        places = []
        for at in range(tiles):
            here = pl.ds(at * bins, bins)
            place = (prefix_ref[here, pl.ds(0, LANES)] + wide(carry)) * hots[at].astype(jnp.float32)
            places.append(jnp.sum(place, axis=0, keepdims=True))
            carry += prefix_ref[here, pl.ds(LANES, 128)]
        pos = jnp.concatenate(places, axis=1).astype(jnp.int32)
        pos_ref[pl.ds(slot, 1), :] = pos
        key, lane = permute(pos, [keys[slot : slot + 1], signed[slot : slot + 1]], pieces)
        key, lane = key.astype(jnp.int32), lane.astype(jnp.int32)
        row, level = quotient(key, levels)
        lon = jnp.where(lane < 0, middle - 1 - lane, lane)
        here = pl.ds(turn * pieces, pieces)
        for near, place_ref, lane_ref in zip((PICK_LONS, SCATTER_LONS), place_refs[::2], place_refs[1::2]):
            part, lane = quotient(lon, near)
            place_ref[here, :] = (row * (lons // near) + part) * levels + level
            lane_ref[here, :] = lane.astype(jnp.float32)
        begin_row = quotient(row, BIN)[0] * BIN
        first = jnp.minimum(begin_row[:, :1], rows - WINDOW)
        last = begin_row[:, PIECE - 1 :] + BIN - 1
        begin = jnp.concatenate([first[:1], first[:-1]], axis=0)
        ends_tile = quotient(ids_of((pieces, 1), 0), LANES // PIECE)[1] == LANES // PIECE - 1
        far = jnp.max(jnp.where(ends_tile, last - begin, 0), axis=0, keepdims=True)
        spread = [jnp.broadcast_to(v.astype(jnp.float32), (pieces, 128)).T[:1].astype(jnp.int32) for v in (first, last)]
        spread.append(jnp.broadcast_to(far, (1, pieces)))
        for kind, v in enumerate(spread):
            bounds_ref[pl.ds(kind * len(group) + turn, 1), pl.ds(0, pieces)] = v


def arrange_kernel(group, pos_ref, innov_ref, weight_ref, quality_ref, keep_ref, want_ref):
    pieces = pos_ref.shape[1] // PIECE
    mine = slice(group[0], group[-1] + 1)
    keeps = two_parts(quality_ref[mine, :].astype(jnp.float32) * weight_ref[mine, :])
    wants = two_parts(innov_ref[mine, :])
    for turn, slot in enumerate(group):
        at = slice(turn, turn + 1)
        moved = permute(pos_ref[slot : slot + 1, :], [part[at] for part in keeps + wants], pieces)
        here = pl.ds(turn * pieces, pieces)
        keep_ref[here, :] = moved[0] + moved[1]
        want_ref[here, :] = moved[2] + moved[3]


def tile_row(ref, at):
    parts = LANES // PIECE
    return jnp.concatenate([ref[pl.ds(at * parts + k, 1), :] for k in range(parts)], axis=1)


def window_places(place_ref, at, start, low_row, per_row):
    place = tile_row(place_ref, at) - start * per_row
    if low_row is None:
        return place
    return jnp.where(place < (low_row - start) * per_row, -1, place)


def over_windows(tiles, slots, rows, bounds_ref, scalar_ref, sem, step):
    parts = LANES // PIECE
    bounds = bounds_ref[...]
    for tile in range(tiles):
        for slot in range(slots):
            step(slot, tile, bounds[slot, tile * parts], None)

    for slot in range(slots):

        @pl.when(bounds[2 * slots + slot, 0] >= WINDOW)
        def _():
            pltpu.async_copy(bounds_ref, scalar_ref, sem).wait()

            @pl.loop(0, tiles)
            def _(tile):
                begin = scalar_ref[slot, tile * parts]
                end = scalar_ref[slots + slot, (tile + 1) * parts - 1]

                @pl.loop(1, lax.div(end - begin, WINDOW) + 1)
                def _(turn):
                    low_row = begin + turn * WINDOW
                    step(slot, tile, jnp.minimum(low_row, rows - WINDOW), low_row)


def pick_kernel(group, sides, own_ref, circ_high_ref, circ_low_ref, *refs):
    if sides:
        low, high = halo(refs[:sides])
        refs = refs[sides:]
    ens_ref, place_ref, lane_ref, bounds_ref, out_ref, *part_refs, scalar_ref, sem = refs
    rows, levels, lons = own_ref.shape
    slots = len(group)
    tiles = place_ref.shape[0] * PIECE // (slots * LANES)
    local_ref = own_ref
    if sides:
        local_ref, *part_refs = part_refs
        mixed = smooth_rows(low, own_ref[...], high).reshape(rows * levels, lons)
        local_ref[...] = smooth_lons(mixed, circ_high_ref[...], circ_low_ref[...]).reshape(local_ref.shape)
    for slot in range(slots):
        field = ens_ref[group[slot]].astype(jnp.float32) * local_ref[...]
        first = field.astype(jnp.bfloat16).astype(jnp.float32)
        part_refs[slot][...] = jnp.concatenate([first, field - first], axis=1).astype(jnp.bfloat16)
    parts = lons // PICK_LONS
    size = WINDOW * parts * levels
    place_ids = ids_of((size, LANES), 0)
    lane_ids = small_ids((PICK_LONS, LANES))

    def step(slot, tile, start, low_row):
        at = slot * tiles + tile
        place = window_places(place_ref, at, start, low_row, parts * levels)
        part = part_refs[slot][pl.ds(start, WINDOW)]
        left = jnp.stack([part[:, :, k * PICK_LONS : (k + 1) * PICK_LONS] for k in range(parts)], axis=1).reshape(2 * size, PICK_LONS)
        hot = one_hot(lane_ids, tile_row(lane_ref, at).astype(jnp.bfloat16))
        both = jnp.dot(left, hot, preferred_element_type=jnp.float32).reshape(WINDOW * parts, 2, levels, LANES)
        value = (both[:, 0] + both[:, 1]).reshape(size, LANES)
        value = jnp.sum(jnp.where(place_ids == place, value, 0.0), axis=0, keepdims=True)
        for k in range(LANES // PIECE):
            here, part = pl.ds(at * (LANES // PIECE) + k, 1), value[:, k * PIECE : (k + 1) * PIECE]
            out_ref[here, :] = part if low_row is None else out_ref[here, :] + part

    over_windows(tiles, slots, rows, bounds_ref, scalar_ref, sem, step)


def scatter_kernel(group, norm_scale, earlier, seen_ref, want_ref, keep_ref, place_ref, lane_ref, ens_ref, *refs):
    before_refs, refs = refs[:earlier], refs[earlier:]
    bounds_ref, back_ref, cost_ref, wres_ref, *grad_refs, scalar_ref, sem = refs
    slots = len(group)
    _, rows, levels, lons = ens_ref.shape
    tiles = place_ref.shape[0] * PIECE // (slots * LANES)
    resid = seen_ref[...] * norm_scale - want_ref[...]
    wres_ref[...] = keep_ref[...] * resid
    cost = jnp.sum((wres_ref[...] * resid).reshape(-1, *cost_ref.shape), axis=0)
    cost_ref[...] = cost + before_refs[1][...] if earlier else cost
    parts = lons // SCATTER_LONS
    size = WINDOW * parts * levels
    place_ids = small_ids((size, LANES))
    lane_ids = small_ids((SCATTER_LONS, LANES))
    for slot in range(slots):
        grad_refs[slot][...] = jnp.zeros(grad_refs[slot].shape, jnp.float32)

    def step(slot, tile, start, low_row):
        at = slot * tiles + tile
        place = window_places(place_ref, at, start, low_row, parts * levels)
        chosen = place_ids == place.astype(jnp.float32).astype(jnp.bfloat16)
        left = [jnp.where(chosen, part, jnp.bfloat16(0)) for part in two_parts(tile_row(wres_ref, at))]
        left = jnp.concatenate(left, axis=0)
        hot = one_hot(lane_ids, tile_row(lane_ref, at).astype(jnp.bfloat16))
        both = across(left, hot)
        grad_refs[slot][pl.ds(start, WINDOW)] += (both[:size] + both[size:]).reshape(WINDOW, parts, levels, SCATTER_LONS)

    over_windows(tiles, slots, rows, bounds_ref, scalar_ref, sem, step)
    total = jnp.zeros((rows, levels, lons), jnp.float32)
    for slot in range(slots):
        grad = jnp.concatenate([grad_refs[slot][:, k] for k in range(parts)], axis=2)
        total += ens_ref[group[slot]].astype(jnp.float32) * grad
    total = total * norm_scale
    back_ref[...] = total + before_refs[0][...] if earlier else total


def grad_kernel(sides, *refs):
    low, high = halo(refs[:sides])
    own_ref, circ_high_ref, circ_low_ref, weights_ref, obs_cost_ref, grad_ref, sums_ref = refs[sides:]
    rows, levels, lons = own_ref.shape
    mixed = smooth_rows(low, own_ref[...], high).reshape(rows * levels, lons)
    weights = weights_ref[...].reshape(rows * levels, lons)
    grad = weights + smooth_lons(mixed, circ_high_ref[...], circ_low_ref[...])
    grad_ref[...] = grad.reshape(grad_ref.shape)
    lane = lax.broadcasted_iota(jnp.int32, sums_ref.shape, 1)
    prior = jnp.sum(weights * weights)
    square = jnp.sum(grad * grad)
    obs_cost = jnp.sum(obs_cost_ref[...])
    sums_ref[...] = jnp.where(lane == 0, square, jnp.where(lane == 1, prior, jnp.where(lane == 2, obs_cost, 0.0)))


def update_kernel(members, entries, sums_ref, own_ref, grad_ref, new_ref, cost_ref):
    totals = jnp.sum(sums_ref[...], axis=0, keepdims=True)
    length = jnp.sqrt(totals[:, :1] / entries + EPSILON)
    new_ref[...] = own_ref[...] - grad_ref[...] * (STEP_LENGTH / length)[None]
    cost_ref[...] = (0.5 * totals[:, 1:2] + 0.5 * totals[:, 2:3] / members) / entries


def call(body, out_shape, scratch, flops, *operands):
    vmem = pl.BlockSpec(memory_space=pltpu.VMEM)
    return pl.pallas_call(
        body,
        out_shape=out_shape,
        in_specs=[vmem] * len(operands),
        out_specs=jax.tree.map(lambda _: vmem, out_shape),
        scratch_shapes=scratch,
        compiler_params=pltpu.CompilerParams(vmem_limit_bytes=48 * MIB),
        cost_estimate=pl.CostEstimate(flops=flops, bytes_accessed=2 * MIB, transcendentals=0),
    )(*operands)


def edges(field):
    count = lax.axis_size("lat")
    if count == 2:
        rows = field.shape[0]
        start = (rows - HALF) * (1 - lax.axis_index("lat"))
        edge = lax.dynamic_slice_in_dim(field, start, HALF, 0)
        return [lax.ppermute(edge, "lat", [(0, 1), (1, 0)])]
    forward = [(i, i + 1) for i in range(count - 1)]
    backward = [(target, source) for source, target in forward]
    low = lax.ppermute(field[-HALF:], "lat", forward)
    high = lax.ppermute(field[:HALF], "lat", backward)
    return [low, high]


def halo(refs):
    if len(refs) == 2:
        return refs[0][...], refs[1][...]
    last = lax.axis_index("lat") == 1
    rows = refs[0].shape[0]
    return jnp.where(last, refs[0][rows - HALF :], 0.0), jnp.where(last, 0.0, refs[0][:HALF])


def summed(value, axis, turn=0):
    count = lax.axis_size(axis)
    if count & (count - 1):
        return lax.psum(value, axis)
    aways = [1 << k for k in range(count.bit_length() - 1)]
    for away in aways[turn:] + aways[:turn]:
        value = value + lax.ppermute(value, axis, [(i, i ^ away) for i in range(count)])
    return value


def like(shape, kind=jnp.float32):
    return jax.ShapeDtypeStruct(shape, kind)


def sort_cells(obs_cell, shape, groups):
    slots, obs = obs_cell.shape
    kinds = [like((slots, obs), jnp.int32)]
    for group in groups:
        ordered = (len(group) * obs // PIECE, PIECE)
        kinds += [like(ordered, jnp.int32), like(ordered)] * 2
        kinds += [like((-(-3 * len(group) // 8) * 8, -(-(obs // PIECE) // 128) * 128), jnp.int32)]
    scratch = [pltpu.VMEM((obs // LANES * shape[0] // BIN, LANES + 128), jnp.float32)] * slots
    pos, *outs = call(functools.partial(sort_kernel, shape, groups), kinds, scratch, COST, obs_cell)
    outs = [outs[k : k + 5] for k in range(0, len(outs), 5)]
    return pos, [(out[:2], out[2:4], out[4]) for out in outs]


def arrange(pos, innovation, obs_weight, quality, group):
    ordered = like((len(group) * pos.shape[1] // PIECE, PIECE))
    body = functools.partial(arrange_kernel, group)
    return call(body, [ordered, ordered], [], COST, pos, innovation, obs_weight, quality)


def pick(sides, own, circ, ens, at, bounds, group):
    rows, levels, lons = own.shape
    kinds = [like(at[0].shape)] + [like(own.shape)] * (len(sides) > 0)
    scratch = [pltpu.VMEM((rows, 2 * levels, lons), jnp.bfloat16)] * len(group)
    scratch += [pltpu.SMEM(bounds.shape, jnp.int32), pltpu.SemaphoreType.DMA]
    body = functools.partial(pick_kernel, group, len(sides))
    return call(body, kinds, scratch, COST, own, *circ, *sides, ens, *at, bounds)


def scatter(seen, want, keep, ens, at, bounds, norm_scale, group, earlier):
    _, rows, levels, lons = ens.shape
    scratch = [pltpu.VMEM(seen.shape, jnp.float32)]
    scratch += [pltpu.VMEM((rows, lons // SCATTER_LONS, levels, SCATTER_LONS), jnp.float32)] * len(group)
    kinds = [like((rows, levels, lons)), like((8, 128))]
    scratch += [pltpu.SMEM(bounds.shape, jnp.int32), pltpu.SemaphoreType.DMA]
    body = functools.partial(scatter_kernel, group, norm_scale, len(earlier))
    return call(body, kinds, scratch, COST, seen, want, keep, *at, ens, *earlier, bounds)


def gradient(sides, own, circ, weights, obs_cost, devices):
    kinds = [like(own.shape), like((devices, 128))]
    body = functools.partial(grad_kernel, len(sides))
    return call(body, kinds, [], COST, *sides, own, *circ, weights, obs_cost)


def local(ensemble, weights, obs_cell, innovation, obs_weight, quality):
    _, rows, levels, lons = weights.shape
    members, bands = lax.axis_size("mem"), lax.axis_size("lat")
    norm_scale = 1.0 / math.sqrt(members - 1)
    ens, own = ensemble[0], weights[0]
    circ = [jnp.asarray(part) for part in circulant_parts(lons)]
    slots = obs_cell.shape[0]
    size = slots // GROUPS
    groups = [range(k, k + size) for k in range(0, slots, size)]
    sides = [lax.ppermute(own, "lat", [(0, 1), (1, 0)])] if bands == 2 else edges(own)
    pos, ordered = sort_cells(obs_cell, own.shape, groups)
    arranged = [arrange(pos, innovation, obs_weight, quality, group) for group in groups]
    local_weights, seen = None, []
    for turn, (group, (pick_at, _, bounds)) in enumerate(zip(groups, ordered)):
        if turn == 0:
            picked, local_weights = pick(sides, own, circ, ens, pick_at, bounds, group)
        else:
            (picked,) = pick([], local_weights, circ, ens, pick_at, bounds, group)
        seen.append(summed(picked, "mem", 2 * turn))
    sofar = []
    for group, total, (keep, want), (_, scatter_at, bounds) in zip(groups, seen, arranged, ordered):
        sofar = scatter(total, want, keep, ens, scatter_at, bounds, norm_scale, group, sofar)
    back, obs_cost = sofar
    grad, sums = gradient(edges(back), back, circ, own, obs_cost, members * bands)
    sums = lax.all_to_all(sums, ("mem", "lat"), 0, 0, tiled=True)
    body = functools.partial(update_kernel, members, float(members * bands * rows * levels * lons))
    new_weights, cost = call(body, [like(own.shape), like((1, 1))], [], 10**8, sums, own, grad)
    return new_weights[None], cost[0, 0]


def solution(mesh):
    placed = (
        P("mem", None, "lat", None, None),
        P("mem", "lat", None, None),
        P(None, "lat"),
        P(None, "lat"),
        P(None, "lat"),
        P(None, "lat"),
    )
    return jax.shard_map(
        local,
        mesh=mesh,
        in_specs=placed,
        out_specs=(P("mem", "lat", None, None), P()),
        check_vma=False,
    )
```

```python
import functools
import math

import jax
import jax.numpy as jnp
import numpy as np
from jax import lax
from jax.experimental import pallas as pl
from jax.experimental.pallas import tpu as pltpu
from jax.sharding import PartitionSpec as P

HALF = 8
STEP_LENGTH = 0.5
EPSILON = 1e-06
LANES = 256
PIECE = 128
PICK_LONS = 256
SCATTER_LONS = 128
GROUP = 1024
BIN = 1
WINDOW = 3
GROUPS = 2
COST = 10**9
MIB = 1024 * 1024


def taps():
    sigma = HALF / 2.0
    every = np.arange(-HALF, HALF + 1).astype(np.float64)
    normal = np.sqrt(np.sum(np.exp(-((every / sigma) ** 2))))
    return np.exp(-0.5 * (every / sigma) ** 2) / normal


def circulant_parts(lon_count):
    full = np.zeros((lon_count, lon_count), np.float32)
    at = np.arange(lon_count)
    for shift_by, tap in zip(range(-HALF, HALF + 1), taps()):
        full[at, (at + shift_by) % lon_count] += np.float32(tap)
    high = full.astype(jnp.bfloat16)
    low = (full - high.astype(np.float32)).astype(jnp.bfloat16)
    return high, low


def two_parts(value):
    high = value.astype(jnp.bfloat16)
    low = (value - high.astype(jnp.float32)).astype(jnp.bfloat16)
    return high, low


def smooth_rows(low, own, high):
    tap = [float(t) for t in taps()]
    padded = jnp.concatenate([low, own, high], axis=0)
    rows = own.shape[0]
    total = padded[HALF : HALF + rows] * tap[HALF]
    for away in range(1, HALF + 1):
        pair = padded[HALF - away : HALF - away + rows] + padded[HALF + away : HALF + away + rows]
        total = total + pair * tap[HALF + away]
    return total


def smooth_lons(field, circ_high, circ_low):
    first, second = two_parts(field)
    dot = functools.partial(jnp.dot, preferred_element_type=jnp.float32)
    return dot(first, circ_high) + (dot(second, circ_high) + dot(first, circ_low))


def quotient(value, by):
    if by & (by - 1):
        return lax.div(value, by), lax.rem(value, by)
    return lax.shift_right_logical(value, by.bit_length() - 1), lax.bitwise_and(value, by - 1)


def small_ids(shape):
    return lax.broadcasted_iota(jnp.int32, shape, 0).astype(jnp.bfloat16)


def one_hot(ids, at):
    return jnp.where(ids == at, jnp.bfloat16(1), jnp.bfloat16(0))


def ids_of(shape, dim):
    return lax.broadcasted_iota(jnp.int32, shape, dim)


def across(left, right):
    return lax.dot_general(left, right, (((1,), (1,)), ((), ())), preferred_element_type=jnp.float32)


def permute(pos, values, pieces):
    hi_ids, lo_ids = small_ids((pieces, GROUP)), small_ids((PIECE, GROUP))
    hi, lo = (part.astype(jnp.float32).astype(jnp.bfloat16) for part in quotient(pos, PIECE))
    total = jnp.zeros((len(values) * pieces, PIECE), jnp.float32)
    for at in range(0, pos.shape[1], GROUP):
        here = slice(at, at + GROUP)
        chosen = hi_ids == hi[:, here]
        left = jnp.concatenate([jnp.where(chosen, v[:, here], jnp.bfloat16(0)) for v in values], axis=0)
        total += across(left, one_hot(lo_ids, lo[:, here]))
    return [total[k * pieces : (k + 1) * pieces] for k in range(len(values))]


def sort_kernel(shape, groups, cell_ref, pos_ref, *refs):
    slots, obs = cell_ref.shape
    refs, prefix_refs = refs[:-slots], refs[-slots:]
    rows, levels, lons = shape
    tiles, pieces = obs // LANES, obs // PIECE
    bins = rows // BIN
    bin_ids = small_ids((bins, LANES))
    square = (LANES, LANES)
    upper = (ids_of(square, 0) <= ids_of(square, 1)).astype(jnp.bfloat16)
    ones = jnp.ones((LANES, 128), jnp.bfloat16)
    before = (ids_of((bins, bins), 1) < ids_of((bins, bins), 0)).astype(jnp.bfloat16)
    count = functools.partial(jnp.dot, before, preferred_element_type=jnp.float32)
    wide = lambda v: jnp.concatenate([v] * (LANES // 128), axis=1)
    _, cells = quotient(cell_ref[...], rows * levels * lons)
    keys, lons_of = quotient(cells, lons)
    bins_of, _ = quotient(keys, levels * BIN)
    middle = lons // 2
    signed = jnp.where(lons_of < middle, lons_of, middle - 1 - lons_of)
    keys, bins_of, signed = (v.astype(jnp.float32).astype(jnp.bfloat16) for v in (keys, bins_of, signed))
    outs = len(refs) // len(groups)
    for slot, (group, mine) in enumerate([(g, m) for m, g in enumerate(groups) for _ in g]):
        *place_refs, bounds_ref = refs[mine * outs : (mine + 1) * outs]
        turn = slot - group[0]
        prefix_ref = prefix_refs[slot]
        in_bin = bins_of[slot : slot + 1]
        hots = [one_hot(bin_ids, in_bin[:, at * LANES : (at + 1) * LANES]) for at in range(tiles)]
        prefix_ref[...] = jnp.dot(jnp.concatenate(hots, axis=0), upper, preferred_element_type=jnp.float32)
        total = jnp.dot(sum(hots[1:], hots[0]), ones, preferred_element_type=jnp.float32)
        many = jnp.floor(total * (1.0 / LANES))
        few = total - many * LANES
        carry = count(many.astype(jnp.bfloat16)) * LANES + count(few.astype(jnp.bfloat16)) - 1.0
        places = []
        for at in range(tiles):
            here = pl.ds(at * bins, bins)
            place = (prefix_ref[here, pl.ds(0, LANES)] + wide(carry)) * hots[at].astype(jnp.float32)
            places.append(jnp.sum(place, axis=0, keepdims=True))
            carry += prefix_ref[here, pl.ds(LANES - 1, 1)]
        pos = jnp.concatenate(places, axis=1).astype(jnp.int32)
        pos_ref[pl.ds(slot, 1), :] = pos
        key, lane = permute(pos, [keys[slot : slot + 1], signed[slot : slot + 1]], pieces)
        key, lane = key.astype(jnp.int32), lane.astype(jnp.int32)
        row, level = quotient(key, levels)
        lon = jnp.where(lane < 0, middle - 1 - lane, lane)
        here = pl.ds(turn * pieces, pieces)
        for near, place_ref, lane_ref in zip((PICK_LONS, SCATTER_LONS), place_refs[::2], place_refs[1::2]):
            part, lane = quotient(lon, near)
            place_ref[here, :] = (row * (lons // near) + part) * levels + level
            lane_ref[here, :] = lane.astype(jnp.float32)
        begin_row = quotient(row, BIN)[0] * BIN
        first = jnp.minimum(begin_row[:, :1], rows - WINDOW)
        last = begin_row[:, PIECE - 1 :] + BIN - 1
        begin = jnp.concatenate([first[:1], first[:-1]], axis=0)
        ends_tile = quotient(ids_of((pieces, 1), 0), LANES // PIECE)[1] == LANES // PIECE - 1
        far = jnp.max(jnp.where(ends_tile, last - begin, 0), axis=0, keepdims=True)
        spread = [jnp.broadcast_to(v.astype(jnp.float32), (pieces, 128)).T[:1].astype(jnp.int32) for v in (first, last)]
        spread.append(jnp.broadcast_to(far, (1, pieces)))
        for kind, v in enumerate(spread):
            bounds_ref[pl.ds(kind * len(group) + turn, 1), pl.ds(0, pieces)] = v


def arrange_kernel(group, pos_ref, innov_ref, weight_ref, quality_ref, keep_ref, want_ref):
    pieces = pos_ref.shape[1] // PIECE
    mine = slice(group[0], group[-1] + 1)
    keeps = two_parts(quality_ref[mine, :].astype(jnp.float32) * weight_ref[mine, :])
    wants = two_parts(innov_ref[mine, :])
    for turn, slot in enumerate(group):
        at = slice(turn, turn + 1)
        moved = permute(pos_ref[slot : slot + 1, :], [part[at] for part in keeps + wants], pieces)
        here = pl.ds(turn * pieces, pieces)
        keep_ref[here, :] = moved[0] + moved[1]
        want_ref[here, :] = moved[2] + moved[3]


def tile_row(ref, at):
    parts = LANES // PIECE
    return jnp.concatenate([ref[pl.ds(at * parts + k, 1), :] for k in range(parts)], axis=1)


def window_places(place_ref, at, start, low_row, per_row):
    place = tile_row(place_ref, at) - start * per_row
    if low_row is None:
        return place
    return jnp.where(place < (low_row - start) * per_row, -1, place)


def over_windows(tiles, slots, rows, bounds_ref, scalar_ref, sem, step):
    parts = LANES // PIECE
    bounds = bounds_ref[...]
    for tile in range(tiles):
        for slot in range(slots):
            step(slot, tile, bounds[slot, tile * parts], None)

    for slot in range(slots):

        @pl.when(bounds[2 * slots + slot, 0] >= WINDOW)
        def _():
            pltpu.async_copy(bounds_ref, scalar_ref, sem).wait()

            @pl.loop(0, tiles)
            def _(tile):
                begin = scalar_ref[slot, tile * parts]
                end = scalar_ref[slots + slot, (tile + 1) * parts - 1]

                @pl.loop(1, lax.div(end - begin, WINDOW) + 1)
                def _(turn):
                    low_row = begin + turn * WINDOW
                    step(slot, tile, jnp.minimum(low_row, rows - WINDOW), low_row)


def pick_kernel(group, sides, own_ref, circ_high_ref, circ_low_ref, *refs):
    if sides:
        low, high = halo(refs[:sides])
        refs = refs[sides:]
    ens_ref, place_ref, lane_ref, bounds_ref, out_ref, *part_refs, scalar_ref, sem = refs
    rows, levels, lons = own_ref.shape
    slots = len(group)
    tiles = place_ref.shape[0] * PIECE // (slots * LANES)
    local_ref = own_ref
    if sides:
        local_ref, *part_refs = part_refs
        mixed = smooth_rows(low, own_ref[...], high).reshape(rows * levels, lons)
        local_ref[...] = smooth_lons(mixed, circ_high_ref[...], circ_low_ref[...]).reshape(local_ref.shape)
    for slot in range(slots):
        field = ens_ref[group[slot]].astype(jnp.float32) * local_ref[...]
        first = field.astype(jnp.bfloat16).astype(jnp.float32)
        part_refs[slot][...] = jnp.concatenate([first, field - first], axis=1).astype(jnp.bfloat16)
    parts = lons // PICK_LONS
    size = WINDOW * parts * levels
    place_ids = ids_of((size, LANES), 0)
    lane_ids = small_ids((PICK_LONS, LANES))

    def step(slot, tile, start, low_row):
        at = slot * tiles + tile
        place = window_places(place_ref, at, start, low_row, parts * levels)
        part = part_refs[slot][pl.ds(start, WINDOW)]
        left = jnp.stack([part[:, :, k * PICK_LONS : (k + 1) * PICK_LONS] for k in range(parts)], axis=1).reshape(2 * size, PICK_LONS)
        hot = one_hot(lane_ids, tile_row(lane_ref, at).astype(jnp.bfloat16))
        both = jnp.dot(left, hot, preferred_element_type=jnp.float32).reshape(WINDOW * parts, 2, levels, LANES)
        value = (both[:, 0] + both[:, 1]).reshape(size, LANES)
        value = jnp.sum(jnp.where(place_ids == place, value, 0.0), axis=0, keepdims=True)
        for k in range(LANES // PIECE):
            here, part = pl.ds(at * (LANES // PIECE) + k, 1), value[:, k * PIECE : (k + 1) * PIECE]
            out_ref[here, :] = part if low_row is None else out_ref[here, :] + part

    over_windows(tiles, slots, rows, bounds_ref, scalar_ref, sem, step)


def scatter_kernel(group, norm_scale, earlier, seen_ref, want_ref, keep_ref, place_ref, lane_ref, ens_ref, *refs):
    before_refs, refs = refs[:earlier], refs[earlier:]
    bounds_ref, back_ref, cost_ref, wres_ref, *grad_refs, scalar_ref, sem = refs
    slots = len(group)
    _, rows, levels, lons = ens_ref.shape
    tiles = place_ref.shape[0] * PIECE // (slots * LANES)
    resid = seen_ref[...] * norm_scale - want_ref[...]
    wres_ref[...] = keep_ref[...] * resid
    cost = jnp.sum((wres_ref[...] * resid).reshape(-1, *cost_ref.shape), axis=0)
    cost_ref[...] = cost + before_refs[1][...] if earlier else cost
    parts = lons // SCATTER_LONS
    size = WINDOW * parts * levels
    place_ids = small_ids((size, LANES))
    lane_ids = small_ids((SCATTER_LONS, LANES))
    for slot in range(slots):
        grad_refs[slot][...] = jnp.zeros(grad_refs[slot].shape, jnp.float32)

    def step(slot, tile, start, low_row):
        at = slot * tiles + tile
        place = window_places(place_ref, at, start, low_row, parts * levels)
        chosen = place_ids == place.astype(jnp.float32).astype(jnp.bfloat16)
        left = [jnp.where(chosen, part, jnp.bfloat16(0)) for part in two_parts(tile_row(wres_ref, at))]
        left = jnp.concatenate(left, axis=0)
        hot = one_hot(lane_ids, tile_row(lane_ref, at).astype(jnp.bfloat16))
        both = across(left, hot)
        grad_refs[slot][pl.ds(start, WINDOW)] += (both[:size] + both[size:]).reshape(WINDOW, parts, levels, SCATTER_LONS)

    over_windows(tiles, slots, rows, bounds_ref, scalar_ref, sem, step)
    total = jnp.zeros((rows, levels, lons), jnp.float32)
    for slot in range(slots):
        grad = jnp.concatenate([grad_refs[slot][:, k] for k in range(parts)], axis=2)
        total += ens_ref[group[slot]].astype(jnp.float32) * grad
    total = total * norm_scale
    back_ref[...] = total + before_refs[0][...] if earlier else total


def grad_kernel(sides, *refs):
    low, high = halo(refs[:sides])
    own_ref, circ_high_ref, circ_low_ref, weights_ref, obs_cost_ref, grad_ref, sums_ref = refs[sides:]
    rows, levels, lons = own_ref.shape
    mixed = smooth_rows(low, own_ref[...], high).reshape(rows * levels, lons)
    weights = weights_ref[...].reshape(rows * levels, lons)
    grad = weights + smooth_lons(mixed, circ_high_ref[...], circ_low_ref[...])
    grad_ref[...] = grad.reshape(grad_ref.shape)
    lane = lax.broadcasted_iota(jnp.int32, sums_ref.shape, 1)
    prior = jnp.sum(weights * weights)
    square = jnp.sum(grad * grad)
    obs_cost = jnp.sum(obs_cost_ref[...])
    sums_ref[...] = jnp.where(lane == 0, square, jnp.where(lane == 1, prior, jnp.where(lane == 2, obs_cost, 0.0)))


def update_kernel(members, entries, sums_ref, own_ref, grad_ref, new_ref, cost_ref):
    totals = jnp.sum(sums_ref[...], axis=0, keepdims=True)
    length = jnp.sqrt(totals[:, :1] / entries + EPSILON)
    new_ref[...] = own_ref[...] - grad_ref[...] * (STEP_LENGTH / length)[None]
    cost_ref[...] = (0.5 * totals[:, 1:2] + 0.5 * totals[:, 2:3] / members) / entries


def call(body, out_shape, scratch, flops, *operands):
    vmem = pl.BlockSpec(memory_space=pltpu.VMEM)
    return pl.pallas_call(
        body,
        out_shape=out_shape,
        in_specs=[vmem] * len(operands),
        out_specs=jax.tree.map(lambda _: vmem, out_shape),
        scratch_shapes=scratch,
        compiler_params=pltpu.CompilerParams(vmem_limit_bytes=48 * MIB),
        cost_estimate=pl.CostEstimate(flops=flops, bytes_accessed=2 * MIB, transcendentals=0),
    )(*operands)


def edges(field):
    count = lax.axis_size("lat")
    if count == 2:
        rows = field.shape[0]
        start = (rows - HALF) * (1 - lax.axis_index("lat"))
        edge = lax.dynamic_slice_in_dim(field, start, HALF, 0)
        return [lax.ppermute(edge, "lat", [(0, 1), (1, 0)])]
    forward = [(i, i + 1) for i in range(count - 1)]
    backward = [(target, source) for source, target in forward]
    low = lax.ppermute(field[-HALF:], "lat", forward)
    high = lax.ppermute(field[:HALF], "lat", backward)
    return [low, high]


def halo(refs):
    if len(refs) == 2:
        return refs[0][...], refs[1][...]
    last = lax.axis_index("lat") == 1
    rows = refs[0].shape[0]
    return jnp.where(last, refs[0][rows - HALF :], 0.0), jnp.where(last, 0.0, refs[0][:HALF])


def summed(value, axis, turn=0):
    count = lax.axis_size(axis)
    if count & (count - 1):
        return lax.psum(value, axis)
    aways = [1 << k for k in range(count.bit_length() - 1)]
    for away in aways[turn:] + aways[:turn]:
        value = value + lax.ppermute(value, axis, [(i, i ^ away) for i in range(count)])
    return value


def like(shape, kind=jnp.float32):
    return jax.ShapeDtypeStruct(shape, kind)


def sort_cells(obs_cell, shape, groups):
    slots, obs = obs_cell.shape
    kinds = [like((slots, obs), jnp.int32)]
    for group in groups:
        ordered = (len(group) * obs // PIECE, PIECE)
        kinds += [like(ordered, jnp.int32), like(ordered)] * 2
        kinds += [like((-(-3 * len(group) // 8) * 8, -(-(obs // PIECE) // 128) * 128), jnp.int32)]
    scratch = [pltpu.VMEM((obs // LANES * shape[0] // BIN, LANES), jnp.float32)] * slots
    pos, *outs = call(functools.partial(sort_kernel, shape, groups), kinds, scratch, COST, obs_cell)
    outs = [outs[k : k + 5] for k in range(0, len(outs), 5)]
    return pos, [(out[:2], out[2:4], out[4]) for out in outs]


def arrange(pos, innovation, obs_weight, quality, group):
    ordered = like((len(group) * pos.shape[1] // PIECE, PIECE))
    body = functools.partial(arrange_kernel, group)
    return call(body, [ordered, ordered], [], COST, pos, innovation, obs_weight, quality)


def pick(sides, own, circ, ens, at, bounds, group):
    rows, levels, lons = own.shape
    kinds = [like(at[0].shape)] + [like(own.shape)] * (len(sides) > 0)
    scratch = [pltpu.VMEM((rows, 2 * levels, lons), jnp.bfloat16)] * len(group)
    scratch += [pltpu.SMEM(bounds.shape, jnp.int32), pltpu.SemaphoreType.DMA]
    body = functools.partial(pick_kernel, group, len(sides))
    return call(body, kinds, scratch, COST, own, *circ, *sides, ens, *at, bounds)


def scatter(seen, want, keep, ens, at, bounds, norm_scale, group, earlier):
    _, rows, levels, lons = ens.shape
    scratch = [pltpu.VMEM(seen.shape, jnp.float32)]
    scratch += [pltpu.VMEM((rows, lons // SCATTER_LONS, levels, SCATTER_LONS), jnp.float32)] * len(group)
    kinds = [like((rows, levels, lons)), like((8, 128))]
    scratch += [pltpu.SMEM(bounds.shape, jnp.int32), pltpu.SemaphoreType.DMA]
    body = functools.partial(scatter_kernel, group, norm_scale, len(earlier))
    return call(body, kinds, scratch, COST, seen, want, keep, *at, ens, *earlier, bounds)


def gradient(sides, own, circ, weights, obs_cost, devices):
    kinds = [like(own.shape), like((devices, 128))]
    body = functools.partial(grad_kernel, len(sides))
    return call(body, kinds, [], COST, *sides, own, *circ, weights, obs_cost)


def local(ensemble, weights, obs_cell, innovation, obs_weight, quality):
    _, rows, levels, lons = weights.shape
    members, bands = lax.axis_size("mem"), lax.axis_size("lat")
    norm_scale = 1.0 / math.sqrt(members - 1)
    ens, own = ensemble[0], weights[0]
    circ = [jnp.asarray(part) for part in circulant_parts(lons)]
    slots = obs_cell.shape[0]
    size = slots // GROUPS
    groups = [range(k, k + size) for k in range(0, slots, size)]
    sides = [lax.ppermute(own, "lat", [(0, 1), (1, 0)])] if bands == 2 else edges(own)
    pos, ordered = sort_cells(obs_cell, own.shape, groups)
    arranged = [arrange(pos, innovation, obs_weight, quality, group) for group in groups]
    local_weights, seen = None, []
    for turn, (group, (pick_at, _, bounds)) in enumerate(zip(groups, ordered)):
        if turn == 0:
            picked, local_weights = pick(sides, own, circ, ens, pick_at, bounds, group)
        else:
            (picked,) = pick([], local_weights, circ, ens, pick_at, bounds, group)
        seen.append(summed(picked, "mem", 2 * turn))
    sofar = []
    for group, total, (keep, want), (_, scatter_at, bounds) in zip(groups, seen, arranged, ordered):
        sofar = scatter(total, want, keep, ens, scatter_at, bounds, norm_scale, group, sofar)
    back, obs_cost = sofar
    grad, sums = gradient(edges(back), back, circ, own, obs_cost, members * bands)
    sums = lax.all_to_all(sums, ("mem", "lat"), 0, 0, tiled=True)
    body = functools.partial(update_kernel, members, float(members * bands * rows * levels * lons))
    new_weights, cost = call(body, [like(own.shape), like((1, 1))], [], 10**8, sums, own, grad)
    return new_weights[None], cost[0, 0]


def solution(mesh):
    placed = (
        P("mem", None, "lat", None, None),
        P("mem", "lat", None, None),
        P(None, "lat"),
        P(None, "lat"),
        P(None, "lat"),
        P(None, "lat"),
    )
    return jax.shard_map(
        local,
        mesh=mesh,
        in_specs=placed,
        out_specs=(P("mem", "lat", None, None), P()),
        check_vma=False,
    )
```

```python
import functools
import math

import jax
import jax.numpy as jnp
import numpy as np
from jax import lax
from jax.experimental import pallas as pl
from jax.experimental.pallas import tpu as pltpu
from jax.sharding import PartitionSpec as P

HALF = 8
STEP_LENGTH = 0.5
EPSILON = 1e-06
LANES = 256
PIECE = 128
PICK_LONS = 256
SCATTER_LONS = 128
GROUP = 1024
BIN = 1
WINDOW = 3
GROUPS = 2
COST = 10**9
MIB = 1024 * 1024


def taps():
    sigma = HALF / 2.0
    every = np.arange(-HALF, HALF + 1).astype(np.float64)
    normal = np.sqrt(np.sum(np.exp(-((every / sigma) ** 2))))
    return np.exp(-0.5 * (every / sigma) ** 2) / normal


def circulant_parts(lon_count):
    full = np.zeros((lon_count, lon_count), np.float32)
    at = np.arange(lon_count)
    for shift_by, tap in zip(range(-HALF, HALF + 1), taps()):
        full[at, (at + shift_by) % lon_count] += np.float32(tap)
    high = full.astype(jnp.bfloat16)
    low = (full - high.astype(np.float32)).astype(jnp.bfloat16)
    return high, low


def two_parts(value):
    high = value.astype(jnp.bfloat16)
    low = (value - high.astype(jnp.float32)).astype(jnp.bfloat16)
    return high, low


def smooth_rows(low, own, high):
    tap = [float(t) for t in taps()]
    padded = jnp.concatenate([low, own, high], axis=0)
    rows = own.shape[0]
    total = padded[HALF : HALF + rows] * tap[HALF]
    for away in range(1, HALF + 1):
        pair = padded[HALF - away : HALF - away + rows] + padded[HALF + away : HALF + away + rows]
        total = total + pair * tap[HALF + away]
    return total


def smooth_lons(field, circ_high, circ_low):
    first, second = two_parts(field)
    dot = functools.partial(jnp.dot, preferred_element_type=jnp.float32)
    return dot(first, circ_high) + (dot(second, circ_high) + dot(first, circ_low))


def quotient(value, by):
    if by & (by - 1):
        return lax.div(value, by), lax.rem(value, by)
    return lax.shift_right_logical(value, by.bit_length() - 1), lax.bitwise_and(value, by - 1)


def small_ids(shape):
    return lax.broadcasted_iota(jnp.int32, shape, 0).astype(jnp.bfloat16)


def one_hot(ids, at):
    return jnp.where(ids == at, jnp.bfloat16(1), jnp.bfloat16(0))


def ids_of(shape, dim):
    return lax.broadcasted_iota(jnp.int32, shape, dim)


def across(left, right):
    return lax.dot_general(left, right, (((1,), (1,)), ((), ())), preferred_element_type=jnp.float32)


def permute(pos, values, pieces):
    hi_ids, lo_ids = small_ids((pieces, GROUP)), small_ids((PIECE, GROUP))
    hi, lo = (part.astype(jnp.float32).astype(jnp.bfloat16) for part in quotient(pos, PIECE))
    total = jnp.zeros((len(values) * pieces, PIECE), jnp.float32)
    for at in range(0, pos.shape[1], GROUP):
        here = slice(at, at + GROUP)
        chosen = hi_ids == hi[:, here]
        left = jnp.concatenate([jnp.where(chosen, v[:, here], jnp.bfloat16(0)) for v in values], axis=0)
        total += across(left, one_hot(lo_ids, lo[:, here]))
    return [total[k * pieces : (k + 1) * pieces] for k in range(len(values))]


def sort_kernel(shape, groups, cell_ref, pos_ref, *refs):
    slots, obs = cell_ref.shape
    refs, prefix_refs = refs[:-slots], refs[-slots:]
    rows, levels, lons = shape
    tiles, pieces = obs // LANES, obs // PIECE
    bins = rows // BIN
    bin_ids = small_ids((bins, LANES))
    square = (LANES, LANES)
    upper = (ids_of(square, 0) <= ids_of(square, 1)).astype(jnp.bfloat16)
    ones = jnp.ones((LANES, 128), jnp.bfloat16)
    before = (ids_of((bins, bins), 1) < ids_of((bins, bins), 0)).astype(jnp.bfloat16)
    count = functools.partial(jnp.dot, before, preferred_element_type=jnp.float32)
    wide = lambda v: jnp.concatenate([v] * (LANES // 128), axis=1)
    _, cells = quotient(cell_ref[...], rows * levels * lons)
    keys, lons_of = quotient(cells, lons)
    bins_of, _ = quotient(keys, levels * BIN)
    middle = lons // 2
    signed = jnp.where(lons_of < middle, lons_of, middle - 1 - lons_of)
    keys, bins_of, signed = (v.astype(jnp.float32).astype(jnp.bfloat16) for v in (keys, bins_of, signed))
    outs = len(refs) // len(groups)
    for slot, (group, mine) in enumerate([(g, m) for m, g in enumerate(groups) for _ in g]):
        *place_refs, bounds_ref = refs[mine * outs : (mine + 1) * outs]
        turn = slot - group[0]
        prefix_ref = prefix_refs[slot]
        in_bin = bins_of[slot : slot + 1]
        hots = [one_hot(bin_ids, in_bin[:, at * LANES : (at + 1) * LANES]) for at in range(tiles)]
        prefix_ref[...] = jnp.dot(jnp.concatenate(hots, axis=0), upper, preferred_element_type=jnp.float32)
        total = jnp.dot(sum(hots[1:], hots[0]), ones, preferred_element_type=jnp.float32)
        many = jnp.floor(total * (1.0 / LANES))
        few = total - many * LANES
        carry = count(many.astype(jnp.bfloat16)) * LANES + count(few.astype(jnp.bfloat16)) - 1.0
        places = []
        for at in range(tiles):
            here = pl.ds(at * bins, bins)
            place = (prefix_ref[here, pl.ds(0, LANES)] + wide(carry)) * hots[at].astype(jnp.float32)
            places.append(jnp.sum(place, axis=0, keepdims=True))
            carry += prefix_ref[here, pl.ds(LANES - 1, 1)]
        pos = jnp.concatenate(places, axis=1).astype(jnp.int32)
        pos_ref[pl.ds(slot, 1), :] = pos
        key, lane = permute(pos, [keys[slot : slot + 1], signed[slot : slot + 1]], pieces)
        key, lane = key.astype(jnp.int32), lane.astype(jnp.int32)
        row, level = quotient(key, levels)
        lon = jnp.where(lane < 0, middle - 1 - lane, lane)
        here = pl.ds(turn * pieces, pieces)
        for near, place_ref, lane_ref in zip((PICK_LONS, SCATTER_LONS), place_refs[::2], place_refs[1::2]):
            part, lane = quotient(lon, near)
            place_ref[here, :] = (row * (lons // near) + part) * levels + level
            lane_ref[here, :] = lane.astype(jnp.float32)
        begin_row = quotient(row, BIN)[0] * BIN
        first = jnp.minimum(begin_row[:, :1], rows - WINDOW)
        last = begin_row[:, PIECE - 1 :] + BIN - 1
        begin = jnp.concatenate([first[:1], first[:-1]], axis=0)
        ends_tile = quotient(ids_of((pieces, 1), 0), LANES // PIECE)[1] == LANES // PIECE - 1
        far = jnp.max(jnp.where(ends_tile, last - begin, 0), axis=0, keepdims=True)
        spread = [jnp.broadcast_to(v.astype(jnp.float32), (pieces, 128)).T[:1].astype(jnp.int32) for v in (first, last)]
        spread.append(jnp.broadcast_to(far, (1, pieces)))
        for kind, v in enumerate(spread):
            bounds_ref[pl.ds(kind * len(group) + turn, 1), pl.ds(0, pieces)] = v


def arrange_kernel(group, pos_ref, innov_ref, weight_ref, quality_ref, keep_ref, want_ref):
    pieces = pos_ref.shape[1] // PIECE
    mine = slice(group[0], group[-1] + 1)
    keeps = two_parts(quality_ref[mine, :].astype(jnp.float32) * weight_ref[mine, :])
    wants = two_parts(innov_ref[mine, :])
    for turn, slot in enumerate(group):
        at = slice(turn, turn + 1)
        moved = permute(pos_ref[slot : slot + 1, :], [part[at] for part in keeps + wants], pieces)
        here = pl.ds(turn * pieces, pieces)
        keep_ref[here, :] = moved[0] + moved[1]
        want_ref[here, :] = moved[2] + moved[3]


def tile_row(ref, at):
    parts = LANES // PIECE
    return jnp.concatenate([ref[pl.ds(at * parts + k, 1), :] for k in range(parts)], axis=1)


def window_places(place_ref, at, start, low_row, per_row):
    place = tile_row(place_ref, at) - start * per_row
    if low_row is None:
        return place
    return jnp.where(place < (low_row - start) * per_row, -1, place)


def over_windows(tiles, slots, rows, bounds_ref, scalar_ref, sem, step):
    parts = LANES // PIECE
    bounds = bounds_ref[...]
    for tile in range(tiles):
        for slot in range(slots):
            step(slot, tile, bounds[slot, tile * parts], None)

    for slot in range(slots):

        @pl.when(bounds[2 * slots + slot, 0] >= WINDOW)
        def _():
            pltpu.async_copy(bounds_ref, scalar_ref, sem).wait()

            @pl.loop(0, tiles)
            def _(tile):
                begin = scalar_ref[slot, tile * parts]
                end = scalar_ref[slots + slot, (tile + 1) * parts - 1]

                @pl.loop(1, lax.div(end - begin, WINDOW) + 1)
                def _(turn):
                    low_row = begin + turn * WINDOW
                    step(slot, tile, jnp.minimum(low_row, rows - WINDOW), low_row)


def pick_kernel(group, sides, own_ref, circ_high_ref, circ_low_ref, *refs):
    if sides:
        low, high = halo(refs[:sides])
        refs = refs[sides:]
    ens_ref, place_ref, lane_ref, bounds_ref, out_ref, *part_refs, scalar_ref, sem = refs
    rows, levels, lons = own_ref.shape
    slots = len(group)
    tiles = place_ref.shape[0] * PIECE // (slots * LANES)
    local_ref = own_ref
    if sides:
        local_ref, *part_refs = part_refs
        mixed = smooth_rows(low, own_ref[...], high).reshape(rows * levels, lons)
        local_ref[...] = smooth_lons(mixed, circ_high_ref[...], circ_low_ref[...]).reshape(local_ref.shape)
    for slot in range(slots):
        field = ens_ref[group[slot]].astype(jnp.float32) * local_ref[...]
        first = field.astype(jnp.bfloat16).astype(jnp.float32)
        part_refs[slot][...] = jnp.concatenate([first, field - first], axis=1).astype(jnp.bfloat16)
    parts = lons // PICK_LONS
    size = WINDOW * parts * levels
    place_ids = ids_of((size, LANES), 0)
    lane_ids = small_ids((PICK_LONS, LANES))

    def step(slot, tile, start, low_row):
        at = slot * tiles + tile
        place = window_places(place_ref, at, start, low_row, parts * levels)
        part = part_refs[slot][pl.ds(start, WINDOW)]
        left = jnp.stack([part[:, :, k * PICK_LONS : (k + 1) * PICK_LONS] for k in range(parts)], axis=1).reshape(2 * size, PICK_LONS)
        hot = one_hot(lane_ids, tile_row(lane_ref, at).astype(jnp.bfloat16))
        both = jnp.dot(left, hot, preferred_element_type=jnp.float32).reshape(WINDOW * parts, 2, levels, LANES)
        value = (both[:, 0] + both[:, 1]).reshape(size, LANES)
        value = jnp.sum(jnp.where(place_ids == place, value, 0.0), axis=0, keepdims=True)
        for k in range(LANES // PIECE):
            here, part = pl.ds(at * (LANES // PIECE) + k, 1), value[:, k * PIECE : (k + 1) * PIECE]
            out_ref[here, :] = part if low_row is None else out_ref[here, :] + part

    over_windows(tiles, slots, rows, bounds_ref, scalar_ref, sem, step)


def scatter_kernel(group, norm_scale, earlier, seen_ref, want_ref, keep_ref, place_ref, lane_ref, ens_ref, *refs):
    before_refs, refs = refs[:earlier], refs[earlier:]
    bounds_ref, back_ref, cost_ref, wres_ref, *grad_refs, scalar_ref, sem = refs
    slots = len(group)
    _, rows, levels, lons = ens_ref.shape
    tiles = place_ref.shape[0] * PIECE // (slots * LANES)
    resid = seen_ref[...] * norm_scale - want_ref[...]
    wres_ref[...] = keep_ref[...] * resid
    cost = jnp.sum((wres_ref[...] * resid).reshape(-1, *cost_ref.shape), axis=0)
    cost_ref[...] = cost + before_refs[1][...] if earlier else cost
    parts = lons // SCATTER_LONS
    size = WINDOW * parts * levels
    place_ids = small_ids((size, LANES))
    lane_ids = small_ids((SCATTER_LONS, LANES))
    for slot in range(slots):
        grad_refs[slot][...] = jnp.zeros(grad_refs[slot].shape, jnp.float32)

    def step(slot, tile, start, low_row):
        at = slot * tiles + tile
        place = window_places(place_ref, at, start, low_row, parts * levels)
        chosen = place_ids == place.astype(jnp.float32).astype(jnp.bfloat16)
        left = [jnp.where(chosen, part, jnp.bfloat16(0)) for part in two_parts(tile_row(wres_ref, at))]
        left = jnp.concatenate(left, axis=0)
        hot = one_hot(lane_ids, tile_row(lane_ref, at).astype(jnp.bfloat16))
        both = across(left, hot)
        grad_refs[slot][pl.ds(start, WINDOW)] += (both[:size] + both[size:]).reshape(WINDOW, parts, levels, SCATTER_LONS)

    over_windows(tiles, slots, rows, bounds_ref, scalar_ref, sem, step)
    total = jnp.zeros((rows, levels, lons), jnp.float32)
    for slot in range(slots):
        grad = jnp.concatenate([grad_refs[slot][:, k] for k in range(parts)], axis=2)
        total += ens_ref[group[slot]].astype(jnp.float32) * grad
    total = total * norm_scale
    back_ref[...] = total + before_refs[0][...] if earlier else total


def grad_kernel(sides, *refs):
    low, high = halo(refs[:sides])
    own_ref, circ_high_ref, circ_low_ref, weights_ref, obs_cost_ref, grad_ref, sums_ref = refs[sides:]
    rows, levels, lons = own_ref.shape
    mixed = smooth_rows(low, own_ref[...], high).reshape(rows * levels, lons)
    weights = weights_ref[...].reshape(rows * levels, lons)
    grad = weights + smooth_lons(mixed, circ_high_ref[...], circ_low_ref[...])
    grad_ref[...] = grad.reshape(grad_ref.shape)
    lane = lax.broadcasted_iota(jnp.int32, sums_ref.shape, 1)
    prior = jnp.sum(weights * weights)
    square = jnp.sum(grad * grad)
    obs_cost = jnp.sum(obs_cost_ref[...])
    sums_ref[...] = jnp.where(lane == 0, square, jnp.where(lane == 1, prior, jnp.where(lane == 2, obs_cost, 0.0)))


def update_kernel(members, entries, sums_ref, own_ref, grad_ref, new_ref, cost_ref, ready_ref, sems):
    totals = jnp.sum(sums_ref[...], axis=0, keepdims=True)
    length = jnp.sqrt(totals[:, :1] / entries + EPSILON)
    scale = (STEP_LENGTH / length)[None]
    rows = own_ref.shape[0]
    copies = []
    for k, begin in enumerate(range(0, rows, HALF)):
        here = pl.ds(begin, HALF)
        ready_ref[here] = own_ref[here] - grad_ref[here] * scale
        copies.append(pltpu.make_async_copy(ready_ref.at[here], new_ref.at[here], sems.at[k]))
        copies[-1].start()
    cost_ref[...] = (0.5 * totals[:, 1:2] + 0.5 * totals[:, 2:3] / members) / entries
    for copy in copies:
        copy.wait()


def call(body, out_shape, scratch, flops, *operands, unplaced=0):
    vmem = pl.BlockSpec(memory_space=pltpu.VMEM)
    return pl.pallas_call(
        body,
        out_shape=out_shape,
        in_specs=[vmem] * len(operands),
        out_specs=[pl.BlockSpec(memory_space=pl.ANY)] * unplaced + [vmem] * (len(out_shape) - unplaced)
        if unplaced
        else jax.tree.map(lambda _: vmem, out_shape),
        scratch_shapes=scratch,
        compiler_params=pltpu.CompilerParams(vmem_limit_bytes=48 * MIB),
        cost_estimate=pl.CostEstimate(flops=flops, bytes_accessed=2 * MIB, transcendentals=0),
    )(*operands)


def edges(field):
    count = lax.axis_size("lat")
    if count == 2:
        rows = field.shape[0]
        start = (rows - HALF) * (1 - lax.axis_index("lat"))
        edge = lax.dynamic_slice_in_dim(field, start, HALF, 0)
        return [lax.ppermute(edge, "lat", [(0, 1), (1, 0)])]
    forward = [(i, i + 1) for i in range(count - 1)]
    backward = [(target, source) for source, target in forward]
    low = lax.ppermute(field[-HALF:], "lat", forward)
    high = lax.ppermute(field[:HALF], "lat", backward)
    return [low, high]


def halo(refs):
    if len(refs) == 2:
        return refs[0][...], refs[1][...]
    last = lax.axis_index("lat") == 1
    rows = refs[0].shape[0]
    return jnp.where(last, refs[0][rows - HALF :], 0.0), jnp.where(last, 0.0, refs[0][:HALF])


def summed(value, axis, turn=0):
    count = lax.axis_size(axis)
    if count & (count - 1):
        return lax.psum(value, axis)
    aways = [1 << k for k in range(count.bit_length() - 1)]
    for away in aways[turn:] + aways[:turn]:
        value = value + lax.ppermute(value, axis, [(i, i ^ away) for i in range(count)])
    return value


def like(shape, kind=jnp.float32):
    return jax.ShapeDtypeStruct(shape, kind)


def sort_cells(obs_cell, shape, groups):
    slots, obs = obs_cell.shape
    kinds = [like((slots, obs), jnp.int32)]
    for group in groups:
        ordered = (len(group) * obs // PIECE, PIECE)
        kinds += [like(ordered, jnp.int32), like(ordered)] * 2
        kinds += [like((-(-3 * len(group) // 8) * 8, -(-(obs // PIECE) // 128) * 128), jnp.int32)]
    scratch = [pltpu.VMEM((obs // LANES * shape[0] // BIN, LANES), jnp.float32)] * slots
    pos, *outs = call(functools.partial(sort_kernel, shape, groups), kinds, scratch, COST, obs_cell)
    outs = [outs[k : k + 5] for k in range(0, len(outs), 5)]
    return pos, [(out[:2], out[2:4], out[4]) for out in outs]


def arrange(pos, innovation, obs_weight, quality, group):
    ordered = like((len(group) * pos.shape[1] // PIECE, PIECE))
    body = functools.partial(arrange_kernel, group)
    return call(body, [ordered, ordered], [], COST, pos, innovation, obs_weight, quality)


def pick(sides, own, circ, ens, at, bounds, group):
    rows, levels, lons = own.shape
    kinds = [like(at[0].shape)] + [like(own.shape)] * (len(sides) > 0)
    scratch = [pltpu.VMEM((rows, 2 * levels, lons), jnp.bfloat16)] * len(group)
    scratch += [pltpu.SMEM(bounds.shape, jnp.int32), pltpu.SemaphoreType.DMA]
    body = functools.partial(pick_kernel, group, len(sides))
    return call(body, kinds, scratch, COST, own, *circ, *sides, ens, *at, bounds)


def scatter(seen, want, keep, ens, at, bounds, norm_scale, group, earlier):
    _, rows, levels, lons = ens.shape
    scratch = [pltpu.VMEM(seen.shape, jnp.float32)]
    scratch += [pltpu.VMEM((rows, lons // SCATTER_LONS, levels, SCATTER_LONS), jnp.float32)] * len(group)
    kinds = [like((rows, levels, lons)), like((8, 128))]
    scratch += [pltpu.SMEM(bounds.shape, jnp.int32), pltpu.SemaphoreType.DMA]
    body = functools.partial(scatter_kernel, group, norm_scale, len(earlier))
    return call(body, kinds, scratch, COST, seen, want, keep, *at, ens, *earlier, bounds)


def gradient(sides, own, circ, weights, obs_cost, devices):
    kinds = [like(own.shape), like((devices, 128))]
    body = functools.partial(grad_kernel, len(sides))
    return call(body, kinds, [], COST, *sides, own, *circ, weights, obs_cost)


def local(ensemble, weights, obs_cell, innovation, obs_weight, quality):
    _, rows, levels, lons = weights.shape
    members, bands = lax.axis_size("mem"), lax.axis_size("lat")
    norm_scale = 1.0 / math.sqrt(members - 1)
    ens, own = ensemble[0], weights[0]
    circ = [jnp.asarray(part) for part in circulant_parts(lons)]
    slots = obs_cell.shape[0]
    size = slots // GROUPS
    groups = [range(k, k + size) for k in range(0, slots, size)]
    sides = [lax.ppermute(own, "lat", [(0, 1), (1, 0)])] if bands == 2 else edges(own)
    pos, ordered = sort_cells(obs_cell, own.shape, groups)
    arranged = [arrange(pos, innovation, obs_weight, quality, group) for group in groups]
    local_weights, seen = None, []
    for turn, (group, (pick_at, _, bounds)) in enumerate(zip(groups, ordered)):
        if turn == 0:
            picked, local_weights = pick(sides, own, circ, ens, pick_at, bounds, group)
        else:
            (picked,) = pick([], local_weights, circ, ens, pick_at, bounds, group)
        seen.append(summed(picked, "mem", 2 * turn))
    sofar = []
    for group, total, (keep, want), (_, scatter_at, bounds) in zip(groups, seen, arranged, ordered):
        sofar = scatter(total, want, keep, ens, scatter_at, bounds, norm_scale, group, sofar)
    back, obs_cost = sofar
    grad, sums = gradient(edges(back), back, circ, own, obs_cost, members * bands)
    sums = lax.all_to_all(sums, ("mem", "lat"), 0, 0, tiled=True)
    body = functools.partial(update_kernel, members, float(members * bands * rows * levels * lons))
    scratch = [pltpu.VMEM(own.shape, jnp.float32), pltpu.SemaphoreType.DMA((rows // HALF,))]
    new_weights, cost = call(body, [like(own.shape), like((1, 1))], scratch, COST, sums, own, grad, unplaced=1)
    return new_weights[None], cost[0, 0]


def solution(mesh):
    placed = (
        P("mem", None, "lat", None, None),
        P("mem", "lat", None, None),
        P(None, "lat"),
        P(None, "lat"),
        P(None, "lat"),
        P(None, "lat"),
    )
    return jax.shard_map(
        local,
        mesh=mesh,
        in_specs=placed,
        out_specs=(P("mem", "lat", None, None), P()),
        check_vma=False,
    )
```
